32 devices in a mesh: rep: 4 (over z), fsdp: 2 (over x), ctx: 4 (over y, core).
Axes of the slice: x: 2, y: 2, z: 4, core: 2. Of those that a mesh axis runs over, the one named last changes fastest.
Arguments:
- tokens: bfloat16 [24, 1024, 768], P(('rep', 'fsdp'), 'ctx'), may hold values from -6 to 6
- segment: int32 [24, 1024], P(('rep', 'fsdp'), 'ctx'), may hold values from 0 to 3, never falling along the last dimension, each value on 1 to 512 neighbouring positions
- ln1_gain: bfloat16 [768], P(('fsdp', 'ctx')), may hold values from 0.099609375 to 1.8984375
- ln1_bias: bfloat16 [768], P(('fsdp', 'ctx')), may hold values from -1.75 to 1.75
- qkv_weight: bfloat16 [768, 2304], P(('fsdp', 'ctx')), may hold values from -0.21875 to 0.21875
- qkv_bias: bfloat16 [2304], P(('fsdp', 'ctx')), may hold values from -0.3125 to 0.3125
- out_weight: bfloat16 [768, 768], P(('fsdp', 'ctx')), may hold values from -1.75 to 1.75
- out_bias: bfloat16 [768], P(('fsdp', 'ctx')), may hold values from -1.75 to 1.75
- ln2_gain: bfloat16 [768], P(('fsdp', 'ctx')), may hold values from 0.099609375 to 1.8984375
- ln2_bias: bfloat16 [768], P(('fsdp', 'ctx')), may hold values from -1.75 to 1.75
- fc_weight: bfloat16 [768, 3072], P(('fsdp', 'ctx')), may hold values from -0.21875 to 0.21875
- fc_bias: bfloat16 [3072], P(('fsdp', 'ctx')), may hold values from -3 to 3
- proj_weight: bfloat16 [3072, 768], P(('fsdp', 'ctx')), may hold values from -0.109375 to 0.109375
- proj_bias: bfloat16 [768], P(('fsdp', 'ctx')), may hold values from -1.75 to 1.75
- cotangent: bfloat16 [24, 1024, 768], P(('rep', 'fsdp'), 'ctx'), may hold values from -6 to 6
Outputs:
- output: bfloat16 [24, 1024, 768], P(('rep', 'fsdp'), 'ctx')
- grad_tokens: bfloat16 [24, 1024, 768], P(('rep', 'fsdp'), 'ctx')
- grad_ln1_gain: float32 [768], P(('fsdp', 'ctx'))
- grad_ln1_bias: float32 [768], P(('fsdp', 'ctx'))
- grad_qkv_weight: float32 [768, 2304], P(('fsdp', 'ctx'))
- grad_qkv_bias: float32 [2304], P(('fsdp', 'ctx'))
- grad_out_weight: float32 [768, 768], P(('fsdp', 'ctx'))
- grad_out_bias: float32 [768], P(('fsdp', 'ctx'))
- grad_ln2_gain: float32 [768], P(('fsdp', 'ctx'))
- grad_ln2_bias: float32 [768], P(('fsdp', 'ctx'))
- grad_fc_weight: float32 [768, 3072], P(('fsdp', 'ctx'))
- grad_fc_bias: float32 [3072], P(('fsdp', 'ctx'))
- grad_proj_weight: float32 [3072, 768], P(('fsdp', 'ctx'))
- grad_proj_bias: float32 [768], P(('fsdp', 'ctx'))
The draws below stay inside these ranges and needn't reach their ends.
All inputs are finite; a program needn't handle non-finite values.
Results may differ from the reference program's by a relative error of at most 0.017.
Values may be sent and summed in bfloat16 or wider, within the bound.
No kernel may reach another device: no remote copies, remote signals or barrier semaphores. Data moves between devices by JAX's collectives and lax.ppermute only.
A program may use at most 192 MiB of HBM per device.

```python
import math
import jax
import jax.numpy as jnp
import numpy as np
from jax import lax

D = 768
HEADS = 12
HEAD = 64
FF = 3072
ROT = 16
LEN = 1024
SEQS = 24


def steps_of(stream_key, extent, split, low, high):
    gain = 1.0
    for position, parts in split:
        heights = jax.random.uniform(jax.random.fold_in(jax.random.fold_in(stream_key, 6), position), (parts,), jnp.float32, low / len(split), high / len(split))
        gain = gain * jnp.repeat(jnp.exp(heights), extent[position] // parts).reshape((-1,) + (1,) * (len(extent) - 1 - position))
    return gain


def split_up(count, total, bound, slope):
    loads = [(1 << 20) // math.isqrt(rank ** slope) + 1 for rank in range(2, count + 1)]
    surplus, counts = total - bound - (count - 1), [1] * (count - 1)
    while surplus > 0:
        free = [i for i in range(count - 1) if counts[i] < bound]
        whole, remaining = sum([loads[i] for i in free]), surplus
        for i in free:
            addition = min(bound - counts[i], max(1, remaining * loads[i] // whole), surplus)
            counts[i] = counts[i] + addition
            surplus = surplus - addition
    return np.array([bound] + counts)


def uneven_parts(own_key, count, total, reach, slope):
    if count == 2:
        one = jax.random.randint(own_key, (), max(1, total - reach), min(reach, total - 1) + 1)
        return jnp.stack([one, total - one])
    sizes = jnp.asarray(split_up(count, total, reach, slope), jnp.int32)
    pairs = (count - 1) // 2
    source_of, sink = sizes[1:1 + 2 * pairs:2], sizes[2:2 + 2 * pairs:2]
    slack = jnp.minimum(source_of - 1, reach - sink)
    shifted = jax.random.randint(jax.random.fold_in(own_key, 1), (pairs,), 0, 1 << 20) % (slack + 1)
    sizes = sizes.at[1:1 + 2 * pairs:2].set(source_of - shifted).at[2:2 + 2 * pairs:2].set(sink + shifted)
    return sizes[jax.random.permutation(jax.random.fold_in(own_key, 2), count)]


def centred(stream_key, extent, scale, reach, shards=(), held_as=jnp.bfloat16):
    drawn = jax.random.normal(stream_key, extent, jnp.float32) * scale
    if len(shards) > 0:
        drawn = steps_of(stream_key, extent, shards, -0.22, 0.18) * drawn
    return jnp.clip(drawn, min=-reach, max=reach).astype(held_as)


def setup_inputs(seed: int = 0) -> dict:
    seeds = jax.random.split(jax.random.key(seed), 16)
    tokens = centred(seeds[0], (SEQS, LEN, D), 1.0, 6.0, ((0, 8), (1, 4)))
    segment = jax.vmap(lambda own: jnp.searchsorted(jnp.cumsum(uneven_parts(own, 4, LEN, LEN // 2, 1)), jnp.arange(LEN), side="right"))(jax.random.split(seeds[1], SEQS)).reshape((SEQS, LEN)).astype(jnp.int32)
    ln1_gain = jnp.clip(1.0 + 0.18 * jax.random.normal(seeds[2], (D,), jnp.float32), 0.099609375, 1.8984375).astype(jnp.bfloat16)
    ln1_bias = centred(seeds[3], (D,), 0.3, 1.75, ((0, 8),))
    qkv_weight = centred(seeds[4], (D, 3 * D), D ** -0.5, 0.21875, ((0, 8),))
    qkv_bias = centred(seeds[5], (3 * D,), 0.05, 0.3125, ((0, 8),))
    out_weight = centred(seeds[6], (D, D), (D // 64) ** -0.5, 1.75, ((0, 8),))
    out_bias = centred(seeds[7], (D,), 0.3, 1.75, ((0, 8),))
    ln2_gain = jnp.clip(1.0 + 0.18 * jax.random.normal(seeds[8], (D,), jnp.float32), 0.099609375, 1.8984375).astype(jnp.bfloat16)
    ln2_bias = centred(seeds[9], (D,), 0.3, 1.75, ((0, 8),))
    fc_weight = centred(seeds[10], (D, FF), D ** -0.5, 0.21875, ((0, 8),))
    fc_bias = centred(seeds[11], (FF,), 0.5, 3.0, ((0, 8),))
    proj_weight = centred(seeds[12], (FF, D), FF ** -0.5, 0.109375, ((0, 8),))
    proj_bias = centred(seeds[13], (D,), 0.3, 1.75, ((0, 8),))
    cotangent = centred(seeds[14], (SEQS, LEN, D), 1.0, 6.0, ((0, 8), (1, 4)))
    return dict(tokens=tokens, segment=segment, ln1_gain=ln1_gain, ln1_bias=ln1_bias, qkv_weight=qkv_weight, qkv_bias=qkv_bias, out_weight=out_weight, out_bias=out_bias, ln2_gain=ln2_gain, ln2_bias=ln2_bias, fc_weight=fc_weight, fc_bias=fc_bias, proj_weight=proj_weight, proj_bias=proj_bias, cotangent=cotangent)


@jax.custom_vjp
def low(v):
    return lax.optimization_barrier(v.astype(jnp.bfloat16)).astype(jnp.float32)

@jax.custom_vjp
def low_back(v):
    return v

def low_keep(v):
    return (low(v), None)

def low_pass(kept, grad):
    return (grad,)

def back_keep(v):
    return (v, None)

def back_low(kept, grad):
    return (low(grad),)
low.defvjp(low_keep, low_pass)
low_back.defvjp(back_keep, back_low)
epsilon = 1e-05
far_below = -1e+30
highest = lax.Precision.HIGHEST

def layer_norm(values, scales, shifts):
    center = values - lax.optimization_barrier(jnp.mean(values, axis=-1, keepdims=True))
    spread = lax.optimization_barrier(jnp.mean(center * center, axis=-1, keepdims=True))
    return center * lax.rsqrt(spread + epsilon) * scales + shifts

def tables(places):
    inverse = 1.0 / 10000.0 ** (jnp.arange(0, ROT, 2).astype(jnp.float32) / ROT)
    angles = places.astype(jnp.float32)[:, None] * inverse[None, :]
    cosine_table = jnp.concatenate([jnp.cos(angles), jnp.cos(angles)], axis=-1)
    sine_table = jnp.concatenate([jnp.sin(angles), jnp.sin(angles)], axis=-1)
    return (cosine_table, sine_table)

def rotate(head_vals, cosine_table, sine_table):
    turned = head_vals[..., :ROT]
    front_half = turned[..., :ROT // 2]
    latter = turned[..., ROT // 2:]
    swapped = jnp.concatenate([-latter, front_half], axis=-1)
    spun_part = turned * cosine_table[:, None, :] + swapped * sine_table[:, None, :]
    return jnp.concatenate([spun_part, head_vals[..., ROT:]], axis=-1)

def attend(batch_in):
    query_part, key_part, value_part, seg_ids = batch_in
    length = query_part.shape[0]
    scores = low_back(jnp.einsum('qhd,khd->hqk', query_part, key_part, precision=highest) * (1.0 / math.sqrt(HEAD)))
    places = jnp.arange(length)
    allowed = (seg_ids[:, None] == seg_ids[None, :]) & (places[None, :] <= places[:, None])
    weights = jax.nn.softmax(jnp.where(allowed[None], scores, far_below), axis=-1)
    return jnp.einsum('hqk,khd->qhd', low(weights), value_part, precision=highest)

def forward(params, batch_rows, seg_ids):
    gain_one, shift_one, w_qkv, b_qkv, w_out, b_out, gain_two, shift_two, w_fc, b_fc, w_proj, b_proj = params
    seq_count, length, features = batch_rows.shape
    flat_rows = batch_rows.reshape(seq_count * length, features)
    first_in = low(layer_norm(flat_rows, gain_one, shift_one))
    qkv_rows = low_back(jnp.dot(first_in, w_qkv, precision=highest) + b_qkv)
    cosine_table, sine_table = tables(jnp.tile(jnp.arange(length), seq_count))
    query_part = low(rotate(qkv_rows[:, :features].reshape(-1, HEADS, HEAD), cosine_table, sine_table))
    key_part = low(rotate(qkv_rows[:, features:2 * features].reshape(-1, HEADS, HEAD), cosine_table, sine_table))
    value_part = low(qkv_rows[:, 2 * features:].reshape(-1, HEADS, HEAD))
    seq_shape = (seq_count, length, HEADS, HEAD)
    attended = lax.map(jax.checkpoint(attend), (query_part.reshape(seq_shape), key_part.reshape(seq_shape), value_part.reshape(seq_shape), seg_ids))
    attended = low(low_back(attended.reshape(seq_count * length, features)))
    branch = jnp.dot(attended, w_out, precision=highest) + b_out
    second_in = low(layer_norm(flat_rows, gain_two, shift_two))
    before = low_back(jnp.dot(second_in, w_fc, precision=highest) + b_fc)
    hidden = low(jax.nn.gelu(before, approximate=False))
    summed = flat_rows + branch + jnp.dot(hidden, w_proj, precision=highest) + b_proj
    return summed.reshape(seq_count, length, features)

def reference(tokens, segment, ln1_gain, ln1_bias, qkv_weight, qkv_bias, out_weight, out_bias, ln2_gain, ln2_bias, fc_weight, fc_bias, proj_weight, proj_bias, cotangent):
    params = tuple((tensor.astype(jnp.float32) for tensor in (ln1_gain, ln1_bias, qkv_weight, qkv_bias, out_weight, out_bias, ln2_gain, ln2_bias, fc_weight, fc_bias, proj_weight, proj_bias)))
    group_size = math.gcd(SEQS, 4)
    steps_count = SEQS // group_size

    def in_groups(array):
        return array.reshape((steps_count, group_size) + array.shape[1:])

    def advance(totals, batch_in):
        batch_tok, batch_seg, batch_cot = batch_in

        def run_layer(weight_set, inputs):
            return forward(weight_set, inputs, batch_seg)
        result, pullback = jax.vjp(run_layer, params, batch_tok.astype(jnp.float32))
        grad_params, grad_inputs = pullback(batch_cot.astype(jnp.float32))
        totals = tuple((running + update for running, update in zip(totals, grad_params)))
        return (totals, (result.astype(jnp.bfloat16), grad_inputs.astype(jnp.bfloat16)))
    starting = tuple((jnp.zeros(tensor.shape, jnp.float32) for tensor in params))
    totals, (outputs, grad_inputs) = lax.scan(advance, starting, (in_groups(tokens), in_groups(segment), in_groups(cotangent)))
    return (outputs.reshape(tokens.shape), grad_inputs.reshape(tokens.shape), totals[0], totals[1], totals[2], totals[3], totals[4], totals[5], totals[6], totals[7], totals[8], totals[9], totals[10], totals[11])
```

```python
from functools import partial
import math

import jax
import jax.numpy as jnp
import numpy as np
from jax import lax
from jax.experimental import pallas as pl
from jax.experimental.pallas import tpu as pltpu
from jax.sharding import PartitionSpec as P

HEADS = 12
HEAD = 64
ROT = 16

epsilon = 1e-05
far_below = -1e30
low = jnp.bfloat16
wide = jnp.float32
log2e = math.log2(math.e)


def nn(a, b):
    return lax.dot_general(a, b, (((1,), (0,)), ((), ())), preferred_element_type=wide)


def nt(a, b):
    return lax.dot_general(a, b, (((1,), (1,)), ((), ())), preferred_element_type=wide)


def swap(value, axis, bits):
    size = lax.axis_size(axis)
    return lax.ppermute(value, axis, [(i, i ^ bits) for i in range(size)])


def in_order(rel, me):
    out = []
    for k in range(len(rel)):
        value = rel[k]
        for m in range(1, len(rel)):
            value = jnp.where(me == m, rel[k ^ m], value)
        out.append(value)
    return out


def pick(stacked, index):
    return lax.dynamic_index_in_dim(stacked, index, 0, keepdims=False)


def row_norm(block):
    values = block.astype(wide)
    center = values - jnp.mean(values, axis=-1, keepdims=True)
    spread = jnp.mean(center * center, axis=-1, keepdims=True)
    return center * lax.rsqrt(spread + epsilon)


def gelu_parts(v):
    bell = jnp.exp2(v * v * (-0.5 * log2e))
    base = 1.0 + (0.3275911 / math.sqrt(2.0)) * jnp.abs(v)
    t = pl.reciprocal(base, approx=True)
    t = t * (2.0 - base * t)
    poly = 0.5 * 1.061405429
    for coef in (-1.453152027, 1.421413741, -0.284496736, 0.254829592):
        poly = poly * t + 0.5 * coef
    tail = poly * t * bell
    phi = jnp.where(v >= 0, 1.0 - tail, tail)
    return phi, phi + v * bell * (1.0 / math.sqrt(2.0 * math.pi))


def ff_kernel(blocks, first_call, *refs):
    x_refs, refs = refs[:blocks], refs[blocks:]
    c_refs, refs = refs[:blocks], refs[blocks:]
    fc, proj, gain, shift, bias = refs[:5]
    refs = refs[5:]
    if not first_call:
        acc_fc, acc_proj, acc_vec = refs[:3]
        refs = refs[3:]
    outp, ep, dfc, dproj, vec, sec_s, hid_s, gp_s, cot_s, n_s = refs
    rows = x_refs[0].shape[0]
    hidden = fc.shape[1]
    dgain = jnp.zeros((1, fc.shape[0]), wide)
    dshift = jnp.zeros((1, fc.shape[0]), wide)
    dbias = jnp.zeros((1, hidden), wide)
    for j in range(blocks):
        here = pl.ds(j * rows, rows)
        n = row_norm(x_refs[j][...])
        second = (n * gain[...] + shift[...]).astype(low)
        sec_s[here, :] = second
        cot = c_refs[j][...]
        cot_s[here, :] = cot
        pre = nn(second, fc[...]) + bias[...]
        phi, slope = gelu_parts(pre)
        hid = (pre * phi).astype(low)
        gp = nt(cot, proj[...]) * slope
        dbias = dbias + jnp.sum(gp, axis=0, keepdims=True)
        gp = gp.astype(low)
        hid_s[here, :] = hid
        gp_s[here, :] = gp
        outp[j] = nn(hid, proj[...]).astype(outp.dtype)
        dsec = nt(gp, fc[...])
        dgain = dgain + jnp.sum(dsec * n, axis=0, keepdims=True)
        dshift = dshift + jnp.sum(dsec, axis=0, keepdims=True)
        ep[j] = (dsec * gain[...]).astype(ep.dtype)
    w_fc = nn(jnp.transpose(sec_s[...]), gp_s[...])
    w_proj = nn(jnp.transpose(hid_s[...]), cot_s[...])
    if not first_call:
        w_fc = w_fc + acc_fc[...]
        w_proj = w_proj + acc_proj[...]
        dgain = dgain + acc_vec[0:1, :]
        dshift = dshift + acc_vec[1:2, :]
        dbias = dbias + acc_vec[2:3, :]
    dfc[...] = w_fc
    dproj[...] = w_proj
    vec[0:1, :] = dgain
    vec[1:2, :] = dshift
    vec[2:3, :] = dbias


def ff_call(xs, cots, fc, proj, gain, shift, bias, acc):
    blocks, (rows, features) = len(xs), xs[0].shape
    hidden = fc.shape[1]
    total = blocks * rows
    first_call = acc is None
    operands = [*xs, *cots, fc, proj, gain, shift, bias] + ([] if first_call else list(acc))
    vmem = pl.BlockSpec(memory_space=pltpu.VMEM)
    aliases = {} if first_call else {2 * blocks + 5 + k: 2 + k for k in range(3)}
    return pl.pallas_call(
        partial(ff_kernel, blocks, first_call),
        out_shape=(
            jax.ShapeDtypeStruct((blocks, rows, features), low),
            jax.ShapeDtypeStruct((blocks, rows, features), low),
            jax.ShapeDtypeStruct((features, hidden), wide),
            jax.ShapeDtypeStruct((hidden, features), wide),
            jax.ShapeDtypeStruct((8, features), wide),
        ),
        in_specs=[vmem] * len(operands),
        out_specs=(vmem,) * 5,
        scratch_shapes=[
            pltpu.VMEM((total, features), low),
            pltpu.VMEM((total, hidden), low),
            pltpu.VMEM((total, hidden), low),
            pltpu.VMEM((total, features), low),
            pltpu.VMEM((8, features), wide),
        ],
        input_output_aliases=aliases,
        compiler_params=pltpu.CompilerParams(vmem_limit_bytes=44 * 2**20),
        cost_estimate=pl.CostEstimate(
            flops=12 * total * features * hidden,
            bytes_accessed=30 * 2**20,
            transcendentals=total * hidden,
        ),
        name="feed_forward",
    )(*operands)


def turn(block, cosine, sine):
    half = ROT // 2
    a, b = block[0:half], block[half:ROT]
    return jnp.concatenate(
        [a * cosine - b * sine, b * cosine + a * sine, block[ROT:]], axis=0
    )


def att_kernel(blocks, heads, first_call, *refs):
    me_ref, refs = refs[0], refs[1:]
    x_refs, refs = refs[:blocks], refs[blocks:]
    c_refs, refs = refs[:blocks], refs[blocks:]
    w, bias, wout, gain, shift, seg, cosine, sine, outp, ep = refs[:10]
    refs = refs[10:]
    if not first_call:
        acc_w, acc_o, acc_vec = refs[:3]
        refs = refs[3:]
    out_keep, out_send, e_keep, e_send, dw, dwo, vec = refs[:7]
    first_s, n_s, cot_s, wt_s, qt_s, kt_s, vt_s, k_s, v_s, dot_s, mask_s, att_s, d_s, dk_s, dv_s = refs[7:]
    me = me_ref[0]
    rows, features = x_refs[0].shape
    length = blocks * rows
    part = heads * HEAD
    reach = length // 2
    scale = 1.0 / math.sqrt(HEAD)

    wt_s[...] = jnp.transpose(w[...])

    seg_row = seg[...]
    seg_col = jnp.transpose(jnp.broadcast_to(seg_row, (128, length)))
    spans, place = [], 0
    for i in range(blocks):
        start = max(0, i * rows - reach)
        count = (i + 1) * rows - start
        spans.append((start, count, place))
        ours = seg_row[:, i * rows : (i + 1) * rows]
        theirs = seg_col[start : start + count]
        theirs = jnp.concatenate([theirs] * (rows // 128), axis=1)
        key = start + lax.broadcasted_iota(jnp.int32, (count, rows), 0)
        query = i * rows + lax.broadcasted_iota(jnp.int32, (count, rows), 1)
        allowed = (theirs == ours) & (key <= query)
        mask_s[place : place + count, :] = jnp.where(allowed, 0.0, far_below)
        place += count

    for j in range(blocks):
        off = pl.multiple_of((me ^ j) * rows, rows)
        n = row_norm(x_refs[j][...])
        n_s[pl.ds(off, rows), :] = n.astype(low)
        first = (n * gain[...] + shift[...]).astype(low)
        first_s[pl.ds(off, rows), :] = first
        cot = c_refs[j][...]
        cot_s[pl.ds(off, rows), :] = cot
        cos_b, sin_b = cosine[:, pl.ds(off, rows)], sine[:, pl.ds(off, rows)]
        made = nt(wt_s[...], first) + bias[...]
        for h in range(heads):
            lo, hi = h * HEAD, (h + 1) * HEAD
            query = turn(made[lo:hi], cos_b, sin_b).astype(low)
            qt_s[lo:hi, pl.ds(off, rows)] = (query.astype(wide) * scale).astype(low)
            key = turn(made[part + lo : part + hi], cos_b, sin_b).astype(low)
            kt_s[lo:hi, pl.ds(off, rows)] = key
            value = made[2 * part + lo : 2 * part + hi].astype(low)
            vt_s[lo:hi, pl.ds(off, rows)] = value
            k_s[h, pl.ds(off, rows), :] = jnp.transpose(key)
            v_s[h, pl.ds(off, rows), :] = jnp.transpose(value)
        dot_s[:, pl.ds(off, rows)] = nt(wout[...], cot).astype(low)

    dk_s[...] = jnp.zeros_like(dk_s)
    dv_s[...] = jnp.zeros_like(dv_s)

    def one_head(h, carry):
        base = pl.multiple_of(h * HEAD, HEAD)
        mine = pl.ds(base, HEAD)
        for i in range(blocks):
            start, count, place = spans[i]
            here, there = slice(i * rows, (i + 1) * rows), slice(start, start + count)
            query, grad = qt_s[mine, here], dot_s[mine, here]
            score = nn(k_s[h, there, :], query) + mask_s[place : place + count, :]
            top = jnp.max(score, axis=0, keepdims=True)
            lifted = jnp.exp2((score - top) * log2e)
            total = jnp.sum(lifted, axis=0, keepdims=True)
            prob = lifted * (1.0 / total)
            prob_low = prob.astype(low)
            att_s[mine, here] = nn(vt_s[mine, there], prob_low).astype(low)
            dprob = nn(v_s[h, there, :], grad)
            inner = jnp.sum(prob * dprob, axis=0, keepdims=True)
            dscore = (prob * (dprob - inner)).astype(low)
            dv_s[mine, there] += nt(grad, prob_low)
            dk_s[mine, there] += nt(query, dscore)
            dq = nn(kt_s[mine, there], dscore) * scale
            cos_b, sin_b = cosine[:, here], sine[:, here]
            d_s[mine, here] = turn(dq, cos_b, -sin_b).astype(low)
        return carry

    lax.fori_loop(0, heads, one_head, 0)
    for h in range(heads):
        lo, hi = h * HEAD, (h + 1) * HEAD
        d_s[part + lo : part + hi, :] = turn(dk_s[lo:hi, :], cosine[...], -sine[...]).astype(low)
    d_s[2 * part : 3 * part, :] = dv_s[...].astype(low)

    dgain = jnp.zeros((1, features), wide)
    dshift = jnp.zeros((1, features), wide)
    dbias = jnp.zeros((8, 3 * part), wide)
    for j in range(blocks):
        off = pl.multiple_of((me ^ j) * rows, rows)
        att = jnp.transpose(att_s[:, pl.ds(off, rows)])
        out = nn(att, wout[...]) + outp[j].astype(wide)
        dqkv = jnp.transpose(d_s[:, pl.ds(off, rows)])
        dbias = dbias + nn(jnp.ones((8, rows), low), dqkv)
        dfirst = nn(dqkv, wt_s[...])
        n = n_s[pl.ds(off, rows), :].astype(wide)
        dgain = dgain + jnp.sum(dfirst * n, axis=0, keepdims=True)
        dshift = dshift + jnp.sum(dfirst, axis=0, keepdims=True)
        e = dfirst * gain[...] + ep[j].astype(wide)
        (out_send if j % 2 else out_keep)[j // 2] = out.astype(low)
        (e_send if j % 2 else e_keep)[j // 2] = e.astype(low)
    g_w = nn(d_s[...], first_s[...])
    g_o = nn(att_s[...], cot_s[...])
    dbias = dbias[0:1]
    if not first_call:
        g_w = g_w + acc_w[...]
        g_o = g_o + acc_o[...]
        dgain = dgain + acc_vec[0:1, :]
        dshift = dshift + acc_vec[1:2, :]
        dbias = dbias + acc_vec[2:3, 0 : 3 * part]
    dw[...] = g_w
    dwo[...] = g_o
    vec[0:1, :] = dgain
    vec[1:2, :] = dshift
    vec[2:3, 0 : 3 * part] = dbias


def att_call(me, xs, cots, w, bias, wout, gain, shift, seg, cosine, sine, outp, ep, acc):
    blocks, (rows, features) = len(xs), xs[0].shape
    part = wout.shape[0]
    heads = part // HEAD
    length = blocks * rows
    first_call = acc is None
    operands = [me, *xs, *cots, w, bias, wout, gain, shift, seg, cosine, sine, outp, ep]
    base = len(operands)
    operands += [] if first_call else list(acc)
    vmem = pl.BlockSpec(memory_space=pltpu.VMEM)
    aliases = {} if first_call else {base + k: 4 + k for k in range(3)}
    half = jax.ShapeDtypeStruct((blocks // 2, rows, features), low)
    reach = length // 2
    masked = sum((i + 1) * rows - max(0, i * rows - reach) for i in range(blocks))
    return pl.pallas_call(
        partial(att_kernel, blocks, heads, first_call),
        out_shape=(
            half,
            half,
            half,
            half,
            jax.ShapeDtypeStruct((3 * part, features), wide),
            jax.ShapeDtypeStruct((part, features), wide),
            jax.ShapeDtypeStruct((8, features), wide),
        ),
        in_specs=[pl.BlockSpec(memory_space=pltpu.SMEM)] + [vmem] * (len(operands) - 1),
        out_specs=(vmem,) * 7,
        scratch_shapes=[
            pltpu.VMEM((length, features), low),
            pltpu.VMEM((length, features), low),
            pltpu.VMEM((length, features), low),
            pltpu.VMEM((3 * part, features), low),
            pltpu.VMEM((part, length), low),
            pltpu.VMEM((part, length), low),
            pltpu.VMEM((part, length), low),
            pltpu.VMEM((heads, length, HEAD), low),
            pltpu.VMEM((heads, length, HEAD), low),
            pltpu.VMEM((part, length), low),
            pltpu.VMEM((masked, rows), wide),
            pltpu.VMEM((part, length), low),
            pltpu.VMEM((3 * part, length), low),
            pltpu.VMEM((part, length), wide),
            pltpu.VMEM((part, length), wide),
        ],
        input_output_aliases=aliases,
        compiler_params=pltpu.CompilerParams(vmem_limit_bytes=50 * 2**20),
        cost_estimate=pl.CostEstimate(
            flops=24 * length * features * part + 12 * heads * masked * rows * 256,
            bytes_accessed=30 * 2**20,
            transcendentals=heads * masked * rows,
        ),
        name="attention",
    )(*operands)


def shards(
    tokens,
    segment,
    ln1_gain,
    ln1_bias,
    qkv_weight,
    qkv_bias,
    out_weight,
    out_bias,
    ln2_gain,
    ln2_bias,
    fc_weight,
    fc_bias,
    proj_weight,
    proj_bias,
    cotangent,
):
    ctx, fsdp, rep = lax.axis_size("ctx"), lax.axis_size("fsdp"), lax.axis_size("rep")
    c, f, r = lax.axis_index("ctx"), lax.axis_index("fsdp"), lax.axis_index("rep")
    paired = fsdp == 2 and ctx == 4 and rep == 4
    seqs, local_len, features = tokens.shape
    length = local_len * ctx
    owned = qkv_weight.shape[0]
    hidden_own = proj_weight.shape[0]
    hidden_all = fc_weight.shape[1]
    hidden = hidden_all // ctx
    part = features // ctx
    me = f * ctx + c

    def head_block(index):
        return ((index & 1) << 1) | (index >> 1) if paired else index

    vectors = (ln1_gain, ln1_bias, ln2_gain, ln2_bias, out_bias, proj_bias, qkv_bias, fc_bias)
    if paired:
        placed = jnp.concatenate(
            [
                lax.dynamic_update_slice(
                    jnp.zeros((v.shape[0] * fsdp * ctx,), low), v, (me * v.shape[0],)
                )
                for v in vectors
            ]
        ).reshape(-1, 128)
        for axis, bits in (("ctx", 2), ("ctx", 1), ("fsdp", 1)):
            placed = placed + swap(placed, axis, bits)
        placed = placed.reshape(-1)
        ends = np.cumsum([0] + [v.shape[0] * fsdp * ctx for v in vectors])
        vectors = [placed[int(a) : int(b)] for a, b in zip(ends[:-1], ends[1:])]
    else:
        vectors = [lax.all_gather(v, ("fsdp", "ctx"), axis=0, tiled=True) for v in vectors]
    gain_one, shift_one, gain_two, shift_two, b_out, b_proj, b_qkv, b_fc = [
        v.astype(wide) for v in vectors
    ]
    b_qkv = pick(b_qkv.reshape(3, ctx, part).transpose(1, 0, 2), head_block(c)).reshape(3 * part, 1)
    b_fc = pick(b_fc.reshape(fsdp, ctx, hidden_own).transpose(1, 0, 2), c).reshape(1, hidden)
    gain_one, shift_one, gain_two, shift_two = [
        v.reshape(1, features) for v in (gain_one, shift_one, gain_two, shift_two)
    ]

    qkv_cols = qkv_weight.reshape(owned, 3, ctx, part).transpose(2, 0, 1, 3).reshape(ctx, owned, 3 * part)
    fc_cols = fc_weight.reshape(owned, fsdp, ctx, hidden_own).transpose(2, 0, 1, 3).reshape(ctx, owned, hidden)

    def gather_columns(cols, block_of):
        rel = [pick(cols, block_of(c))]
        rel += [swap(pick(cols, block_of(c ^ k)), "ctx", k) for k in range(1, ctx)]
        mine = jnp.stack(in_order(rel, c))
        whole = in_order([mine, swap(mine, "fsdp", 1)], f)
        return jnp.stack(whole).reshape(features, cols.shape[2])

    def gather_columns_any(cols, block_of):
        whole = lax.all_gather(cols, ("fsdp", "ctx"), axis=1, tiled=True)
        return pick(whole, block_of(c))

    gather = gather_columns if paired else gather_columns_any
    w_qkv = gather(qkv_cols, head_block)
    w_fc = gather(fc_cols, lambda index: index)
    core = c & 1
    if paired:
        pair = jnp.concatenate(in_order([out_weight, swap(out_weight, "ctx", 1)], core))
        across = lax.ppermute(
            pair,
            ("fsdp", "ctx"),
            [((i & 1) * ctx + i, (1 - (i & 1)) * ctx + i) for i in range(ctx)],
        )
        w_out = jnp.where(core == f, pair, across)
        w_proj = jnp.concatenate(in_order([proj_weight, swap(proj_weight, "fsdp", 1)], f))
    else:
        w_out = lax.all_gather(out_weight, ("fsdp", "ctx"), axis=0, tiled=True)
        w_out = pick(w_out.reshape(ctx, part, features), c)
        w_proj = lax.all_gather(proj_weight, "fsdp", axis=0, tiled=True)

    def gather_rows(value):
        over = swap(value, "ctx", 2)
        return [value, swap(value, "ctx", 1), over, swap(over, "ctx", 1)]

    seg_all = jnp.concatenate(in_order(gather_rows(segment.astype(low)), c), axis=1).astype(wide)
    half = ROT // 2
    inverse = (1.0 / np.float32(10000.0) ** (np.arange(0, ROT, 2, dtype=np.float32) / ROT)).astype(np.float32)
    angles = inverse[:, None] * np.arange(length, dtype=np.float32)[None, :]
    cosine, sine = jnp.asarray(np.cos(angles)), jnp.asarray(np.sin(angles))
    me_arr = c.astype(jnp.int32).reshape(1)

    xs, cots = [], []
    for s in range(seqs):
        xs.append(gather_rows(tokens[s]))
        cots.append(gather_rows(cotangent[s]))

    def run_ff(s, acc):
        outp, ep, *acc = ff_call(xs[s], cots[s], w_fc, w_proj, gain_two, shift_two, b_fc, acc)
        return outp, ep, acc

    def run_att(s, outp, ep, acc):
        *parts, a, b, v = att_call(
            me_arr, xs[s], cots[s], w_qkv, b_qkv, w_out, gain_one, shift_one,
            seg_all[s : s + 1], cosine, sine, outp, ep, acc,
        )
        return parts, (a, b, v)

    ff_parts, ff_acc, att_acc, att_parts = [], None, None, []
    for s in range(seqs):
        outp, ep, ff_acc = run_ff(s, ff_acc)
        ff_parts.append((outp, ep))
        if s == 0:
            parts, att_acc = run_att(0, outp, ep, att_acc)
            att_parts.append(parts)
    for s in range(1, seqs):
        parts, att_acc = run_att(s, *ff_parts[s], att_acc)
        att_parts.append(parts)

    def own_rows(keep, send):
        got = swap(send, "ctx", 1)
        both = keep.astype(wide) + got.astype(wide)
        return both[0] + swap(both[1].astype(low), "ctx", 2).astype(wide)

    biases = (b_out + b_proj)[None, :]
    outputs, grads = [], []
    for s in range(seqs):
        out_keep, out_send, e_keep, e_send = att_parts[s]
        x = tokens[s].astype(wide)
        outputs.append((x + own_rows(out_keep, out_send) + biases).astype(low))
        e = own_rows(e_keep, e_send)
        center = x - jnp.mean(x, axis=-1, keepdims=True)
        spread = jnp.mean(center * center, axis=-1, keepdims=True)
        root = lax.rsqrt(spread + epsilon)
        n = center * root
        back = root * (
            e - jnp.mean(e, axis=-1, keepdims=True) - n * jnp.mean(e * n, axis=-1, keepdims=True)
        )
        grads.append((cotangent[s].astype(wide) + back).astype(low))
    output, grad_tokens = jnp.stack(outputs), jnp.stack(grads)

    d_fc, d_proj, ff_vec = ff_acc
    d_qkv, d_out, att_vec = att_acc
    d_qkv = jnp.transpose(d_qkv)

    def across_fsdp(grad):
        parts = grad.reshape(fsdp, -1, grad.shape[1])
        got = swap(pick(parts, 1 - f).astype(low), "fsdp", 1)
        return pick(parts, f) + got.astype(wide)

    def scatter_rep(parts):
        total = pick(parts, r)
        for k in range(1, rep):
            total = total + swap(pick(parts, r ^ k).astype(low), "rep", k).astype(wide)
        return total.astype(low)

    def gather_rep(piece):
        return in_order([piece] + [swap(piece, "rep", k) for k in range(1, rep)], r)

    def reduce_columns(grad):
        cols = grad.shape[1]
        mine = across_fsdp(grad).reshape(ctx, rep, owned // rep, cols)
        total = scatter_rep(mine.transpose(1, 0, 2, 3))
        rel = [pick(total, c)] + [swap(pick(total, c ^ k), "ctx", k) for k in range(1, ctx)]
        return jnp.concatenate(gather_rep(jnp.stack(in_order(rel, c), axis=1)))

    def reduce_rows(mine):
        total = scatter_rep(mine.reshape(rep, -1, mine.shape[1]))
        return jnp.concatenate(gather_rep(total))

    if paired:
        g_fc = reduce_columns(d_fc)
        g_qkv = reduce_columns(d_qkv)
        g_proj = reduce_rows(across_fsdp(d_proj))
        got = lax.ppermute(
            d_out.astype(low),
            ("fsdp", "ctx"),
            [((1 - (i & 1)) * ctx + i, (i & 1) * ctx + i) for i in range(ctx)],
        )
        halves = (d_out + got.astype(wide)).reshape(2, owned, features)
        got = lax.ppermute(
            pick(halves, 1 - core).astype(low),
            ("fsdp", "ctx"),
            [(k * ctx + i, k * ctx + (i ^ 1)) for k in range(fsdp) for i in range(ctx) if (i & 1) == k],
        )
        g_out = reduce_rows(jnp.where(core == f, pick(halves, core), got.astype(wide)))
    else:

        def any_columns(grad):
            grad = lax.psum_scatter(grad.astype(low), "fsdp", scatter_dimension=0, tiled=True)
            grad = lax.psum(grad, "rep")
            return lax.all_to_all(
                grad.reshape(ctx, owned, -1), "ctx", split_axis=0, concat_axis=0
            ).transpose(1, 0, 2)

        g_fc, g_qkv = any_columns(d_fc), any_columns(d_qkv)
        g_proj = lax.psum(
            lax.psum_scatter(d_proj.astype(low), "fsdp", scatter_dimension=0, tiled=True), "rep"
        )
        d_out = jnp.where(jnp.arange(ctx)[:, None, None] == c, d_out[None], 0.0)
        g_out = lax.psum(
            lax.psum_scatter(
                d_out.reshape(features, features).astype(low),
                ("fsdp", "ctx"),
                scatter_dimension=0,
                tiled=True,
            ),
            "rep",
        )
    g_fc = g_fc.reshape(owned, ctx, fsdp, hidden_own).transpose(0, 2, 1, 3).reshape(owned, hidden_all)
    order = [head_block(k) for k in range(ctx)]
    g_qkv = g_qkv.reshape(owned, ctx, 3, part)
    g_qkv = jnp.stack([g_qkv[:, order.index(k)] for k in range(ctx)], axis=2).reshape(owned, 3 * features)

    bias_sum = jnp.sum(cotangent.astype(wide), axis=(0, 1))
    d_b_qkv = jnp.where(
        (jnp.arange(ctx) == head_block(c))[None, :, None],
        att_vec[2, : 3 * part].reshape(3, 1, part),
        0.0,
    ).reshape(-1)
    d_b_fc = jnp.where(
        (jnp.arange(ctx) == c)[None, :, None], ff_vec[2].reshape(fsdp, 1, hidden_own), 0.0
    ).reshape(-1)
    small = (att_vec[0], att_vec[1], ff_vec[0], ff_vec[1], bias_sum, d_b_qkv, d_b_fc)
    summed = jnp.concatenate(small).reshape(-1, 128)
    if paired:
        for axis, bits in (("ctx", 1), ("ctx", 2), ("fsdp", 1), ("rep", 1), ("rep", 2)):
            summed = summed + swap(summed, axis, bits)
    else:
        summed = lax.psum(summed, ("ctx", "fsdp", "rep"))
    summed = summed.reshape(-1)
    ends = np.cumsum([0] + [v.shape[0] for v in small])
    mine = []
    for a, v in zip(ends, small):
        size = v.shape[0] // (fsdp * ctx)
        mine.append(lax.dynamic_slice(summed, (int(a) + me * size,), (size,)))
    g_gain_one, g_shift_one, g_gain_two, g_shift_two, g_bias, g_b_qkv, g_b_fc = mine
    return (
        output,
        grad_tokens,
        g_gain_one,
        g_shift_one,
        g_qkv.astype(wide),
        g_b_qkv,
        g_out.astype(wide),
        g_bias,
        g_gain_two,
        g_shift_two,
        g_fc.astype(wide),
        g_b_fc,
        g_proj.astype(wide),
        g_bias,
    )


def solution(mesh):
    rows, row = P(("rep", "fsdp"), "ctx", None), P(("rep", "fsdp"), "ctx")
    vector, matrix = P(("fsdp", "ctx")), P(("fsdp", "ctx"), None)
    params = (
        vector, vector, matrix, vector, matrix, vector,
        vector, vector, matrix, vector, matrix, vector,
    )
    return jax.shard_map(
        shards,
        mesh=mesh,
        in_specs=(rows, row, *params, rows),
        out_specs=(rows, rows, *params),
        check_vma=False,
    )
```

```python
from functools import partial
import math

import jax
import jax.numpy as jnp
import numpy as np
from jax import lax
from jax.experimental import pallas as pl
from jax.experimental.pallas import tpu as pltpu
from jax.sharding import PartitionSpec as P

HEADS = 12
HEAD = 64
ROT = 16

epsilon = 1e-05
far_below = -1e30
low = jnp.bfloat16
wide = jnp.float32
log2e = math.log2(math.e)


def nn(a, b):
    return lax.dot_general(a, b, (((1,), (0,)), ((), ())), preferred_element_type=wide)


def nt(a, b):
    return lax.dot_general(a, b, (((1,), (1,)), ((), ())), preferred_element_type=wide)


def swap(value, axis, bits):
    size = lax.axis_size(axis)
    return lax.ppermute(value, axis, [(i, i ^ bits) for i in range(size)])


def in_order(rel, me):
    out = []
    for k in range(len(rel)):
        value = rel[k]
        for m in range(1, len(rel)):
            value = jnp.where(me == m, rel[k ^ m], value)
        out.append(value)
    return out


def pick(stacked, index):
    return lax.dynamic_index_in_dim(stacked, index, 0, keepdims=False)


def after(value, *before):
    return lax.optimization_barrier((value, before))[0]


anywhere = pl.BlockSpec(memory_space=pl.ANY)
in_vmem = pl.BlockSpec(memory_space=pltpu.VMEM)
in_smem = pl.BlockSpec(memory_space=pltpu.SMEM)
extra_rows = 16


def head_block(index):
    return ((index & 1) << 1) | (index >> 1)


def pack_kernel(vectors, me_ref, qkv, fc, segment, *refs):
    vector_refs, refs = refs[:vectors], refs[vectors:]
    q0, q1, q2, q3, f0, f1, f2, f3, scratch, extra = refs
    c = me_ref[0]
    owned, part, unit = qkv.shape[0], qkv.shape[1] // 12, fc.shape[1] // 8
    extra[...] = jnp.zeros_like(extra)
    for row, ref in enumerate(vector_refs):
        extra[row : row + 1, 0 : ref.shape[0]] = ref[...].astype(wide).reshape(1, -1)
    extra[8 : 8 + segment.shape[0], 0 : segment.shape[1]] = segment[...].astype(wide)
    for k in range(4):
        block = head_block(k)
        for t in range(3):
            lo = (4 * t + block) * part
            scratch[k ^ c, :, t * part : (t + 1) * part] = qkv[:, lo : lo + part]
    for k, (q, g) in enumerate(((q0, f0), (q1, f1), (q2, f2), (q3, f3))):
        q[...] = scratch[k]
        for t in range(2):
            lo = pl.multiple_of((4 * t + (c ^ k)) * unit, 128)
            g[0:owned, t * unit : (t + 1) * unit] = fc[:, pl.ds(lo, unit)]
        g[owned:, :] = extra[...].astype(low)


def pack_call(me, qkv, fc, segment, vectors):
    owned = qkv.shape[0]
    narrow, broad = (owned, qkv.shape[1] // 4), (owned + extra_rows, fc.shape[1] // 4)
    shapes = (narrow,) * 4 + (broad,) * 4
    return pl.pallas_call(
        partial(pack_kernel, len(vectors)),
        out_shape=tuple(jax.ShapeDtypeStruct(s, low) for s in shapes),
        in_specs=[in_smem] + [in_vmem] * (3 + len(vectors)),
        out_specs=(in_vmem,) * 8,
        scratch_shapes=[
            pltpu.VMEM((4, owned, narrow[1]), low),
            pltpu.VMEM((extra_rows, broad[1]), wide),
        ],
        name="pack_columns",
    )(me, qkv, fc, segment, *vectors)


def rows_kernel(owned, me_ref, p0, p1, p2, p3, half):
    c = me_ref[0]
    tail = p0.shape[0] - owned
    for k, p in enumerate((p0, p1, p2, p3)):
        half[pl.ds(pl.multiple_of((c ^ k) * owned, 16), owned), :] = p[0:owned, :]
        if tail:
            half[pl.ds(pl.multiple_of(4 * owned + (c ^ k) * tail, 16), tail), :] = p[owned:, :]


def rows_call(me, owned, pieces):
    rows, cols = pieces[0].shape
    return pl.pallas_call(
        partial(rows_kernel, owned),
        out_shape=jax.ShapeDtypeStruct((4 * rows, cols), low),
        in_specs=[in_smem] + [in_vmem] * 4,
        out_specs=in_vmem,
        name="rows_by_ctx",
    )(me, *pieces)


def prep_kernel(owned, part, seqs, me_ref, mine, other, vecs, bias, seg):
    c, f = me_ref[0], me_ref[1]
    extra_mine, extra_other = mine[...].astype(wide), other[...].astype(wide)
    first = jnp.where(f == 0, extra_mine, extra_other)
    last = jnp.where(f == 0, extra_other, extra_mine)

    def vector(row, size):
        pieces = [
            e[k * extra_rows + row : k * extra_rows + row + 1, 0:size]
            for e in (first, last)
            for k in range(4)
        ]
        return jnp.concatenate(pieces, axis=1)

    block = head_block(c)
    vecs[...] = jnp.zeros_like(vecs)
    for row in range(4):
        vecs[row : row + 1, :] = vector(row, owned)
    vecs[4:5, :] = vector(4, owned) + vector(5, owned)
    unit = mine.shape[1] // 2
    for t, e in enumerate((first, last)):
        chosen = e[7:8, 0:unit]
        for k in range(1, 4):
            chosen = jnp.where(c == k, e[k * extra_rows + 7 : k * extra_rows + 8, 0:unit], chosen)
        vecs[5:6, t * unit : (t + 1) * unit] = chosen
    all_qkv = vector(6, 3 * owned)
    picked = []
    for t in range(3):
        chosen = all_qkv[:, 4 * t * part : (4 * t + 1) * part]
        for k in range(1, 4):
            chosen = jnp.where(block == k, all_qkv[:, (4 * t + k) * part : (4 * t + k + 1) * part], chosen)
        picked.append(chosen)
    row_bias = jnp.concatenate(picked, axis=1)
    bias[...] = jnp.transpose(jnp.broadcast_to(row_bias, (128, 3 * part)))
    seg[...] = jnp.zeros_like(seg)
    width = seg.shape[1] // 4
    for s in range(seqs):
        for k in range(4):
            row = k * extra_rows + 8 + s
            seg[s : s + 1, k * width : (k + 1) * width] = extra_mine[row : row + 1, 0:width]


def prep_call(me, owned, part, seqs, length, mine, other):
    tail = pl.BlockSpec((4 * extra_rows, mine.shape[1]), lambda i: (4 * owned // (4 * extra_rows), 0))
    assert 4 * owned % (4 * extra_rows) == 0
    shapes = ((8, 8 * owned), (3 * part, 128), (8, length))
    return pl.pallas_call(
        partial(prep_kernel, owned, part, seqs),
        grid=(1,),
        out_shape=tuple(jax.ShapeDtypeStruct(s, wide) for s in shapes),
        in_specs=[in_smem, tail, tail],
        out_specs=tuple(pl.BlockSpec(s, lambda i: (0, 0)) for s in shapes),
        name="prepare_vectors",
    )(me, mine, other)


def row_norm(block):
    values = block.astype(wide)
    center = values - jnp.mean(values, axis=-1, keepdims=True)
    spread = jnp.mean(center * center, axis=-1, keepdims=True)
    return center * lax.rsqrt(spread + epsilon)


def gelu_parts(v):
    bell = jnp.exp2(v * v * (-0.5 * log2e))
    base = 1.0 + (0.3275911 / math.sqrt(2.0)) * jnp.abs(v)
    t = pl.reciprocal(base, approx=True)
    t = t * (2.0 - base * t)
    poly = 0.5 * 1.061405429
    for coef in (-1.453152027, 1.421413741, -0.284496736, 0.254829592):
        poly = poly * t + 0.5 * coef
    tail = poly * t * bell
    phi = jnp.where(v >= 0, 1.0 - tail, tail)
    return phi, phi + v * bell * (1.0 / math.sqrt(2.0 * math.pi))


def bring(pairs, sem):
    copies = [pltpu.make_async_copy(a, b, sem.at[k]) for k, (a, b) in enumerate(pairs)]
    for copy in copies:
        copy.start()
    return copies


def token_pairs(s, refs, xs, cs):
    tok, cot, tok1, cot1, far, far1 = refs
    pairs = []
    for j, (t, c) in enumerate(
        ((tok.at[s], cot.at[s]), (tok1.at[s], cot1.at[s]), (far.at[0], far.at[1]), (far1.at[0], far1.at[1]))
    ):
        pairs += [(t, xs.at[j]), (c, cs.at[j])]
    return pairs


def ff_kernel(s, with_acc, with_part, is_last, *refs):
    me_ref, refs = refs[0], refs[1:]
    token_refs, refs = refs[:6], refs[6:]
    fc_a, fc_b, proj_a, proj_b, vecs = refs[:5]
    refs = refs[5:]
    if with_acc:
        acc_fc_in, acc_proj_in, acc_vec_in = refs[:3]
        refs = refs[3:]
    if with_part:
        part_send, part_keep = refs[:2]
        refs = refs[2:]
    send, keep = refs[:2]
    refs = refs[2:]
    if is_last:
        grad_keep, grad_send, vec = refs[:3]
        refs = refs[3:]
    else:
        fc_out, proj_out, vec = refs[:3]
        refs = refs[3:]
    xs, cs, fc, proj, sec_s, hid_s, gp_s, send_s, keep_s, acc_fc, acc_proj, sem, sem_w, sem_p, sem_o = refs
    f = me_ref[1]
    blocks, rows, features = xs.shape
    hidden = fc.shape[1]
    third, half = features // 2, proj_a.shape[0]
    tokens_in = bring(token_pairs(s, token_refs, xs, cs), sem)
    weights_in = bring(
        [
            (fc_a.at[0:third], fc.at[pl.ds(pl.multiple_of(f * third, 16), third), :]),
            (fc_b.at[0:third], fc.at[pl.ds(pl.multiple_of((1 - f) * third, 16), third), :]),
            (proj_a, proj.at[pl.ds(pl.multiple_of(f * half, 16), half), :]),
            (proj_b, proj.at[pl.ds(pl.multiple_of((1 - f) * half, 16), half), :]),
        ],
        sem_w,
    )
    later = []
    if with_part:
        later += [(part_send, send_s), (part_keep, keep_s)]
    if with_acc:
        later += [(acc_fc_in, acc_fc), (acc_proj_in, acc_proj)]
    later = bring(later, sem_p)
    for copy in weights_in:
        copy.wait()
    gain, shift, bias = vecs[2:3, :], vecs[3:4, :], vecs[5:6, 0:hidden]
    dgain = jnp.zeros((1, features), wide)
    dshift = jnp.zeros((1, features), wide)
    dbias = jnp.zeros((1, hidden), wide)
    if with_part:
        later[0].wait()
        later[1].wait()
    for j in range(blocks):
        here = pl.ds(j * rows, rows)
        tokens_in[2 * j].wait()
        tokens_in[2 * j + 1].wait()
        n = row_norm(xs[j])
        second = (n * gain + shift).astype(low)
        sec_s[here, :] = second
        cot = cs[j]
        pre = nn(second, fc[...]) + bias
        phi, slope = gelu_parts(pre)
        hid = (pre * phi).astype(low)
        gp = nt(cot, proj[...]) * slope
        dbias = dbias + jnp.sum(gp, axis=0, keepdims=True)
        gp = gp.astype(low)
        hid_s[here, :] = hid
        gp_s[here, :] = gp
        out = nn(hid, proj[...])
        dsec = nt(gp, fc[...])
        dgain = dgain + jnp.sum(dsec * n, axis=0, keepdims=True)
        dshift = dshift + jnp.sum(dsec, axis=0, keepdims=True)
        e = dsec * gain
        to = send_s if j % 2 else keep_s
        if with_part:
            out = out + to[j // 2 * 2].astype(wide)
            e = e + to[j // 2 * 2 + 1].astype(wide)
        to[j // 2 * 2] = out.astype(low)
        to[j // 2 * 2 + 1] = e.astype(low)
    results = bring([(send_s, send), (keep_s, keep)], sem_o)
    dcot = jnp.sum(cs[0].astype(wide), axis=0, keepdims=True)
    w_fc = nn(jnp.transpose(sec_s[...]), gp_s[...])
    w_proj = nn(jnp.transpose(hid_s[...]), cs[...].reshape(blocks * rows, features))
    if with_acc:
        later[-2].wait()
        later[-1].wait()
        w_fc = w_fc + acc_fc[...]
        w_proj = w_proj + acc_proj[...]
        dgain = dgain + acc_vec_in[0:1, :]
        dshift = dshift + acc_vec_in[1:2, :]
        dbias = dbias + acc_vec_in[2:3, 0:hidden]
        dcot = dcot + acc_vec_in[3:4, :]
    acc_fc[...] = w_fc
    if is_last:
        acc_proj[...] = w_proj
        mine, away = pl.ds(pl.multiple_of(f * third, 16), third), pl.ds(pl.multiple_of((1 - f) * third, 16), third)
        grad_keep[0:third, :] = acc_fc[mine, :]
        grad_send[0:third, :] = acc_fc[away, :].astype(low)
        mine, away = pl.ds(pl.multiple_of(f * half, 16), half), pl.ds(pl.multiple_of((1 - f) * half, 16), half)
        grad_keep[third:, :] = acc_proj[mine, :]
        grad_send[third:, :] = acc_proj[away, :].astype(low)
    else:
        acc_proj[...] = w_proj
        more = [
            pltpu.make_async_copy(acc_fc, fc_out, sem_o.at[2]),
            pltpu.make_async_copy(acc_proj, proj_out, sem_o.at[3]),
        ]
        for copy in more:
            copy.start()
        results += more
    vec[0:1, :] = dgain
    vec[1:2, :] = dshift
    vec[2:3, 0:hidden] = dbias
    vec[3:4, :] = dcot
    for copy in results:
        copy.wait()


def ff_call(s, me, token_args, fc_a, fc_b, proj_a, proj_b, vecs, acc, part, is_last):
    rows, features = token_args[0].shape[1:]
    hidden, blocks = fc_a.shape[1], 4
    total = blocks * rows
    third = features // 2
    operands = [me, *token_args, fc_a, fc_b, proj_a, proj_b, vecs]
    specs = [in_smem] + [anywhere] * 10 + [in_vmem]
    aliases = {}
    if acc is not None:
        if not is_last:
            aliases = {len(operands): 2, len(operands) + 1: 3}
        operands += list(acc)
        specs += [anywhere, anywhere, in_vmem]
    if part is not None:
        aliases[len(operands)] = 0
        aliases[len(operands) + 1] = 1
        operands += list(part)
        specs += [anywhere, anywhere]
    shared = jax.ShapeDtypeStruct((4, rows, features), low)
    vec = jax.ShapeDtypeStruct((8, features), wide)
    if is_last:
        rows_out = third + proj_a.shape[0]
        grads = (
            jax.ShapeDtypeStruct((rows_out, features), wide),
            jax.ShapeDtypeStruct((rows_out, features), low),
        )
        grad_specs = (in_vmem,) * 2
    else:
        grads = (
            jax.ShapeDtypeStruct((features, hidden), wide),
            jax.ShapeDtypeStruct((hidden, features), wide),
        )
        grad_specs = (anywhere,) * 2
    return pl.pallas_call(
        partial(ff_kernel, s, acc is not None, part is not None, is_last),
        out_shape=(shared, shared, *grads, vec),
        in_specs=specs,
        out_specs=(anywhere, anywhere, *grad_specs, in_vmem),
        scratch_shapes=[
            pltpu.VMEM((blocks, rows, features), low),
            pltpu.VMEM((blocks, rows, features), low),
            pltpu.VMEM((features, hidden), low),
            pltpu.VMEM((hidden, features), low),
            pltpu.VMEM((total, features), low),
            pltpu.VMEM((total, hidden), low),
            pltpu.VMEM((total, hidden), low),
            pltpu.VMEM((4, rows, features), low),
            pltpu.VMEM((4, rows, features), low),
            pltpu.VMEM((features, hidden), wide),
            pltpu.VMEM((hidden, features), wide),
            pltpu.SemaphoreType.DMA((8,)),
            pltpu.SemaphoreType.DMA((4,)),
            pltpu.SemaphoreType.DMA((4,)),
            pltpu.SemaphoreType.DMA((4,)),
        ],
        input_output_aliases=aliases,
        compiler_params=pltpu.CompilerParams(vmem_limit_bytes=48 * 2**20),
        cost_estimate=pl.CostEstimate(flops=1, bytes_accessed=1, transcendentals=0),
        name="feed_forward",
    )(*operands)


def turn(block, cosine, sine):
    half = ROT // 2
    a, b = block[0:half], block[half:ROT]
    return jnp.concatenate([a * cosine - b * sine, b * cosine + a * sine, block[ROT:]], axis=0)


def att_kernel(s, heads, with_acc, with_part, is_last, *refs):
    me_ref, refs = refs[0], refs[1:]
    token_refs, refs = refs[:6], refs[6:]
    w_a, w_b, bias, wout_a, wout_b, vecs, segs, cosine, sine = refs[:9]
    refs = refs[9:]
    if is_last:
        ff_vec, refs = refs[0], refs[1:]
    if with_acc:
        acc_w_in, acc_o_in, acc_vec_in = refs[:3]
        refs = refs[3:]
    if with_part:
        part_send, part_keep = refs[:2]
        refs = refs[2:]
    send, keep = refs[:2]
    refs = refs[2:]
    if is_last:
        w_keep, w_send, o_keep, o_send, o_send_far, vec = refs[:6]
        refs = refs[6:]
    else:
        w_out, o_out, vec = refs[:3]
        refs = refs[3:]
    xs, cs, wt_s, wout, first_s, n_s, cot_s, qt_s, kt_s, vt_s, k_s, v_s, dot_s, mask_s, att_s, d_s, dk_s, dv_s = refs[:18]
    send_s, keep_s, acc_w, acc_o, sem, sem_p, sem_o = refs[18:]
    me, f, core = me_ref[0], me_ref[1], me_ref[2]
    blocks, rows, features = xs.shape
    part = heads * HEAD
    length = blocks * rows
    reach = length // 2
    scale = 1.0 / math.sqrt(HEAD)
    tokens_in = bring(token_pairs(s, token_refs, xs, cs), sem)
    later = []
    if with_part:
        later += [(part_send, send_s), (part_keep, keep_s)]
    if with_acc:
        later += [(acc_w_in, acc_w), (acc_o_in, acc_o)]
    later = bring(later, sem_p)
    gain, shift = vecs[0:1, :], vecs[1:2, :]
    share = w_a.shape[0]
    wt_s[:, pl.ds(pl.multiple_of(f * share, 128), share)] = jnp.transpose(w_a[...])
    wt_s[:, pl.ds(pl.multiple_of((1 - f) * share, 128), share)] = jnp.transpose(w_b[...])
    owned = wout_a.shape[0]
    wout[pl.ds(pl.multiple_of(core * owned, 16), owned), :] = wout_a[...]
    wout[pl.ds(pl.multiple_of((1 - core) * owned, 16), owned), :] = wout_b[...]

    seg_row = segs[s : s + 1, :]
    seg_col = jnp.transpose(jnp.broadcast_to(seg_row, (128, length)))
    spans, place = [], 0
    for i in range(blocks):
        start = max(0, i * rows - reach)
        count = (i + 1) * rows - start
        spans.append((start, count, place))
        ours = seg_row[:, i * rows : (i + 1) * rows]
        theirs = seg_col[start : start + count]
        theirs = jnp.concatenate([theirs] * (rows // 128), axis=1)
        key = start + lax.broadcasted_iota(jnp.int32, (count, rows), 0)
        query = i * rows + lax.broadcasted_iota(jnp.int32, (count, rows), 1)
        allowed = (theirs == ours) & (key <= query)
        mask_s[place : place + count, :] = jnp.where(allowed, 0.0, far_below)
        place += count

    wide_bias = jnp.concatenate([bias[...]] * (rows // 128), axis=1)
    for j in range(blocks):
        off = pl.multiple_of((me ^ j) * rows, rows)
        tokens_in[2 * j].wait()
        tokens_in[2 * j + 1].wait()
        n = row_norm(xs[j])
        n_s[pl.ds(off, rows), :] = n.astype(low)
        first = (n * gain + shift).astype(low)
        first_s[pl.ds(off, rows), :] = first
        cot = cs[j]
        cot_s[pl.ds(off, rows), :] = cot
        cos_b, sin_b = cosine[:, pl.ds(off, rows)], sine[:, pl.ds(off, rows)]
        made = nt(wt_s[...], first) + wide_bias
        for h in range(heads):
            lo, hi = h * HEAD, (h + 1) * HEAD
            query = turn(made[lo:hi], cos_b, sin_b).astype(low)
            qt_s[lo:hi, pl.ds(off, rows)] = (query.astype(wide) * scale).astype(low)
            key = turn(made[part + lo : part + hi], cos_b, sin_b).astype(low)
            kt_s[lo:hi, pl.ds(off, rows)] = key
            value = made[2 * part + lo : 2 * part + hi].astype(low)
            vt_s[lo:hi, pl.ds(off, rows)] = value
            k_s[h, pl.ds(off, rows), :] = jnp.transpose(key)
            v_s[h, pl.ds(off, rows), :] = jnp.transpose(value)
        dot_s[:, pl.ds(off, rows)] = nt(wout[...], cot).astype(low)

    dk_s[...] = jnp.zeros_like(dk_s)
    dv_s[...] = jnp.zeros_like(dv_s)

    def one_head(h, carry):
        base = pl.multiple_of(h * HEAD, HEAD)
        mine = pl.ds(base, HEAD)
        for i in range(blocks):
            start, count, place = spans[i]
            here, there = slice(i * rows, (i + 1) * rows), slice(start, start + count)
            query, grad = qt_s[mine, here], dot_s[mine, here]
            score = nn(k_s[h, there, :], query) + mask_s[place : place + count, :]
            top = jnp.max(score, axis=0, keepdims=True)
            lifted = jnp.exp2((score - top) * log2e)
            total = jnp.sum(lifted, axis=0, keepdims=True)
            prob = lifted * (1.0 / total)
            prob_low = prob.astype(low)
            att_s[mine, here] = nn(vt_s[mine, there], prob_low).astype(low)
            dprob = nn(v_s[h, there, :], grad)
            inner = jnp.sum(prob * dprob, axis=0, keepdims=True)
            dscore = (prob * (dprob - inner)).astype(low)
            dv_s[mine, there] += nt(grad, prob_low)
            dk_s[mine, there] += nt(query, dscore)
            dq = nn(kt_s[mine, there], dscore) * scale
            cos_b, sin_b = cosine[:, here], sine[:, here]
            d_s[mine, here] = turn(dq, cos_b, -sin_b).astype(low)
        return carry

    lax.fori_loop(0, heads, one_head, 0)
    for h in range(heads):
        lo, hi = h * HEAD, (h + 1) * HEAD
        d_s[part + lo : part + hi, :] = turn(dk_s[lo:hi, :], cosine[...], -sine[...]).astype(low)
    d_s[2 * part : 3 * part, :] = dv_s[...].astype(low)

    g_w = nn(d_s[...], first_s[...])
    g_o = nn(att_s[...], cot_s[...])
    if with_part:
        later[0].wait()
        later[1].wait()
    if with_acc:
        later[-2].wait()
        later[-1].wait()
        g_w = g_w + acc_w[...]
        g_o = g_o + acc_o[...]
    acc_w[...] = g_w
    results = []
    if is_last:
        w_keep[...] = jnp.transpose(acc_w[:, pl.ds(pl.multiple_of(f * share, 128), share)])
        w_send[...] = jnp.transpose(acc_w[:, pl.ds(pl.multiple_of((1 - f) * share, 128), share)]).astype(low)
        acc_o[...] = g_o
        mine = acc_o[pl.ds(pl.multiple_of(f * owned, 16), owned), :]
        o_keep[...] = jnp.where(f == core, mine, 0.0)
        o_send[...] = acc_o[pl.ds(pl.multiple_of((1 - f) * owned, 16), owned), :].astype(low)
        o_send_far[...] = mine.astype(low)
    else:
        acc_o[...] = g_o
        results = [
            pltpu.make_async_copy(acc_w, w_out, sem_o.at[2]),
            pltpu.make_async_copy(acc_o, o_out, sem_o.at[3]),
        ]
        for copy in results:
            copy.start()
    dgain = jnp.zeros((1, features), wide)
    dshift = jnp.zeros((1, features), wide)
    dbias = jnp.zeros((8, 3 * part), wide)
    for j in range(blocks):
        off = pl.multiple_of((me ^ j) * rows, rows)
        att = jnp.transpose(att_s[:, pl.ds(off, rows)])
        out = nn(att, wout[...])
        dqkv = jnp.transpose(d_s[:, pl.ds(off, rows)])
        dbias = dbias + nn(jnp.ones((8, rows), low), dqkv)
        dfirst = nn(dqkv, wt_s[...])
        n = n_s[pl.ds(off, rows), :].astype(wide)
        dgain = dgain + jnp.sum(dfirst * n, axis=0, keepdims=True)
        dshift = dshift + jnp.sum(dfirst, axis=0, keepdims=True)
        e = dfirst * gain
        to = send_s if j % 2 else keep_s
        if with_part:
            out = out + to[j // 2 * 2].astype(wide)
            e = e + to[j // 2 * 2 + 1].astype(wide)
        to[j // 2 * 2] = out.astype(low)
        to[j // 2 * 2 + 1] = e.astype(low)
    results += bring([(send_s, send), (keep_s, keep)], sem_o)
    dbias = dbias[0:1]
    if with_acc:
        dgain = dgain + acc_vec_in[0:1, :]
        dshift = dshift + acc_vec_in[1:2, :]
        dbias = dbias + acc_vec_in[2:3, 0 : 3 * part]
    if is_last:
        vec[...] = jnp.zeros_like(vec)
        vec[2:5, :] = jnp.concatenate([ff_vec[0:2, :], ff_vec[3:4, :]])
        vec[pl.ds(5 + me, 1), :] = ff_vec[2:3, :]
        vec[pl.ds(9 + me, 1), 0 : 3 * part] = dbias
    else:
        vec[2:3, 0 : 3 * part] = dbias
    vec[0:1, :] = dgain
    vec[1:2, :] = dshift
    for copy in results:
        copy.wait()


def att_call(s, me, token_args, w_a, w_b, bias, wout_a, wout_b, vecs, segs, cosine, sine, acc, part_in, ff_vec):
    rows, features = token_args[0].shape[1:]
    part, blocks = w_a.shape[1] // 3, 4
    heads = part // HEAD
    length = blocks * rows
    is_last = ff_vec is not None
    operands = [me, *token_args, w_a, w_b, bias, wout_a, wout_b, vecs, segs, cosine, sine]
    operands += [ff_vec] if is_last else []
    specs = [in_smem] + [anywhere] * 6 + [in_vmem] * (len(operands) - 7)
    aliases = {}
    if acc is not None:
        if not is_last:
            aliases = {len(operands): 2, len(operands) + 1: 3}
        operands += list(acc)
        specs += [anywhere, anywhere, in_vmem]
    if part_in is not None:
        aliases[len(operands)] = 0
        aliases[len(operands) + 1] = 1
        operands += list(part_in)
        specs += [anywhere, anywhere]
    shared = jax.ShapeDtypeStruct((4, rows, features), low)
    vec = jax.ShapeDtypeStruct((16 if is_last else 8, features), wide)
    if is_last:
        grads = (
            jax.ShapeDtypeStruct((features // 2, 3 * part), wide),
            jax.ShapeDtypeStruct((features // 2, 3 * part), low),
            jax.ShapeDtypeStruct((part // 2, features), wide),
            jax.ShapeDtypeStruct((part // 2, features), low),
            jax.ShapeDtypeStruct((part // 2, features), low),
        )
        grad_specs = (in_vmem,) * 5
    else:
        grads = (
            jax.ShapeDtypeStruct((3 * part, features), wide),
            jax.ShapeDtypeStruct((part, features), wide),
        )
        grad_specs = (anywhere,) * 2
    reach = length // 2
    masked = sum((i + 1) * rows - max(0, i * rows - reach) for i in range(blocks))
    return pl.pallas_call(
        partial(att_kernel, s, heads, acc is not None, part_in is not None, is_last),
        out_shape=(shared, shared, *grads, vec),
        in_specs=specs,
        out_specs=(anywhere, anywhere, *grad_specs, in_vmem),
        scratch_shapes=[
            pltpu.VMEM((blocks, rows, features), low),
            pltpu.VMEM((blocks, rows, features), low),
            pltpu.VMEM((3 * part, features), low),
            pltpu.VMEM((part, features), low),
            pltpu.VMEM((length, features), low),
            pltpu.VMEM((length, features), low),
            pltpu.VMEM((length, features), low),
            pltpu.VMEM((part, length), low),
            pltpu.VMEM((part, length), low),
            pltpu.VMEM((part, length), low),
            pltpu.VMEM((heads, length, HEAD), low),
            pltpu.VMEM((heads, length, HEAD), low),
            pltpu.VMEM((part, length), low),
            pltpu.VMEM((masked, rows), wide),
            pltpu.VMEM((part, length), low),
            pltpu.VMEM((3 * part, length), low),
            pltpu.VMEM((part, length), wide),
            pltpu.VMEM((part, length), wide),
            pltpu.VMEM((4, rows, features), low),
            pltpu.VMEM((4, rows, features), low),
            pltpu.VMEM((3 * part, features), wide),
            pltpu.VMEM((part, features), wide),
            pltpu.SemaphoreType.DMA((8,)),
            pltpu.SemaphoreType.DMA((4,)),
            pltpu.SemaphoreType.DMA((4,)),
        ],
        input_output_aliases=aliases,
        compiler_params=pltpu.CompilerParams(vmem_limit_bytes=50 * 2**20),
        cost_estimate=pl.CostEstimate(flops=1, bytes_accessed=1, transcendentals=0),
        name="attention",
    )(*operands)


def split_kernel(offsets, gots, me_ref, col_keep, col_got, row_keep, *refs):
    row_gots, refs = refs[:gots], refs[gots:]
    pieces, col_s, row_s = refs[:4], refs[4], refs[5]
    r = me_ref[3]
    col_rows, n = col_s.shape
    row_rows, features = row_s.shape
    fine, short = col_rows // 16, row_rows // 4
    lo, hi = offsets
    col_s[...] = col_keep[lo : lo + col_rows, :] + col_got[lo : lo + col_rows, :].astype(wide)
    total = row_keep[hi : hi + row_rows, :]
    for got in row_gots:
        total = total + got[hi : hi + row_rows, :].astype(wide)
    row_s[...] = total
    for k, piece in enumerate(pieces):
        cut = r ^ k
        parts = [col_s[pl.ds(pl.multiple_of(b * 4 * fine + cut * fine, 8), fine), :] for b in range(4)]
        piece[0 : 4 * fine, 0:n] = jnp.concatenate(parts).astype(piece.dtype)
        if n < features:
            piece[0 : 4 * fine, n:] = jnp.zeros((4 * fine, features - n), piece.dtype)
        piece[4 * fine :, :] = row_s[pl.ds(pl.multiple_of(cut * short, 8), short), :].astype(piece.dtype)


def split_call(me, col_rows, row_rows, offsets, col_keep, col_got, row_keep, row_gots):
    n, features = col_keep.shape[1], row_keep.shape[1]
    shape = ((col_rows + row_rows) // 4, features)
    return pl.pallas_call(
        partial(split_kernel, offsets, len(row_gots)),
        out_shape=(jax.ShapeDtypeStruct(shape, wide),) + (jax.ShapeDtypeStruct(shape, low),) * 3,
        in_specs=[in_smem] + [in_vmem] * (3 + len(row_gots)),
        out_specs=(in_vmem,) * 4,
        scratch_shapes=[pltpu.VMEM((col_rows, n), wide), pltpu.VMEM((row_rows, features), wide)],
        name="split_gradients",
    )(me, col_keep, col_got, row_keep, *row_gots)


def spread_kernel(me_ref, p0, p1, p2, p3, b0, b1, b2, b3, rows_out, scratch):
    c, r = me_ref[0], me_ref[3]
    owned = b0.shape[0]
    fine, short = owned // 4, rows_out.shape[0] // 4
    for k, p in enumerate((p0, p1, p2, p3)):
        cut = r ^ k
        value = p[...].astype(wide)
        for b in range(4):
            scratch[b, pl.ds(pl.multiple_of(cut * fine, 8), fine), :] = value[b * fine : (b + 1) * fine]
        rows_out[pl.ds(pl.multiple_of(cut * short, 8), short), :] = value[owned:]
    for k, out in enumerate((b0, b1, b2, b3)):
        out[...] = scratch[c ^ k].astype(low)


def spread_call(me, owned, row_rows, pieces):
    features = pieces[0].shape[1]
    return pl.pallas_call(
        spread_kernel,
        out_shape=(jax.ShapeDtypeStruct((owned, features), low),) * 4
        + (jax.ShapeDtypeStruct((row_rows, features), wide),),
        in_specs=[in_smem] + [in_vmem] * 4,
        out_specs=(in_vmem,) * 5,
        scratch_shapes=[pltpu.VMEM((4, owned, features), wide)],
        name="spread_gradients",
    )(me, *pieces)


def join_ff_kernel(me_ref, b0, b1, b2, b3, out):
    c = me_ref[0]
    unit = out.shape[1] // 8
    for k, b in enumerate((b0, b1, b2, b3)):
        for t in range(2):
            lo = pl.multiple_of((4 * t + (c ^ k)) * unit, 128)
            out[:, pl.ds(lo, unit)] = b[:, t * unit : (t + 1) * unit].astype(wide)


def join_ff_call(me, blocks):
    owned, hidden = blocks[0].shape
    return pl.pallas_call(
        join_ff_kernel,
        out_shape=jax.ShapeDtypeStruct((owned, 4 * hidden), wide),
        in_specs=[in_smem] + [in_vmem] * 4,
        out_specs=in_vmem,
        name="join_fc_gradient",
    )(me, *blocks)


def join_att_kernel(me_ref, p0, p1, p2, p3, qkv_out, rows_out, scratch):
    c, r = me_ref[0], me_ref[3]
    owned = qkv_out.shape[0]
    part, fine, short = qkv_out.shape[1] // 12, owned // 4, rows_out.shape[0] // 4
    for k, p in enumerate((p0, p1, p2, p3)):
        cut = r ^ k
        scratch[...] = p[...].astype(wide)
        rows = pl.ds(pl.multiple_of(cut * fine, 8), fine)
        for b in range(4):
            value = scratch[pl.ds(pl.multiple_of((c ^ b) * fine, 8), fine), :]
            for t in range(3):
                lo = (4 * t + head_block(b)) * part
                qkv_out[rows, lo : lo + part] = value[:, t * part : (t + 1) * part]
        rows_out[pl.ds(pl.multiple_of(cut * short, 8), short), :] = scratch[owned:, :]


def join_att_call(me, owned, pieces):
    height, features = pieces[0].shape
    return pl.pallas_call(
        join_att_kernel,
        out_shape=(
            jax.ShapeDtypeStruct((owned, 3 * features), wide),
            jax.ShapeDtypeStruct((4 * (height - owned), features), wide),
        ),
        in_specs=[in_smem] + [in_vmem] * 4,
        out_specs=(in_vmem,) * 2,
        scratch_shapes=[pltpu.VMEM((height, features), wide)],
        name="join_qkv_gradient",
    )(me, *pieces)


def own_vectors_kernel(me_ref, total, *refs):
    outs, row = refs[:7], refs[7]
    c, f = me_ref[0], me_ref[1]
    mine = f * 4 + c

    def choose(values, index):
        value = values[0]
        for k in range(1, len(values)):
            value = jnp.where(index == k, values[k], value)
        return value

    for i in range(5):
        size = outs[i].shape[0]
        outs[i][...] = choose([total[i : i + 1, k * size : (k + 1) * size] for k in range(8)], mine).reshape(size)
    size = outs[5].shape[0]
    part = size * 8 // 12
    for k in range(4):
        for t in range(3):
            lo = (4 * t + head_block(k)) * part
            row[0:1, lo : lo + part] = total[9 + k : 10 + k, t * part : (t + 1) * part]
    outs[5][...] = choose([row[0:1, k * size : (k + 1) * size] for k in range(8)], mine).reshape(size)
    size = outs[6].shape[0]
    pieces = [total[5 + k : 6 + k, t * size : (t + 1) * size] for t in range(2) for k in range(4)]
    outs[6][...] = choose(pieces, mine).reshape(size)


def own_vectors_call(me, total):
    features = total.shape[1]
    sizes = (features // 8,) * 5 + (3 * features // 8, features // 2)
    return pl.pallas_call(
        own_vectors_kernel,
        out_shape=tuple(jax.ShapeDtypeStruct((n,), wide) for n in sizes),
        in_specs=[in_smem, in_vmem],
        out_specs=(in_vmem,) * 7,
        scratch_shapes=[pltpu.VMEM((8, 3 * features), wide)],
        name="own_vectors",
    )(me, total)


def finish_kernel(x_ref, cot_ref, near, over, vecs, *refs):
    out, grad = refs[-2:]
    x = x_ref[0].astype(wide)
    total = near[0].astype(wide) + over[0].astype(wide)
    out[0] = (x + total + vecs[4:5, :]).astype(low)
    e = near[1].astype(wide) + over[1].astype(wide)
    center = x - jnp.mean(x, axis=-1, keepdims=True)
    spread = jnp.mean(center * center, axis=-1, keepdims=True)
    root = lax.rsqrt(spread + epsilon)
    n = center * root
    back = root * (e - jnp.mean(e, axis=-1, keepdims=True) - n * jnp.mean(e * n, axis=-1, keepdims=True))
    grad[0] = (cot_ref[0].astype(wide) + back).astype(low)


def finish_call(s, tokens, cotangent, near, over, vecs, before):
    one = pl.BlockSpec((1, *tokens.shape[1:]), lambda i: (s, 0, 0))
    both = pl.BlockSpec(near.shape, lambda i: (0, 0, 0))
    operands = [tokens, cotangent, near, over, vecs]
    specs = [one, one, both, both, pl.BlockSpec(vecs.shape, lambda i: (0, 0))]
    if before is not None:
        operands += list(before)
        specs += [anywhere, anywhere]
    shape = jax.ShapeDtypeStruct(tokens.shape, low)
    return pl.pallas_call(
        finish_kernel,
        grid=(1,),
        out_shape=(shape, shape),
        in_specs=specs,
        out_specs=(one, one),
        input_output_aliases={} if before is None else {5: 0, 6: 1},
        name="finish_tokens",
    )(*operands)


def shards(
    tokens,
    segment,
    ln1_gain,
    ln1_bias,
    qkv_weight,
    qkv_bias,
    out_weight,
    out_bias,
    ln2_gain,
    ln2_bias,
    fc_weight,
    fc_bias,
    proj_weight,
    proj_bias,
    cotangent,
):
    ctx, fsdp, rep = lax.axis_size("ctx"), lax.axis_size("fsdp"), lax.axis_size("rep")
    c, f, r = lax.axis_index("ctx"), lax.axis_index("fsdp"), lax.axis_index("rep")
    paired = fsdp == 2 and ctx == 4 and rep == 4
    seqs, local_len, features = tokens.shape
    length = local_len * ctx
    owned = qkv_weight.shape[0]
    hidden_own = proj_weight.shape[0]
    hidden_all = fc_weight.shape[1]
    hidden = hidden_all // ctx
    part = features // ctx
    me = f * ctx + c
    core = c & 1

    half = ROT // 2
    inverse = (1.0 / np.float32(10000.0) ** (np.arange(0, ROT, 2, dtype=np.float32) / ROT)).astype(np.float32)
    angles = inverse[:, None] * np.arange(length, dtype=np.float32)[None, :]
    cosine, sine = jnp.asarray(np.cos(angles)), jnp.asarray(np.sin(angles))

    def far_rows(s, *before):
        both = jnp.stack([tokens[s], cotangent[s]])
        return swap(after(both, *before) if before else both, "ctx", 2)

    near = (swap(tokens, "ctx", 1), swap(cotangent, "ctx", 1))

    if paired:
        where = jnp.stack([c, f, core, r]).astype(jnp.int32)
        vectors = (ln1_gain, ln1_bias, ln2_gain, ln2_bias, out_bias, proj_bias, qkv_bias, fc_bias)
        proj_x = swap(proj_weight, "fsdp", 1)
        q0, q1, q2, q3, f0, f1, f2, f3 = pack_call(where, qkv_weight, fc_weight, segment, vectors)
        f_got = [swap(f1, "ctx", 1), swap(f2, "ctx", 2), swap(f3, "ctx", 3)]
        far_send = [jnp.stack([tokens[s], cotangent[s]]) for s in range(seqs)]
        f_got, far_send, proj_x = lax.optimization_barrier((f_got, far_send, proj_x))
        far = [swap(far_send[0], "ctx", 2)]
        f_half = rows_call(where, owned, (f0, *f_got))
        f_other = swap(f_half, "fsdp", 1)
        far[0], f_other = lax.optimization_barrier((far[0], f_other))
        far_core = [swap(far[0], "ctx", 1)]
        vecs, bias, segs = prep_call(where, owned, part, seqs, length, f_half, f_other)
        proj_pair, fc_pair = (proj_weight, proj_x), (f_half, f_other)
    else:
        zero = jnp.zeros_like(c)
        where = jnp.stack([c, zero, zero, zero]).astype(jnp.int32)

        def whole(v, axes=("fsdp", "ctx")):
            return lax.all_gather(v, axes, axis=0, tiled=True)

        far = [far_rows(s) for s in range(seqs)]
        far_core = [swap(v, "ctx", 1) for v in far]
        bias = pick(whole(qkv_bias).reshape(3, ctx, part).transpose(1, 0, 2), c).astype(wide)
        bias = jnp.broadcast_to(bias.reshape(3 * part, 1), (3 * part, 128))
        b_sum = (whole(out_bias).astype(wide) + whole(proj_bias).astype(wide)).reshape(1, features)
        vecs = [whole(v).astype(wide) for v in (ln1_gain, ln1_bias, ln2_gain, ln2_bias)]
        vecs += [b_sum.reshape(features), pick(whole(fc_bias).reshape(ctx, hidden), c).astype(wide)]
        vecs = jnp.concatenate([jnp.stack(vecs), jnp.zeros((2, features), wide)])
        segs = lax.all_gather(segment.astype(low), "ctx", axis=1, tiled=True).astype(wide)
        segs = jnp.concatenate([segs, jnp.zeros((8 - seqs, length), wide)])

        def halves(v):
            return v[: v.shape[0] // 2], v[v.shape[0] // 2 :]

        out_pair = halves(pick(whole(out_weight).reshape(ctx, part, features), c))
        proj_pair = halves(pick(whole(proj_weight).reshape(ctx, hidden, features), c))
        qkv_pair = pick(whole(qkv_weight).reshape(features, 3, ctx, part).transpose(2, 0, 1, 3), c)
        qkv_pair = halves(qkv_pair.reshape(features, 3 * part))
        fc_pair = halves(pick(whole(fc_weight).reshape(features, ctx, hidden).transpose(1, 0, 2), c))

    def run_ff(s, args, acc, part_in, is_last):
        send, keep, *grads = ff_call(s, where, args, *fc_pair, *proj_pair, vecs, acc, part_in, is_last)
        return (send, keep), grads

    def run_att(s, args, weights, acc, part_in, vec=None):
        send, keep, *grads = att_call(
            s, where, args, *weights[0], bias, *weights[1], vecs, segs, cosine, sine, acc, part_in, vec
        )
        return (send, keep), grads

    def near_rows(send, keep):
        both = (keep.astype(wide) + swap(send, "ctx", 1).astype(wide)).astype(low)
        return both[:2], both[2:]

    def finish(s, near_sum, over, before):
        return finish_call(s, tokens, cotangent, near_sum, over, vecs, before)

    def to_rep(pieces):
        return [swap(piece, "rep", k) for k, piece in zip(range(1, rep), pieces)]

    def to_ctx(pieces):
        return [swap(piece, "ctx", k) for k, piece in zip(range(1, ctx), pieces)]

    def add_up(first, others):
        total = first
        for value in others:
            total = total + value.astype(wide)
        return total.astype(low)

    phase = lax.optimization_barrier
    if paired:
        args = (tokens, cotangent, *near, far[0], far_core[0])
        far_send, q1, q2, q3, args = phase((far_send, q1, q2, q3, args))
        far1 = swap(far_send[1], "ctx", 2)
        q_got = [swap(q1, "ctx", 1), swap(q2, "ctx", 2), swap(q3, "ctx", 3)]
        part0, acc = run_ff(0, args, None, None, False)

        part0, acc, far1, q_got = phase((part0, acc, far1, q_got))
        q_half = rows_call(where, owned, (q0, *q_got))
        far1_core = swap(far1, "ctx", 1)
        far1_core, far_send, q_half, acc = phase((far1_core, far_send, q_half, acc))
        far2 = swap(far_send[2], "ctx", 2)
        q_other = swap(q_half, "fsdp", 1)
        out_x = swap(out_weight, "fsdp", 1)
        part1, acc = run_ff(1, (tokens, cotangent, *near, far1, far1_core), acc, None, False)

        part1, acc, far2, q_other, out_x = phase((part1, acc, far2, q_other, out_x))
        far2_core = swap(far2, "ctx", 1)
        out_keep = jnp.where(core == f, out_weight, out_x)
        out_got = swap(jnp.where(core == f, out_x, out_weight), "ctx", 1)
        att_weights = ((q_half, q_other), (out_keep, out_got))
        part2, ff_last = run_ff(2, (tokens, cotangent, *near, far2, far2_core), acc, None, True)

        part0, ff_last, att_weights = phase((part0, ff_last, att_weights))
        ff_got = swap(ff_last[1], "fsdp", 1)
        args = (tokens, cotangent, *near, far[0], far_core[0])
        part0, att_acc = run_att(0, args, att_weights, None, part0)

        part0, att_acc, ff_got = phase((part0, att_acc, ff_got))
        half_rows = features // fsdp
        ff_pieces = split_call(
            where, half_rows, hidden_own, (0, half_rows), ff_last[0], ff_got, ff_last[0], [ff_got]
        )
        near0, away = near_rows(*part0)
        ff_pieces, near0, away, part1, att_acc = phase((ff_pieces, near0, away, part1, att_acc))
        ff_got = to_rep(ff_pieces[1:])
        over0 = swap(away, "ctx", 2)
        args = (tokens, cotangent, *near, far1, far1_core)
        part1, att_acc = run_att(1, args, att_weights, att_acc, part1)

        part1, att_acc, ff_got, over0 = phase((part1, att_acc, ff_got, over0))
        ff_total = add_up(ff_pieces[0], ff_got)
        near1, away = near_rows(*part1)
        ff_total, near1, away, part2, att_acc = phase((ff_total, near1, away, part2, att_acc))
        ff_got = to_rep([ff_total] * (rep - 1))
        over1 = swap(away, "ctx", 2)
        args = (tokens, cotangent, *near, far2, far2_core)
        part2, att_last = run_att(2, args, att_weights, att_acc, part2, ff_last[2])

        part2, att_last, ff_got, over1 = phase((part2, att_last, ff_got, over1))
        got = swap(att_last[1], "fsdp", 1)
        pairs = [(k, i, 1 - k, i) if (i & 1) != k else (k, i, k, i ^ 1) for k in range(fsdp) for i in range(ctx)]
        near_got = lax.ppermute(att_last[3], ("fsdp", "ctx"), [(a * ctx + b, d * ctx + e) for a, b, d, e in pairs])
        pairs = [(k * ctx + i, (1 - k) * ctx + (i ^ 1)) for k in range(fsdp) for i in range(ctx) if (i & 1) != k]
        far_got = lax.ppermute(att_last[4], ("fsdp", "ctx"), pairs)
        total_vec = att_last[5]
        total_vec = total_vec + swap(total_vec, "ctx", 1)
        total_vec = total_vec + swap(total_vec, "ctx", 2)
        near2, away = near_rows(*part2)
        *ff_blocks, g_proj = spread_call(where, owned, hidden_own, (ff_total, *ff_got))
        got, near_got, far_got, near2, away, ff_blocks, total_vec = phase(
            (got, near_got, far_got, near2, away, ff_blocks, total_vec)
        )

        att_pieces = split_call(where, half_rows, owned, (0, 0), att_last[0], got, att_last[2], [near_got, far_got])
        att_got = to_rep(att_pieces[1:])
        over2 = swap(away, "ctx", 2)
        ff_blocks_got = to_ctx(ff_blocks[1:])
        total_vec = total_vec + swap(total_vec, "fsdp", 1)
        done = finish(0, near0, over0, None)
        done = finish(1, near1, over1, done)
        att_pieces, att_got, over2, ff_blocks_got, total_vec, done = phase(
            (att_pieces, att_got, over2, ff_blocks_got, total_vec, done)
        )

        total = add_up(att_pieces[0], att_got)
        blocks = total[:owned].reshape(ctx, owned // rep, features)
        blocks = [pick(blocks, c ^ k) for k in range(ctx)]
        piece = jnp.concatenate([blocks[0], *to_ctx(blocks[1:]), total[owned:]])
        total_vec = total_vec + swap(total_vec, "rep", 1)
        piece, total_vec, done, over2, ff_blocks_got = phase((piece, total_vec, done, over2, ff_blocks_got))
        others = to_rep([piece] * (rep - 1))
        total_vec = total_vec + swap(total_vec, "rep", 2)
        output, grad_tokens = finish(2, near2, over2, done)
        g_fc = join_ff_call(where, (ff_blocks[0], *ff_blocks_got))
        g_gain_one, g_shift_one, g_gain_two, g_shift_two, g_bias, g_b_qkv, g_b_fc = own_vectors_call(
            where, total_vec
        )
        g_qkv, g_out = join_att_call(where, owned, (piece, *others))
    else:
        att_acc = ff_acc = done = None
        for s in range(seqs):
            args = (tokens, cotangent, *near, far[s], far_core[s])
            parts, ff_acc = run_ff(s, args, ff_acc, None, s == seqs - 1)
            vec = ff_acc[2] if s == seqs - 1 else None
            parts, att_acc = run_att(s, args, (qkv_pair, out_pair), att_acc, parts, vec)
            near_sum, away = near_rows(*parts)
            done = finish(s, near_sum, swap(away, "ctx", 2), done)
        output, grad_tokens = done

        def any_columns(kept, sent):
            grad = jnp.concatenate([kept.astype(low), sent])
            grad = lax.psum_scatter(grad, "fsdp", scatter_dimension=0, tiled=True)
            grad = lax.psum(grad, "rep").reshape(ctx, owned, -1)
            return lax.all_to_all(grad, "ctx", split_axis=0, concat_axis=0)

        def any_rows(kept, sent):
            grad = jnp.concatenate([kept.astype(low), sent])
            grad = jnp.where(jnp.arange(ctx)[:, None, None] == c, grad[None], 0).reshape(-1, features)
            return lax.psum(
                lax.psum_scatter(grad, ("fsdp", "ctx"), scatter_dimension=0, tiled=True), "rep"
            )

        cut = features // 2
        g_fc = any_columns(ff_acc[0][:cut], ff_acc[1][:cut])
        g_fc = g_fc.transpose(1, 0, 2).reshape(owned, hidden_all)
        g_proj = any_rows(ff_acc[0][cut:], ff_acc[1][cut:])
        g_qkv = any_columns(*att_acc[:2]).reshape(ctx, owned, 3, part)
        g_qkv = g_qkv.transpose(1, 2, 0, 3).reshape(owned, 3 * features)
        g_out = any_rows(*att_acc[2:4])
        total_vec = lax.psum(att_acc[5], ("ctx", "fsdp", "rep"))
        grads = [total_vec[k] for k in range(5)]
        grads.append(total_vec[9 : 9 + ctx, : 3 * part].reshape(ctx, 3, part).transpose(1, 0, 2).reshape(-1))
        grads.append(total_vec[5 : 5 + ctx, :hidden].reshape(-1))
        own = []
        for v in grads:
            size = v.shape[0] // (fsdp * ctx)
            own.append(lax.dynamic_slice(v, (me * size,), (size,)))
        g_gain_one, g_shift_one, g_gain_two, g_shift_two, g_bias, g_b_qkv, g_b_fc = own
    return (
        output,
        grad_tokens,
        g_gain_one,
        g_shift_one,
        g_qkv.astype(wide),
        g_b_qkv,
        g_out.astype(wide),
        g_bias,
        g_gain_two,
        g_shift_two,
        g_fc.astype(wide),
        g_b_fc,
        g_proj.astype(wide),
        g_bias,
    )


def solution(mesh):
    rows, row = P(("rep", "fsdp"), "ctx", None), P(("rep", "fsdp"), "ctx")
    vector, matrix = P(("fsdp", "ctx")), P(("fsdp", "ctx"), None)
    params = (
        vector, vector, matrix, vector, matrix, vector,
        vector, vector, matrix, vector, matrix, vector,
    )
    return jax.shard_map(
        shards,
        mesh=mesh,
        in_specs=(rows, row, *params, rows),
        out_specs=(rows, rows, *params),
        check_vma=False,
    )
```

```python
from functools import partial
import math

import jax
import jax.numpy as jnp
import numpy as np
from jax import lax
from jax.experimental import pallas as pl
from jax.experimental.pallas import tpu as pltpu
from jax.sharding import PartitionSpec as P

HEADS = 12
HEAD = 64
ROT = 16

epsilon = 1e-05
far_below = -1e30
low = jnp.bfloat16
wide = jnp.float32
log2e = math.log2(math.e)


def nn(a, b):
    return lax.dot_general(a, b, (((1,), (0,)), ((), ())), preferred_element_type=wide)


def nt(a, b):
    return lax.dot_general(a, b, (((1,), (1,)), ((), ())), preferred_element_type=wide)


def swap(value, axis, bits):
    size = lax.axis_size(axis)
    return lax.ppermute(value, axis, [(i, i ^ bits) for i in range(size)])


def in_order(rel, me):
    out = []
    for k in range(len(rel)):
        value = rel[k]
        for m in range(1, len(rel)):
            value = jnp.where(me == m, rel[k ^ m], value)
        out.append(value)
    return out


def pick(stacked, index):
    return lax.dynamic_index_in_dim(stacked, index, 0, keepdims=False)


def after(value, *before):
    return lax.optimization_barrier((value, before))[0]


anywhere = pl.BlockSpec(memory_space=pltpu.HBM)
in_vmem = pl.BlockSpec(memory_space=pltpu.VMEM)
in_smem = pl.BlockSpec(memory_space=pltpu.SMEM)
extra_rows = 16


def head_block(index):
    return ((index & 1) << 1) | (index >> 1)


def pack_kernel(vectors, me_ref, qkv, fc, segment, *refs):
    vector_refs, refs = refs[:vectors], refs[vectors:]
    q0, q1, q2, q3, f0, f1, f2, f3, scratch, extra = refs
    c = me_ref[0]
    owned, part, unit = qkv.shape[0], qkv.shape[1] // 12, fc.shape[1] // 8
    extra[...] = jnp.zeros_like(extra)
    for row, ref in enumerate(vector_refs):
        extra[row : row + 1, 0 : ref.shape[0]] = ref[...].astype(wide).reshape(1, -1)
    extra[8 : 8 + segment.shape[0], 0 : segment.shape[1]] = segment[...].astype(wide)
    for k in range(4):
        block = head_block(k)
        for t in range(3):
            lo = (4 * t + block) * part
            scratch[k ^ c, :, t * part : (t + 1) * part] = qkv[:, lo : lo + part]
    for k, (q, g) in enumerate(((q0, f0), (q1, f1), (q2, f2), (q3, f3))):
        q[...] = scratch[k]
        for t in range(2):
            lo = pl.multiple_of((4 * t + (c ^ k)) * unit, 128)
            g[0:owned, t * unit : (t + 1) * unit] = fc[:, pl.ds(lo, unit)]
        g[owned:, :] = extra[...].astype(low)


def pack_call(me, qkv, fc, segment, vectors):
    owned = qkv.shape[0]
    narrow, broad = (owned, qkv.shape[1] // 4), (owned + extra_rows, fc.shape[1] // 4)
    shapes = (narrow,) * 4 + (broad,) * 4
    return pl.pallas_call(
        partial(pack_kernel, len(vectors)),
        out_shape=tuple(jax.ShapeDtypeStruct(s, low) for s in shapes),
        in_specs=[in_smem] + [in_vmem] * (3 + len(vectors)),
        out_specs=(in_vmem,) * 8,
        scratch_shapes=[
            pltpu.VMEM((4, owned, narrow[1]), low),
            pltpu.VMEM((extra_rows, broad[1]), wide),
        ],
        name="pack_columns",
    )(me, qkv, fc, segment, *vectors)


def rows_kernel(owned, me_ref, p0, p1, p2, p3, half):
    c = me_ref[0]
    tail = p0.shape[0] - owned
    for k, p in enumerate((p0, p1, p2, p3)):
        half[pl.ds(pl.multiple_of((c ^ k) * owned, 16), owned), :] = p[0:owned, :]
        if tail:
            half[pl.ds(pl.multiple_of(4 * owned + (c ^ k) * tail, 16), tail), :] = p[owned:, :]


def rows_call(me, owned, pieces):
    rows, cols = pieces[0].shape
    return pl.pallas_call(
        partial(rows_kernel, owned),
        out_shape=jax.ShapeDtypeStruct((4 * rows, cols), low),
        in_specs=[in_smem] + [in_vmem] * 4,
        out_specs=in_vmem,
        name="rows_by_ctx",
    )(me, *pieces)


def prep_kernel(owned, part, seqs, me_ref, mine, other, vecs, bias, seg):
    c, f = me_ref[0], me_ref[1]
    extra_mine, extra_other = mine[...].astype(wide), other[...].astype(wide)
    first = jnp.where(f == 0, extra_mine, extra_other)
    last = jnp.where(f == 0, extra_other, extra_mine)

    def vector(row, size):
        pieces = [
            e[k * extra_rows + row : k * extra_rows + row + 1, 0:size]
            for e in (first, last)
            for k in range(4)
        ]
        return jnp.concatenate(pieces, axis=1)

    block = head_block(c)
    vecs[...] = jnp.zeros_like(vecs)
    for row in range(4):
        vecs[row : row + 1, :] = vector(row, owned)
    vecs[4:5, :] = vector(4, owned) + vector(5, owned)
    unit = mine.shape[1] // 2
    for t, e in enumerate((first, last)):
        chosen = e[7:8, 0:unit]
        for k in range(1, 4):
            chosen = jnp.where(c == k, e[k * extra_rows + 7 : k * extra_rows + 8, 0:unit], chosen)
        vecs[5:6, t * unit : (t + 1) * unit] = chosen
    all_qkv = vector(6, 3 * owned)
    picked = []
    for t in range(3):
        chosen = all_qkv[:, 4 * t * part : (4 * t + 1) * part]
        for k in range(1, 4):
            chosen = jnp.where(block == k, all_qkv[:, (4 * t + k) * part : (4 * t + k + 1) * part], chosen)
        picked.append(chosen)
    row_bias = jnp.concatenate(picked, axis=1)
    bias[...] = jnp.transpose(jnp.broadcast_to(row_bias, (128, 3 * part)))
    seg[...] = jnp.zeros_like(seg)
    width = seg.shape[1] // 4
    for s in range(seqs):
        for k in range(4):
            row = k * extra_rows + 8 + s
            seg[s : s + 1, k * width : (k + 1) * width] = extra_mine[row : row + 1, 0:width]


def prep_call(me, owned, part, seqs, length, mine, other):
    tail = pl.BlockSpec((4 * extra_rows, mine.shape[1]), lambda i: (4 * owned // (4 * extra_rows), 0))
    assert 4 * owned % (4 * extra_rows) == 0
    shapes = ((8, 8 * owned), (3 * part, 128), (8, length))
    return pl.pallas_call(
        partial(prep_kernel, owned, part, seqs),
        grid=(1,),
        out_shape=tuple(jax.ShapeDtypeStruct(s, wide) for s in shapes),
        in_specs=[in_smem, tail, tail],
        out_specs=tuple(pl.BlockSpec(s, lambda i: (0, 0)) for s in shapes),
        name="prepare_vectors",
    )(me, mine, other)


def row_norm(block):
    values = block.astype(wide)
    center = values - jnp.mean(values, axis=-1, keepdims=True)
    spread = jnp.mean(center * center, axis=-1, keepdims=True)
    return center * lax.rsqrt(spread + epsilon)


def gelu_parts(v):
    bell = jnp.exp2(v * v * (-0.5 * log2e))
    base = 1.0 + (0.3275911 / math.sqrt(2.0)) * jnp.abs(v)
    t = pl.reciprocal(base, approx=True)
    t = t * (2.0 - base * t)
    poly = 0.5 * 1.061405429
    for coef in (-1.453152027, 1.421413741, -0.284496736, 0.254829592):
        poly = poly * t + 0.5 * coef
    tail = poly * t * bell
    phi = jnp.where(v >= 0, 1.0 - tail, tail)
    return phi, phi + v * bell * (1.0 / math.sqrt(2.0 * math.pi))


def bring(pairs, sem):
    copies = [pltpu.make_async_copy(a, b, sem.at[k]) for k, (a, b) in enumerate(pairs)]
    for copy in copies:
        copy.start()
    return copies


def token_pairs(s, refs, xs, cs):
    tok, cot, tok1, cot1, far, far1 = refs
    pairs = []
    for j, (t, c) in enumerate(
        ((tok.at[s], cot.at[s]), (tok1.at[s], cot1.at[s]), (far.at[0], far.at[1]), (far1.at[0], far1.at[1]))
    ):
        pairs += [(t, xs.at[j]), (c, cs.at[j])]
    return pairs


def ff_kernel(s, with_acc, with_part, is_last, *refs):
    me_ref, refs = refs[0], refs[1:]
    token_refs, refs = refs[:6], refs[6:]
    fc_a, fc_b, proj_a, proj_b, vecs = refs[:5]
    refs = refs[5:]
    if with_acc:
        acc_fc_in, acc_proj_in, acc_vec_in = refs[:3]
        refs = refs[3:]
    if with_part:
        part_send, part_keep = refs[:2]
        refs = refs[2:]
    send, keep = refs[:2]
    refs = refs[2:]
    if is_last:
        grad_keep, grad_send, vec = refs[:3]
        refs = refs[3:]
    else:
        fc_out, proj_out, vec = refs[:3]
        refs = refs[3:]
    xs, cs, fc, proj, sec_s, hid_s, gp_s, send_s, keep_s, acc_fc, acc_proj, sem, sem_w, sem_p, sem_o = refs
    f = me_ref[1]
    blocks, rows, features = xs.shape
    hidden = fc.shape[1]
    third, half = features // 2, proj_a.shape[0]
    tokens_in = bring(token_pairs(s, token_refs, xs, cs), sem)
    weights_in = bring(
        [
            (fc_a.at[0:third], fc.at[pl.ds(pl.multiple_of(f * third, 16), third), :]),
            (fc_b.at[0:third], fc.at[pl.ds(pl.multiple_of((1 - f) * third, 16), third), :]),
            (proj_a, proj.at[pl.ds(pl.multiple_of(f * half, 16), half), :]),
            (proj_b, proj.at[pl.ds(pl.multiple_of((1 - f) * half, 16), half), :]),
        ],
        sem_w,
    )
    later = []
    if with_part:
        later += [(part_send, send_s), (part_keep, keep_s)]
    if with_acc:
        later += [(acc_fc_in, acc_fc), (acc_proj_in, acc_proj)]
    later = bring(later, sem_p)
    for copy in weights_in + tokens_in:
        copy.wait()
    gain, shift, bias = vecs[2:3, :], vecs[3:4, :], vecs[5:6, 0:hidden]
    dgain = jnp.zeros((1, features), wide)
    dshift = jnp.zeros((1, features), wide)
    dbias = jnp.zeros((1, hidden), wide)
    if with_part:
        later[0].wait()
        later[1].wait()
    for j in range(blocks):
        here = pl.ds(j * rows, rows)
        n = row_norm(xs[j])
        second = (n * gain + shift).astype(low)
        sec_s[here, :] = second
        cot = cs[j]
        pre = nn(second, fc[...]) + bias
        phi, slope = gelu_parts(pre)
        hid = (pre * phi).astype(low)
        gp = nt(cot, proj[...]) * slope
        dbias = dbias + jnp.sum(gp, axis=0, keepdims=True)
        gp = gp.astype(low)
        hid_s[here, :] = hid
        gp_s[here, :] = gp
        out = nn(hid, proj[...])
        dsec = nt(gp, fc[...])
        dgain = dgain + jnp.sum(dsec * n, axis=0, keepdims=True)
        dshift = dshift + jnp.sum(dsec, axis=0, keepdims=True)
        e = dsec * gain
        to = send_s if j % 2 else keep_s
        if with_part:
            out = out + to[j // 2 * 2].astype(wide)
            e = e + to[j // 2 * 2 + 1].astype(wide)
        to[j // 2 * 2] = out.astype(low)
        to[j // 2 * 2 + 1] = e.astype(low)
    results = bring([(send_s, send), (keep_s, keep)], sem_o)
    dcot = jnp.sum(cs[0].astype(wide), axis=0, keepdims=True)
    w_fc = nn(jnp.transpose(sec_s[...]), gp_s[...])
    w_proj = nn(jnp.transpose(hid_s[...]), cs[...].reshape(blocks * rows, features))
    if with_acc:
        later[-2].wait()
        later[-1].wait()
        w_fc = w_fc + acc_fc[...]
        w_proj = w_proj + acc_proj[...]
        dgain = dgain + acc_vec_in[0:1, :]
        dshift = dshift + acc_vec_in[1:2, :]
        dbias = dbias + acc_vec_in[2:3, 0:hidden]
        dcot = dcot + acc_vec_in[3:4, :]
    acc_fc[...] = w_fc
    if is_last:
        acc_proj[...] = w_proj
        mine, away = pl.ds(pl.multiple_of(f * third, 16), third), pl.ds(pl.multiple_of((1 - f) * third, 16), third)
        grad_keep[0:third, :] = acc_fc[mine, :].astype(low)
        grad_send[0:third, :] = acc_fc[away, :].astype(low)
        mine, away = pl.ds(pl.multiple_of(f * half, 16), half), pl.ds(pl.multiple_of((1 - f) * half, 16), half)
        grad_keep[third:, :] = acc_proj[mine, :].astype(low)
        grad_send[third:, :] = acc_proj[away, :].astype(low)
    else:
        acc_proj[...] = w_proj
        more = [
            pltpu.make_async_copy(acc_fc, fc_out, sem_o.at[2]),
            pltpu.make_async_copy(acc_proj, proj_out, sem_o.at[3]),
        ]
        for copy in more:
            copy.start()
        results += more
    vec[0:1, :] = dgain
    vec[1:2, :] = dshift
    vec[2:3, 0:hidden] = dbias
    vec[3:4, :] = dcot
    for copy in results:
        copy.wait()


def ff_call(s, me, token_args, fc_a, fc_b, proj_a, proj_b, vecs, acc, part, is_last):
    rows, features = token_args[0].shape[1:]
    hidden, blocks = fc_a.shape[1], 4
    total = blocks * rows
    third = features // 2
    operands = [me, *token_args, fc_a, fc_b, proj_a, proj_b, vecs]
    specs = [in_smem] + [anywhere] * 10 + [in_vmem]
    aliases = {}
    if acc is not None:
        if not is_last:
            aliases = {len(operands): 2, len(operands) + 1: 3}
        operands += list(acc)
        specs += [anywhere, anywhere, in_vmem]
    if part is not None:
        aliases[len(operands)] = 0
        aliases[len(operands) + 1] = 1
        operands += list(part)
        specs += [anywhere, anywhere]
    shared = jax.ShapeDtypeStruct((4, rows, features), low)
    vec = jax.ShapeDtypeStruct((8, features), wide)
    if is_last:
        rows_out = third + proj_a.shape[0]
        grads = (
            jax.ShapeDtypeStruct((rows_out, features), low),
            jax.ShapeDtypeStruct((rows_out, features), low),
        )
        grad_specs = (in_vmem,) * 2
    else:
        grads = (
            jax.ShapeDtypeStruct((features, hidden), wide),
            jax.ShapeDtypeStruct((hidden, features), wide),
        )
        grad_specs = (anywhere,) * 2
    return pl.pallas_call(
        partial(ff_kernel, s, acc is not None, part is not None, is_last),
        out_shape=(shared, shared, *grads, vec),
        in_specs=specs,
        out_specs=(anywhere, anywhere, *grad_specs, in_vmem),
        scratch_shapes=[
            pltpu.VMEM((blocks, rows, features), low),
            pltpu.VMEM((blocks, rows, features), low),
            pltpu.VMEM((features, hidden), low),
            pltpu.VMEM((hidden, features), low),
            pltpu.VMEM((total, features), low),
            pltpu.VMEM((total, hidden), low),
            pltpu.VMEM((total, hidden), low),
            pltpu.VMEM((4, rows, features), low),
            pltpu.VMEM((4, rows, features), low),
            pltpu.VMEM((features, hidden), wide),
            pltpu.VMEM((hidden, features), wide),
            pltpu.SemaphoreType.DMA((8,)),
            pltpu.SemaphoreType.DMA((4,)),
            pltpu.SemaphoreType.DMA((4,)),
            pltpu.SemaphoreType.DMA((8,)),
        ],
        input_output_aliases=aliases,
        compiler_params=pltpu.CompilerParams(vmem_limit_bytes=50 * 2**20),
        cost_estimate=pl.CostEstimate(flops=1, bytes_accessed=1, transcendentals=0),
        name="feed_forward",
    )(*operands)


def turn(block, cosine, sine):
    half = ROT // 2
    a, b = block[0:half], block[half:ROT]
    return jnp.concatenate([a * cosine - b * sine, b * cosine + a * sine, block[ROT:]], axis=0)


def att_kernel(s, heads, with_acc, with_part, is_last, *refs):
    me_ref, refs = refs[0], refs[1:]
    token_refs, refs = refs[:6], refs[6:]
    w_a, w_b, bias, wout_a, wout_b, vecs, segs, cosine, sine = refs[:9]
    refs = refs[9:]
    if is_last:
        ff_vec, refs = refs[0], refs[1:]
    if with_acc:
        acc_w_in, acc_o_in, acc_vec_in = refs[:3]
        refs = refs[3:]
    if with_part:
        part_send, part_keep = refs[:2]
        refs = refs[2:]
    send, keep = refs[:2]
    refs = refs[2:]
    if is_last:
        messages, (o_keep, o_send, o_send_far) = refs[:8], refs[8:11]
        refs = refs[11:]
    else:
        w_out, o_out, vec = refs[:3]
        refs = refs[3:]
    xs, cs, wt_s, wout, first_s, n_s, cot_s, qt_s, kt_s, vt_s, k_s, v_s, dot_s, mask_s, att_s, d_s, dk_s, dv_s = refs[:18]
    send_s, keep_s, acc_w, acc_o, sem, sem_p, sem_o = refs[18:25]
    if is_last:
        by_rows = refs[25]
    me, f, core = me_ref[0], me_ref[1], me_ref[2]
    blocks, rows, features = xs.shape
    part = heads * HEAD
    length = blocks * rows
    reach = length // 2
    scale = 1.0 / math.sqrt(HEAD)
    tokens_in = bring(token_pairs(s, token_refs, xs, cs), sem)
    gain, shift = vecs[0:1, :], vecs[1:2, :]
    share = w_a.shape[0]
    wt_s[:, pl.ds(pl.multiple_of(f * share, 128), share)] = jnp.transpose(w_a[...])
    wt_s[:, pl.ds(pl.multiple_of((1 - f) * share, 128), share)] = jnp.transpose(w_b[...])
    owned = wout_a.shape[0]
    wout[pl.ds(pl.multiple_of(core * owned, 16), owned), :] = wout_a[...]
    wout[pl.ds(pl.multiple_of((1 - core) * owned, 16), owned), :] = wout_b[...]

    seg_row = segs[s : s + 1, :]
    seg_col = jnp.transpose(jnp.broadcast_to(seg_row, (128, length)))
    spans, place = [], 0
    for i in range(blocks):
        start = max(0, i * rows - reach)
        count = (i + 1) * rows - start
        spans.append((start, count, place))
        ours = seg_row[:, i * rows : (i + 1) * rows]
        theirs = seg_col[start : start + count]
        theirs = jnp.concatenate([theirs] * (rows // 128), axis=1)
        key = start + lax.broadcasted_iota(jnp.int32, (count, rows), 0)
        query = i * rows + lax.broadcasted_iota(jnp.int32, (count, rows), 1)
        allowed = (theirs == ours) & (key <= query)
        mask_s[place : place + count, :] = jnp.where(allowed, 0.0, far_below)
        place += count

    for copy in tokens_in:
        copy.wait()
    wide_bias = jnp.concatenate([bias[...]] * (rows // 128), axis=1)
    for j in range(blocks):
        off = pl.multiple_of((me ^ j) * rows, rows)
        n = row_norm(xs[j])
        n_s[pl.ds(off, rows), :] = n.astype(low)
        first = (n * gain + shift).astype(low)
        first_s[pl.ds(off, rows), :] = first
        cot = cs[j]
        cot_s[pl.ds(off, rows), :] = cot
        cos_b, sin_b = cosine[:, pl.ds(off, rows)], sine[:, pl.ds(off, rows)]
        made = nt(wt_s[...], first) + wide_bias
        for h in range(heads):
            lo, hi = h * HEAD, (h + 1) * HEAD
            query = turn(made[lo:hi], cos_b, sin_b).astype(low)
            qt_s[lo:hi, pl.ds(off, rows)] = (query.astype(wide) * scale).astype(low)
            key = turn(made[part + lo : part + hi], cos_b, sin_b).astype(low)
            kt_s[lo:hi, pl.ds(off, rows)] = key
            value = made[2 * part + lo : 2 * part + hi].astype(low)
            vt_s[lo:hi, pl.ds(off, rows)] = value
            k_s[h, pl.ds(off, rows), :] = jnp.transpose(key)
            v_s[h, pl.ds(off, rows), :] = jnp.transpose(value)
        dot_s[:, pl.ds(off, rows)] = nt(wout[...], cot).astype(low)

    later = []
    if with_part:
        later += [(part_send, send_s), (part_keep, keep_s)]
    if with_acc:
        later += [(acc_w_in, acc_w), (acc_o_in, acc_o)]
    later = bring(later, sem_p)
    dk_s[...] = jnp.zeros_like(dk_s)
    dv_s[...] = jnp.zeros_like(dv_s)

    def one_head(h, carry):
        base = pl.multiple_of(h * HEAD, HEAD)
        mine = pl.ds(base, HEAD)
        for i in range(blocks):
            start, count, place = spans[i]
            here, there = slice(i * rows, (i + 1) * rows), slice(start, start + count)
            query, grad = qt_s[mine, here], dot_s[mine, here]
            score = nn(k_s[h, there, :], query) + mask_s[place : place + count, :]
            top = jnp.max(score, axis=0, keepdims=True)
            lifted = jnp.exp2((score - top) * log2e)
            total = jnp.sum(lifted, axis=0, keepdims=True)
            prob = lifted * (1.0 / total)
            prob_low = prob.astype(low)
            att_s[mine, here] = nn(vt_s[mine, there], prob_low).astype(low)
            dprob = nn(v_s[h, there, :], grad)
            inner = jnp.sum(prob * dprob, axis=0, keepdims=True)
            dscore = (prob * (dprob - inner)).astype(low)
            dv_s[mine, there] += nt(grad, prob_low)
            dk_s[mine, there] += nt(query, dscore)
            dq = nn(kt_s[mine, there], dscore) * scale
            cos_b, sin_b = cosine[:, here], sine[:, here]
            d_s[mine, here] = turn(dq, cos_b, -sin_b).astype(low)
        return carry

    lax.fori_loop(0, heads, one_head, 0)
    for h in range(heads):
        lo, hi = h * HEAD, (h + 1) * HEAD
        d_s[part + lo : part + hi, :] = turn(dk_s[lo:hi, :], cosine[...], -sine[...]).astype(low)
    d_s[2 * part : 3 * part, :] = dv_s[...].astype(low)

    g_w = nn(d_s[...], first_s[...])
    g_o = nn(att_s[...], cot_s[...])
    if with_part:
        later[0].wait()
        later[1].wait()
    if with_acc:
        later[-2].wait()
        later[-1].wait()
        g_w = g_w + acc_w[...]
        g_o = g_o + acc_o[...]
    acc_w[...] = g_w
    results = []
    if is_last:
        by_rows[...] = jnp.transpose(acc_w[...])
        for k, message in enumerate(messages):
            shard = (f ^ (k // 4)) * 4 + (me ^ (k % 4))
            block = by_rows[pl.ds(pl.multiple_of(shard * owned, 8), owned), :]
            message[0:owned, :] = block.astype(message.dtype)
        acc_o[...] = g_o
        mine = acc_o[pl.ds(pl.multiple_of(f * owned, 16), owned), :]
        o_keep[...] = jnp.where(f == core, mine, 0.0)
        o_send[...] = acc_o[pl.ds(pl.multiple_of((1 - f) * owned, 16), owned), :].astype(low)
        o_send_far[...] = mine.astype(low)
    else:
        acc_o[...] = g_o
        results = [
            pltpu.make_async_copy(acc_w, w_out, sem_o.at[2]),
            pltpu.make_async_copy(acc_o, o_out, sem_o.at[3]),
        ]
        for copy in results:
            copy.start()
    dgain = jnp.zeros((1, features), wide)
    dshift = jnp.zeros((1, features), wide)
    dbias = jnp.zeros((8, 3 * part), wide)
    for j in range(blocks):
        off = pl.multiple_of((me ^ j) * rows, rows)
        att = jnp.transpose(att_s[:, pl.ds(off, rows)])
        out = nn(att, wout[...])
        dqkv = jnp.transpose(d_s[:, pl.ds(off, rows)])
        dbias = dbias + nn(jnp.ones((8, rows), low), dqkv)
        dfirst = nn(dqkv, wt_s[...])
        n = n_s[pl.ds(off, rows), :].astype(wide)
        dgain = dgain + jnp.sum(dfirst * n, axis=0, keepdims=True)
        dshift = dshift + jnp.sum(dfirst, axis=0, keepdims=True)
        e = dfirst * gain
        to, first = send_s if j % 2 else keep_s, j // 2 * 2
        if with_part:
            out = out + to[first].astype(wide)
            e = e + to[first + 1].astype(wide)
        to[first] = out.astype(low)
        to[first + 1] = e.astype(low)
    results += bring([(send_s, send), (keep_s, keep)], sem_o)
    dbias = dbias[0:1]
    if with_acc:
        dgain = dgain + acc_vec_in[0:1, :]
        dshift = dshift + acc_vec_in[1:2, :]
        dbias = dbias + acc_vec_in[2:3, 0 : 3 * part]
    if is_last:
        cols = 3 * part
        rest = jnp.zeros((1, features - cols), wide)
        vec = jnp.concatenate(
            [dgain, dshift, ff_vec[0:2, :], ff_vec[3:4, :], ff_vec[2:3, :], jnp.concatenate([dbias, rest], axis=1)]
            + [jnp.zeros((1, features), wide)]
        )
        for message in messages:
            message[owned : owned + 8, :] = vec[:, 0:cols].astype(message.dtype)
            message[owned + 8 : owned + 16, 0 : features - cols] = vec[:, cols:].astype(message.dtype)
            message[owned + 8 : owned + 16, features - cols :] = jnp.zeros((8, 2 * cols - features), message.dtype)
    else:
        vec[0:1, :] = dgain
        vec[1:2, :] = dshift
        vec[2:3, 0 : 3 * part] = dbias
    for copy in results:
        copy.wait()


def att_call(s, me, token_args, w_a, w_b, bias, wout_a, wout_b, vecs, segs, cosine, sine, acc, part_in, ff_vec):
    rows, features = token_args[0].shape[1:]
    part, blocks = w_a.shape[1] // 3, 4
    heads = part // HEAD
    length = blocks * rows
    is_last = ff_vec is not None
    operands = [me, *token_args, w_a, w_b, bias, wout_a, wout_b, vecs, segs, cosine, sine]
    operands += [ff_vec] if is_last else []
    specs = [in_smem] + [anywhere] * 6 + [in_vmem] * (len(operands) - 7)
    aliases = {}
    if acc is not None:
        if not is_last:
            aliases = {len(operands): 2, len(operands) + 1: 3}
        operands += list(acc)
        specs += [anywhere, anywhere, in_vmem]
    if part_in is not None:
        aliases[len(operands)] = 0
        aliases[len(operands) + 1] = 1
        operands += list(part_in)
        specs += [anywhere, anywhere]
    shared = jax.ShapeDtypeStruct((4, rows, features), low)
    if is_last:
        message = (part // 2 + 16, 3 * part)
        grads = (jax.ShapeDtypeStruct(message, wide),) + (jax.ShapeDtypeStruct(message, low),) * 7
        grads += (
            jax.ShapeDtypeStruct((part // 2, features), wide),
            jax.ShapeDtypeStruct((part // 2, features), low),
            jax.ShapeDtypeStruct((part // 2, features), low),
        )
        grad_specs = (in_vmem,) * 11
        last_vec, vec_specs = (), ()
        more = [pltpu.VMEM((features, 3 * part), wide)]
    else:
        grads = (
            jax.ShapeDtypeStruct((3 * part, features), wide),
            jax.ShapeDtypeStruct((part, features), wide),
        )
        grad_specs = (anywhere,) * 2
        last_vec, vec_specs, more = (jax.ShapeDtypeStruct((8, features), wide),), (in_vmem,), []
    reach = length // 2
    masked = sum((i + 1) * rows - max(0, i * rows - reach) for i in range(blocks))
    return pl.pallas_call(
        partial(att_kernel, s, heads, acc is not None, part_in is not None, is_last),
        out_shape=(shared, shared, *grads, *last_vec),
        in_specs=specs,
        out_specs=(anywhere, anywhere, *grad_specs, *vec_specs),
        scratch_shapes=[
            pltpu.VMEM((blocks, rows, features), low),
            pltpu.VMEM((blocks, rows, features), low),
            pltpu.VMEM((3 * part, features), low),
            pltpu.VMEM((part, features), low),
            pltpu.VMEM((length, features), low),
            pltpu.VMEM((length, features), low),
            pltpu.VMEM((length, features), low),
            pltpu.VMEM((part, length), low),
            pltpu.VMEM((part, length), low),
            pltpu.VMEM((part, length), low),
            pltpu.VMEM((heads, length, HEAD), low),
            pltpu.VMEM((heads, length, HEAD), low),
            pltpu.VMEM((part, length), low),
            pltpu.VMEM((masked, rows), wide),
            pltpu.VMEM((part, length), low),
            pltpu.VMEM((3 * part, length), low),
            pltpu.VMEM((part, length), wide),
            pltpu.VMEM((part, length), wide),
            pltpu.VMEM((4, rows, features), low),
            pltpu.VMEM((4, rows, features), low),
            pltpu.VMEM((3 * part, features), wide),
            pltpu.VMEM((part, features), wide),
            pltpu.SemaphoreType.DMA((8,)),
            pltpu.SemaphoreType.DMA((4,)),
            pltpu.SemaphoreType.DMA((8,)),
            *more,
        ],
        input_output_aliases=aliases,
        compiler_params=pltpu.CompilerParams(vmem_limit_bytes=50 * 2**20),
        cost_estimate=pl.CostEstimate(flops=1, bytes_accessed=1, transcendentals=0),
        name="attention",
    )(*operands)


def split_kernel(me_ref, keep, got, *refs):
    pieces, both = refs[:4], refs[4]
    r = me_ref[3]
    half = both.shape[0] // 2
    fine, short = half // 16, half // 4
    both[...] = keep[...].astype(wide) + got[...].astype(wide)
    for k, piece in enumerate(pieces):
        cut = r ^ k
        parts = [both[pl.ds(pl.multiple_of(b * 4 * fine + cut * fine, 8), fine), :] for b in range(4)]
        piece[0 : 4 * fine, :] = jnp.concatenate(parts).astype(piece.dtype)
        piece[4 * fine :, :] = both[pl.ds(pl.multiple_of(half + cut * short, 8), short), :].astype(piece.dtype)


def split_call(me, keep, got):
    shape = (keep.shape[0] // 4, keep.shape[1])
    return pl.pallas_call(
        split_kernel,
        out_shape=(jax.ShapeDtypeStruct(shape, wide),) + (jax.ShapeDtypeStruct(shape, low),) * 3,
        in_specs=[in_smem] + [in_vmem] * 2,
        out_specs=(in_vmem,) * 4,
        scratch_shapes=[pltpu.VMEM(keep.shape, wide)],
        name="split_gradients",
    )(me, keep, got)


def meet_kernel(me_ref, *refs):
    messages, (o_keep, o_near, o_far), pieces, (came, rows) = refs[:8], refs[8:11], refs[11:15], refs[15:]
    c, r = me_ref[0], me_ref[3]
    owned, features = o_keep.shape
    cols = came.shape[2]
    part, fine = cols // 3, owned // 4
    for k, message in enumerate(messages):
        came[k] = message[...].astype(wide)
    by_ctx = []
    for k in range(4):
        both = came[c ^ k] + came[4 + (c ^ k)]
        by_ctx.append(both)
        for t in range(3):
            lo = (4 * t + head_block(k)) * part
            rows[:, lo : lo + part] = both[0:owned, t * part : (t + 1) * part]
    rows[:, 3 * features :] = o_keep[...] + o_near[...].astype(wide) + o_far[...].astype(wide)
    vecs = [
        jnp.concatenate([b[owned : owned + 8, :], b[owned + 8 : owned + 16, 0 : features - cols]], axis=1)
        for b in by_ctx
    ]
    shared = (vecs[0] + vecs[1]) + (vecs[2] + vecs[3])
    vec = jnp.concatenate([shared[0:5]] + [v[5:6] for v in vecs] + [v[6:7] for v in vecs] + [shared[7:8]] * 3)
    for k, piece in enumerate(pieces):
        cut = r ^ k
        own = vec[0:4]
        for m in range(1, 4):
            own = jnp.where(cut == m, vec[4 * m : 4 * m + 4], own)
        piece[:, 0 : 4 * features] = rows[pl.ds(pl.multiple_of(cut * fine, 8), fine), :].astype(piece.dtype)
        lanes = [own[i // 6 : i // 6 + 1, i % 6 * 128 : i % 6 * 128 + 128] for i in range(24)]
        piece[:, 4 * features :] = jnp.concatenate(lanes).astype(piece.dtype)


def meet_call(me, messages, outs):
    owned, features = outs[0].shape
    assert features == 6 * 128 and owned == 96
    shape = (owned // 4, 4 * features + 128)
    return pl.pallas_call(
        meet_kernel,
        out_shape=(jax.ShapeDtypeStruct(shape, wide),) + (jax.ShapeDtypeStruct(shape, low),) * 3,
        in_specs=[in_smem] + [in_vmem] * 11,
        out_specs=(in_vmem,) * 4,
        scratch_shapes=[
            pltpu.VMEM((8, *messages[0].shape), wide),
            pltpu.VMEM((owned, 4 * features), wide),
        ],
        name="meet_gradients",
    )(me, *messages, *outs)


def spread_kernel(me_ref, p0, p1, p2, p3, b0, b1, b2, b3, rows_out, scratch):
    c, r = me_ref[0], me_ref[3]
    owned = b0.shape[0]
    fine, short = owned // 4, rows_out.shape[0] // 4
    for k, p in enumerate((p0, p1, p2, p3)):
        cut = r ^ k
        value = p[...].astype(wide)
        for b in range(4):
            scratch[b, pl.ds(pl.multiple_of(cut * fine, 8), fine), :] = value[b * fine : (b + 1) * fine]
        rows_out[pl.ds(pl.multiple_of(cut * short, 8), short), :] = value[owned:]
    for k, out in enumerate((b0, b1, b2, b3)):
        out[...] = scratch[c ^ k].astype(low)


def spread_call(me, owned, row_rows, pieces):
    features = pieces[0].shape[1]
    return pl.pallas_call(
        spread_kernel,
        out_shape=(jax.ShapeDtypeStruct((owned, features), low),) * 4
        + (jax.ShapeDtypeStruct((row_rows, features), wide),),
        in_specs=[in_smem] + [in_vmem] * 4,
        out_specs=(in_vmem,) * 5,
        scratch_shapes=[pltpu.VMEM((4, owned, features), wide)],
        name="spread_gradients",
    )(me, *pieces)


def join_ff_kernel(me_ref, b0, b1, b2, b3, out):
    c = me_ref[0]
    unit = out.shape[1] // 8
    for k, b in enumerate((b0, b1, b2, b3)):
        for t in range(2):
            lo = pl.multiple_of((4 * t + (c ^ k)) * unit, 128)
            out[:, pl.ds(lo, unit)] = b[:, t * unit : (t + 1) * unit].astype(wide)


def join_ff_call(me, blocks):
    owned, hidden = blocks[0].shape
    return pl.pallas_call(
        join_ff_kernel,
        out_shape=jax.ShapeDtypeStruct((owned, 4 * hidden), wide),
        in_specs=[in_smem] + [in_vmem] * 4,
        out_specs=in_vmem,
        name="join_fc_gradient",
    )(me, *blocks)


def join_att_kernel(me_ref, p0, p1, p2, p3, qkv_out, rows_out, *refs):
    outs, (vec, row) = refs[:8], refs[8:]
    c, f, r = me_ref[0], me_ref[1], me_ref[3]
    features, fine = rows_out.shape[1], p0.shape[0]
    part = features // 4
    for k, p in enumerate((p0, p1, p2, p3)):
        cut = r ^ k
        rows = pl.ds(pl.multiple_of(cut * fine, 8), fine)
        value = p[...].astype(wide)
        qkv_out[rows, :] = value[:, 0 : 3 * features]
        rows_out[rows, :] = value[:, 3 * features : 4 * features]
        vec[cut] = value[:, 4 * features :]

    mine = f * 4 + c
    total = [
        jnp.concatenate([vec[k // 4, k % 4 * 6 + i : k % 4 * 6 + i + 1, :] for i in range(6)], axis=1) for k in range(13)
    ]

    def choose(values, index):
        value = values[0]
        for k in range(1, len(values)):
            value = jnp.where(index == k, values[k], value)
        return value

    for i in (0, 1, 2, 3, 4, 7):
        size = outs[i].shape[0]
        source = total[min(i, 4)]
        outs[i][...] = choose([source[:, k * size : (k + 1) * size] for k in range(8)], mine).reshape(size)
    size = outs[5].shape[0]
    for k in range(4):
        for t in range(3):
            lo = (4 * t + head_block(k)) * part
            row[0:1, lo : lo + part] = total[9 + k][:, t * part : (t + 1) * part]
    outs[5][...] = choose([row[0:1, k * size : (k + 1) * size] for k in range(8)], mine).reshape(size)
    size = outs[6].shape[0]
    pieces = [total[5 + k][:, t * size : (t + 1) * size] for t in range(2) for k in range(4)]
    outs[6][...] = choose(pieces, mine).reshape(size)


def join_att_call(me, owned, features, pieces):
    sizes = (features // 8,) * 5 + (3 * features // 8, features // 2, features // 8)
    return pl.pallas_call(
        join_att_kernel,
        out_shape=(
            jax.ShapeDtypeStruct((owned, 3 * features), wide),
            jax.ShapeDtypeStruct((owned, features), wide),
        )
        + tuple(jax.ShapeDtypeStruct((n,), wide) for n in sizes),
        in_specs=[in_smem] + [in_vmem] * 4,
        out_specs=(in_vmem,) * 10,
        scratch_shapes=[pltpu.VMEM((4, owned // 4, 128), wide), pltpu.VMEM((8, 3 * features), wide)],
        name="join_qkv_gradient",
    )(me, *pieces)


def finish_kernel(seqs, x_ref, cot_ref, vecs, *refs):
    nears, overs, (out, grad) = refs[:seqs], refs[seqs : 2 * seqs], refs[2 * seqs :]
    for s, (near, over) in enumerate(zip(nears, overs)):
        x = x_ref[s].astype(wide)
        total = near[0].astype(wide) + over[0].astype(wide)
        out[s] = (x + total + vecs[4:5, :]).astype(low)
        e = near[1].astype(wide) + over[1].astype(wide)
        center = x - jnp.mean(x, axis=-1, keepdims=True)
        spread = jnp.mean(center * center, axis=-1, keepdims=True)
        root = lax.rsqrt(spread + epsilon)
        n = center * root
        back = root * (e - jnp.mean(e, axis=-1, keepdims=True) - n * jnp.mean(e * n, axis=-1, keepdims=True))
        grad[s] = (cot_ref[s].astype(wide) + back).astype(low)


def finish_call(tokens, cotangent, vecs, nears, overs):
    seqs = len(nears)
    shape = jax.ShapeDtypeStruct(tokens.shape, low)
    return pl.pallas_call(
        partial(finish_kernel, seqs),
        out_shape=(shape, shape),
        in_specs=[in_vmem] * (3 + 2 * seqs),
        out_specs=(in_vmem,) * 2,
        name="finish_tokens",
    )(tokens, cotangent, vecs, *nears, *overs)


def shards(
    tokens,
    segment,
    ln1_gain,
    ln1_bias,
    qkv_weight,
    qkv_bias,
    out_weight,
    out_bias,
    ln2_gain,
    ln2_bias,
    fc_weight,
    fc_bias,
    proj_weight,
    proj_bias,
    cotangent,
):
    ctx, fsdp, rep = lax.axis_size("ctx"), lax.axis_size("fsdp"), lax.axis_size("rep")
    c, f, r = lax.axis_index("ctx"), lax.axis_index("fsdp"), lax.axis_index("rep")
    paired = fsdp == 2 and ctx == 4 and rep == 4
    seqs, local_len, features = tokens.shape
    length = local_len * ctx
    owned = qkv_weight.shape[0]
    hidden_own = proj_weight.shape[0]
    hidden_all = fc_weight.shape[1]
    hidden = hidden_all // ctx
    part = features // ctx
    me = f * ctx + c
    core = c & 1

    half = ROT // 2
    inverse = (1.0 / np.float32(10000.0) ** (np.arange(0, ROT, 2, dtype=np.float32) / ROT)).astype(np.float32)
    angles = inverse[:, None] * np.arange(length, dtype=np.float32)[None, :]
    cosine, sine = jnp.asarray(np.cos(angles)), jnp.asarray(np.sin(angles))

    def far_rows(s, *before):
        both = jnp.stack([tokens[s], cotangent[s]])
        return swap(after(both, *before) if before else both, "ctx", 2)

    near = (swap(tokens, "ctx", 1), swap(cotangent, "ctx", 1))

    if paired:
        where = jnp.stack([c, f, core, r]).astype(jnp.int32)
        vectors = (ln1_gain, ln1_bias, ln2_gain, ln2_bias, out_bias, proj_bias, qkv_bias, fc_bias)
        proj_x = swap(proj_weight, "fsdp", 1)
        q0, q1, q2, q3, f0, f1, f2, f3 = pack_call(where, qkv_weight, fc_weight, segment, vectors)
        f_got = [swap(f1, "ctx", 1), swap(f2, "ctx", 2), swap(f3, "ctx", 3)]
        far_send = [jnp.stack([tokens[s], cotangent[s]]) for s in range(seqs)]
        f_got, far_send = lax.optimization_barrier((f_got, far_send))
        far = [swap(far_send[0], "ctx", 2)]
        f_half = rows_call(where, owned, (f0, *f_got))
        f_half, proj_x = lax.optimization_barrier((f_half, proj_x))
        f_other = swap(f_half, "fsdp", 1)
        far[0], f_other = lax.optimization_barrier((far[0], f_other))
        far_core = [swap(far[0], "ctx", 1)]
        vecs, bias, segs = prep_call(where, owned, part, seqs, length, f_half, f_other)
        proj_pair, fc_pair = (proj_weight, proj_x), (f_half, f_other)
    else:
        zero = jnp.zeros_like(c)
        where = jnp.stack([c, zero, zero, zero]).astype(jnp.int32)

        def whole(v, axes=("fsdp", "ctx")):
            return lax.all_gather(v, axes, axis=0, tiled=True)

        far = [far_rows(s) for s in range(seqs)]
        far_core = [swap(v, "ctx", 1) for v in far]
        bias = pick(whole(qkv_bias).reshape(3, ctx, part).transpose(1, 0, 2), c).astype(wide)
        bias = jnp.broadcast_to(bias.reshape(3 * part, 1), (3 * part, 128))
        b_sum = (whole(out_bias).astype(wide) + whole(proj_bias).astype(wide)).reshape(1, features)
        vecs = [whole(v).astype(wide) for v in (ln1_gain, ln1_bias, ln2_gain, ln2_bias)]
        vecs += [b_sum.reshape(features), pick(whole(fc_bias).reshape(ctx, hidden), c).astype(wide)]
        vecs = jnp.concatenate([jnp.stack(vecs), jnp.zeros((2, features), wide)])
        segs = lax.all_gather(segment.astype(low), "ctx", axis=1, tiled=True).astype(wide)
        segs = jnp.concatenate([segs, jnp.zeros((8 - seqs, length), wide)])

        def halves(v):
            return v[: v.shape[0] // 2], v[v.shape[0] // 2 :]

        out_pair = halves(pick(whole(out_weight).reshape(ctx, part, features), c))
        proj_pair = halves(pick(whole(proj_weight).reshape(ctx, hidden, features), c))
        qkv_pair = pick(whole(qkv_weight).reshape(features, 3, ctx, part).transpose(2, 0, 1, 3), c)
        qkv_pair = halves(qkv_pair.reshape(features, 3 * part))
        fc_pair = halves(pick(whole(fc_weight).reshape(features, ctx, hidden).transpose(1, 0, 2), c))

    def run_ff(s, args, acc, part_in, is_last):
        send, keep, *grads = ff_call(s, where, args, *fc_pair, *proj_pair, vecs, acc, part_in, is_last)
        return (send, keep), grads

    def run_att(s, args, weights, acc, part_in, vec=None):
        send, keep, *grads = att_call(
            s, where, args, *weights[0], bias, *weights[1], vecs, segs, cosine, sine, acc, part_in, vec
        )
        return (send, keep), grads

    def near_rows(send, keep):
        got = swap(send, "ctx", 1)
        return [(keep[k : k + 2].astype(wide) + got[k : k + 2].astype(wide)).astype(low) for k in (0, 2)]

    def to_rep(pieces):
        return [swap(piece, "rep", k) for k, piece in zip(range(1, rep), pieces)]

    def to_ctx(pieces):
        return [swap(piece, "ctx", k) for k, piece in zip(range(1, ctx), pieces)]

    def add_up(first, others):
        total = first
        for value in others:
            total = total + value.astype(wide)
        return total.astype(low)

    phase = lax.optimization_barrier
    if paired:
        args = (tokens, cotangent, *near, far[0], far_core[0])
        far_send, q1, q2, q3, args = phase((far_send, q1, q2, q3, args))
        far1 = swap(far_send[1], "ctx", 2)
        q_got = [swap(q1, "ctx", 1), swap(q2, "ctx", 2), swap(q3, "ctx", 3)]
        part0, acc = run_ff(0, args, None, None, False)

        part0, acc, far1, q_got = phase((part0, acc, far1, q_got))
        q_half = rows_call(where, owned, (q0, *q_got))
        far1_core = swap(far1, "ctx", 1)
        far1_core, far_send, q_half, acc = phase((far1_core, far_send, q_half, acc))
        far2 = swap(far_send[2], "ctx", 2)
        q_other = swap(q_half, "fsdp", 1)
        out_x = swap(out_weight, "fsdp", 1)
        part1, acc = run_ff(1, (tokens, cotangent, *near, far1, far1_core), acc, None, False)

        part1, acc, far2, q_other, out_x = phase((part1, acc, far2, q_other, out_x))
        far2_core = swap(far2, "ctx", 1)
        out_keep = jnp.where(core == f, out_weight, out_x)
        out_got = swap(jnp.where(core == f, out_x, out_weight), "ctx", 1)
        att_weights = ((q_half, q_other), (out_keep, out_got))
        part2, ff_last = run_ff(2, (tokens, cotangent, *near, far2, far2_core), acc, None, True)

        part0, ff_last, att_weights = phase((part0, ff_last, att_weights))
        ff_got = swap(ff_last[1], "fsdp", 1)
        args = (tokens, cotangent, *near, far[0], far_core[0])
        part0, att_acc = run_att(0, args, att_weights, None, part0)

        part0, att_acc, ff_got = phase((part0, att_acc, ff_got))
        ff_pieces = split_call(where, ff_last[0], ff_got)
        near0, away = near_rows(*part0)
        ff_pieces, near0, away, part1, att_acc = phase((ff_pieces, near0, away, part1, att_acc))
        ff_got = to_rep(ff_pieces[1:])
        over0 = swap(away, "ctx", 2)
        args = (tokens, cotangent, *near, far1, far1_core)
        part1, att_acc = run_att(1, args, att_weights, att_acc, part1)

        part1, att_acc, ff_got, over0 = phase((part1, att_acc, ff_got, over0))
        ff_total = add_up(ff_pieces[0], ff_got)
        near1, away = near_rows(*part1)
        ff_total, near1, away, part2, att_acc = phase((ff_total, near1, away, part2, att_acc))
        ff_got = to_rep([ff_total] * (rep - 1))
        over1 = swap(away, "ctx", 2)
        args = (tokens, cotangent, *near, far2, far2_core)
        part2, att_last = run_att(2, args, att_weights, att_acc, part2, ff_last[2])

        part2, att_last, ff_got, over1 = phase((part2, att_last, ff_got, over1))
        flat = [(k, i) for k in range(fsdp) for i in range(ctx)]
        messages = [att_last[0]]
        for g, h in flat[1:]:
            peers = [(k * ctx + i, (k ^ g) * ctx + (i ^ h)) for k, i in flat]
            messages.append(lax.ppermute(att_last[g * ctx + h], ("fsdp", "ctx"), peers))
        pairs = [(k, i, 1 - k, i) if (i & 1) != k else (k, i, k, i ^ 1) for k, i in flat]
        near_got = lax.ppermute(att_last[9], ("fsdp", "ctx"), [(a * ctx + b, d * ctx + e) for a, b, d, e in pairs])
        pairs = [(k * ctx + i, (1 - k) * ctx + (i ^ 1)) for k, i in flat if (i & 1) != k]
        far_got = lax.ppermute(att_last[10], ("fsdp", "ctx"), pairs)
        near2, away = near_rows(*part2)
        *ff_blocks, g_proj = spread_call(where, owned, hidden_own, (ff_total, *ff_got))
        messages, near_got, far_got, near2, away, ff_blocks = phase(
            (messages, near_got, far_got, near2, away, ff_blocks)
        )

        pieces = meet_call(where, messages, (att_last[8], near_got, far_got))
        pieces, away = phase((pieces, away))
        got = to_rep(pieces[1:])
        over2 = swap(away, "ctx", 2)
        got, over2 = phase((got, over2))

        piece = add_up(pieces[0], got)
        piece, over2, ff_blocks = phase((piece, over2, ff_blocks))
        others = to_rep([piece] * (rep - 1))
        ff_blocks_got = to_ctx(ff_blocks[1:])
        output, grad_tokens = finish_call(tokens, cotangent, vecs, (near0, near1, near2), (over0, over1, over2))
        g_fc = join_ff_call(where, (ff_blocks[0], *ff_blocks_got))
        g_qkv, g_out, *vector_grads = join_att_call(where, owned, features, (piece, *others))
    else:
        att_acc = ff_acc = None
        nears, overs = [], []
        for s in range(seqs):
            args = (tokens, cotangent, *near, far[s], far_core[s])
            parts, ff_acc = run_ff(s, args, ff_acc, None, s == seqs - 1)
            vec = ff_acc[2] if s == seqs - 1 else None
            parts, att_acc = run_att(s, args, (qkv_pair, out_pair), att_acc, parts, vec)
            near_sum, away = near_rows(*parts)
            nears.append(near_sum)
            overs.append(swap(away, "ctx", 2))
        output, grad_tokens = finish_call(tokens, cotangent, vecs, nears, overs)

        def any_columns(kept, sent):
            grad = jnp.concatenate([kept.astype(low), sent])
            grad = lax.psum_scatter(grad, "fsdp", scatter_dimension=0, tiled=True)
            grad = lax.psum(grad, "rep").reshape(ctx, owned, -1)
            return lax.all_to_all(grad, "ctx", split_axis=0, concat_axis=0)

        def any_rows(kept, sent):
            grad = jnp.concatenate([kept.astype(low), sent])
            grad = jnp.where(jnp.arange(ctx)[:, None, None] == c, grad[None], 0).reshape(-1, features)
            return lax.psum(
                lax.psum_scatter(grad, ("fsdp", "ctx"), scatter_dimension=0, tiled=True), "rep"
            )

        cut = features // 2
        g_fc = any_columns(ff_acc[0][:cut], ff_acc[1][:cut])
        g_fc = g_fc.transpose(1, 0, 2).reshape(owned, hidden_all)
        g_proj = any_rows(ff_acc[0][cut:], ff_acc[1][cut:])
        sent = jnp.concatenate([att_acc[0][None].astype(low), jnp.stack(att_acc[1:8])])
        whole_w = jnp.concatenate(in_order([v[: part // 2] for v in sent], c))
        g_qkv = any_columns(whole_w[: features // 2], whole_w[features // 2 :]).reshape(ctx, owned, 3, part)
        g_qkv = g_qkv.transpose(1, 2, 0, 3).reshape(owned, 3 * features)
        g_out = any_rows(*att_acc[8:10])
        vec = att_acc[0][part // 2 :]
        vec = jnp.concatenate([vec[:8], vec[8:, : features - 3 * part]], axis=1)
        total_vec = jnp.zeros((16, features), wide).at[0:5].set(vec[0:5])
        total_vec = lax.dynamic_update_slice(total_vec, vec[5:6], (5 + c, 0))
        total_vec = lax.dynamic_update_slice(total_vec, vec[6:7], (9 + c, 0))
        total_vec = lax.psum(total_vec, ("ctx", "fsdp", "rep"))
        grads = [total_vec[k] for k in range(5)]
        grads.append(total_vec[9 : 9 + ctx, : 3 * part].reshape(ctx, 3, part).transpose(1, 0, 2).reshape(-1))
        grads.append(total_vec[5 : 5 + ctx, :hidden].reshape(-1))
        grads.append(total_vec[4])
        vector_grads = []
        for v in grads:
            size = v.shape[0] // (fsdp * ctx)
            vector_grads.append(lax.dynamic_slice(v, (me * size,), (size,)))
    g_gain_one, g_shift_one, g_gain_two, g_shift_two, g_b_out, g_b_qkv, g_b_fc, g_b_proj = vector_grads
    return (
        output,
        grad_tokens,
        g_gain_one,
        g_shift_one,
        g_qkv.astype(wide),
        g_b_qkv,
        g_out.astype(wide),
        g_b_out,
        g_gain_two,
        g_shift_two,
        g_fc.astype(wide),
        g_b_fc,
        g_proj.astype(wide),
        g_b_proj,
    )


def solution(mesh):
    rows, row = P(("rep", "fsdp"), "ctx", None), P(("rep", "fsdp"), "ctx")
    vector, matrix = P(("fsdp", "ctx")), P(("fsdp", "ctx"), None)
    params = (
        vector, vector, matrix, vector, matrix, vector,
        vector, vector, matrix, vector, matrix, vector,
    )
    return jax.shard_map(
        shards,
        mesh=mesh,
        in_specs=(rows, row, *params, rows),
        out_specs=(rows, rows, *params),
        check_vma=False,
    )
```

```python
from functools import partial
import math

import jax
import jax.numpy as jnp
import numpy as np
from jax import lax
from jax.experimental import pallas as pl
from jax.experimental.pallas import tpu as pltpu
from jax.sharding import PartitionSpec as P

HEADS = 12
HEAD = 64
ROT = 16

epsilon = 1e-05
far_below = -1e30
low = jnp.bfloat16
wide = jnp.float32
log2e = math.log2(math.e)


def nn(a, b):
    return lax.dot_general(a, b, (((1,), (0,)), ((), ())), preferred_element_type=wide)


def nt(a, b):
    return lax.dot_general(a, b, (((1,), (1,)), ((), ())), preferred_element_type=wide)


def swap(value, axis, bits):
    size = lax.axis_size(axis)
    return lax.ppermute(value, axis, [(i, i ^ bits) for i in range(size)])


def in_order(rel, me):
    out = []
    for k in range(len(rel)):
        value = rel[k]
        for m in range(1, len(rel)):
            value = jnp.where(me == m, rel[k ^ m], value)
        out.append(value)
    return out


def pick(stacked, index):
    return lax.dynamic_index_in_dim(stacked, index, 0, keepdims=False)


def after(value, *before):
    return lax.optimization_barrier((value, before))[0]


anywhere = pl.BlockSpec(memory_space=pltpu.HBM)
in_vmem = pl.BlockSpec(memory_space=pltpu.VMEM)
in_smem = pl.BlockSpec(memory_space=pltpu.SMEM)
extra_rows = 16


def head_block(index):
    return ((index & 1) << 1) | (index >> 1)


def pack_kernel(vectors, me_ref, qkv, fc, segment, *refs):
    vector_refs, refs = refs[:vectors], refs[vectors:]
    q0, q1, q2, q3, f0, f1, f2, f3, scratch, extra = refs
    c = me_ref[0]
    owned, part, unit = qkv.shape[0], qkv.shape[1] // 12, fc.shape[1] // 8
    extra[...] = jnp.zeros_like(extra)
    for row, ref in enumerate(vector_refs):
        extra[row : row + 1, 0 : ref.shape[0]] = ref[...].astype(wide).reshape(1, -1)
    extra[8 : 8 + segment.shape[0], 0 : segment.shape[1]] = segment[...].astype(wide)
    for k in range(4):
        block = head_block(k)
        for t in range(3):
            lo = (4 * t + block) * part
            scratch[k ^ c, :, t * part : (t + 1) * part] = qkv[:, lo : lo + part]
    for k, (q, g) in enumerate(((q0, f0), (q1, f1), (q2, f2), (q3, f3))):
        q[...] = scratch[k]
        for t in range(2):
            lo = pl.multiple_of((4 * t + (c ^ k)) * unit, 128)
            g[0:owned, t * unit : (t + 1) * unit] = fc[:, pl.ds(lo, unit)]
        g[owned:, :] = extra[...].astype(low)


def pack_call(me, qkv, fc, segment, vectors):
    owned = qkv.shape[0]
    narrow, broad = (owned, qkv.shape[1] // 4), (owned + extra_rows, fc.shape[1] // 4)
    shapes = (narrow,) * 4 + (broad,) * 4
    return pl.pallas_call(
        partial(pack_kernel, len(vectors)),
        out_shape=tuple(jax.ShapeDtypeStruct(s, low) for s in shapes),
        in_specs=[in_smem] + [in_vmem] * (3 + len(vectors)),
        out_specs=(in_vmem,) * 8,
        scratch_shapes=[
            pltpu.VMEM((4, owned, narrow[1]), low),
            pltpu.VMEM((extra_rows, broad[1]), wide),
        ],
        name="pack_columns",
    )(me, qkv, fc, segment, *vectors)


def rows_kernel(owned, me_ref, p0, p1, p2, p3, half):
    c = me_ref[0]
    tail = p0.shape[0] - owned
    for k, p in enumerate((p0, p1, p2, p3)):
        half[pl.ds(pl.multiple_of((c ^ k) * owned, 16), owned), :] = p[0:owned, :]
        if tail:
            half[pl.ds(pl.multiple_of(4 * owned + (c ^ k) * tail, 16), tail), :] = p[owned:, :]


def rows_call(me, owned, pieces):
    rows, cols = pieces[0].shape
    return pl.pallas_call(
        partial(rows_kernel, owned),
        out_shape=jax.ShapeDtypeStruct((4 * rows, cols), low),
        in_specs=[in_smem] + [in_vmem] * 4,
        out_specs=in_vmem,
        name="rows_by_ctx",
    )(me, *pieces)


def prep_kernel(owned, part, seqs, me_ref, mine, other, vecs, bias, seg):
    c, f = me_ref[0], me_ref[1]
    extra_mine, extra_other = mine[...].astype(wide), other[...].astype(wide)
    first = jnp.where(f == 0, extra_mine, extra_other)
    last = jnp.where(f == 0, extra_other, extra_mine)

    def vector(row, size):
        pieces = [
            e[k * extra_rows + row : k * extra_rows + row + 1, 0:size]
            for e in (first, last)
            for k in range(4)
        ]
        return jnp.concatenate(pieces, axis=1)

    block = head_block(c)
    vecs[...] = jnp.zeros_like(vecs)
    for row in range(4):
        vecs[row : row + 1, :] = vector(row, owned)
    vecs[4:5, :] = vector(4, owned) + vector(5, owned)
    unit = mine.shape[1] // 2
    for t, e in enumerate((first, last)):
        chosen = e[7:8, 0:unit]
        for k in range(1, 4):
            chosen = jnp.where(c == k, e[k * extra_rows + 7 : k * extra_rows + 8, 0:unit], chosen)
        vecs[5:6, t * unit : (t + 1) * unit] = chosen
    all_qkv = vector(6, 3 * owned)
    picked = []
    for t in range(3):
        chosen = all_qkv[:, 4 * t * part : (4 * t + 1) * part]
        for k in range(1, 4):
            chosen = jnp.where(block == k, all_qkv[:, (4 * t + k) * part : (4 * t + k + 1) * part], chosen)
        picked.append(chosen)
    row_bias = jnp.concatenate(picked, axis=1)
    bias[...] = jnp.transpose(jnp.broadcast_to(row_bias, (128, 3 * part)))
    seg[...] = jnp.zeros_like(seg)
    width = seg.shape[1] // 4
    for s in range(seqs):
        for k in range(4):
            row = k * extra_rows + 8 + s
            seg[s : s + 1, k * width : (k + 1) * width] = extra_mine[row : row + 1, 0:width]


def prep_call(me, owned, part, seqs, length, mine, other):
    tail = pl.BlockSpec((4 * extra_rows, mine.shape[1]), lambda i: (4 * owned // (4 * extra_rows), 0))
    assert 4 * owned % (4 * extra_rows) == 0
    shapes = ((8, 8 * owned), (3 * part, 128), (8, length))
    return pl.pallas_call(
        partial(prep_kernel, owned, part, seqs),
        grid=(1,),
        out_shape=tuple(jax.ShapeDtypeStruct(s, wide) for s in shapes),
        in_specs=[in_smem, tail, tail],
        out_specs=tuple(pl.BlockSpec(s, lambda i: (0, 0)) for s in shapes),
        name="prepare_vectors",
    )(me, mine, other)


def row_norm(block):
    values = block.astype(wide)
    center = values - jnp.mean(values, axis=-1, keepdims=True)
    spread = jnp.mean(center * center, axis=-1, keepdims=True)
    return center * lax.rsqrt(spread + epsilon)


def gelu_parts(v):
    bell = jnp.exp2(v * v * (-0.5 * log2e))
    base = 1.0 + (0.3275911 / math.sqrt(2.0)) * jnp.abs(v)
    t = pl.reciprocal(base, approx=True)
    t = t * (2.0 - base * t)
    poly = 0.5 * 1.061405429
    for coef in (-1.453152027, 1.421413741, -0.284496736, 0.254829592):
        poly = poly * t + 0.5 * coef
    tail = poly * t * bell
    phi = jnp.where(v >= 0, 1.0 - tail, tail)
    return phi, phi + v * bell * (1.0 / math.sqrt(2.0 * math.pi))


def bring(pairs, sem):
    copies = [pltpu.make_async_copy(a, b, sem.at[k]) for k, (a, b) in enumerate(pairs)]
    for copy in copies:
        copy.start()
    return copies


def token_pairs(s, refs, xs, cs):
    tok, cot, tok1, cot1, far, far1 = refs
    pairs = []
    for j, (t, c) in enumerate(
        ((tok.at[s], cot.at[s]), (tok1.at[s], cot1.at[s]), (far.at[0], far.at[1]), (far1.at[0], far1.at[1]))
    ):
        pairs += [(t, xs.at[j]), (c, cs.at[j])]
    return pairs


def ff_kernel(s, with_acc, with_part, is_last, *refs):
    me_ref, refs = refs[0], refs[1:]
    token_refs, refs = refs[:6], refs[6:]
    fc_a, fc_b, proj_a, proj_b, vecs = refs[:5]
    refs = refs[5:]
    if with_acc:
        acc_fc_in, acc_proj_in, acc_vec_in = refs[:3]
        refs = refs[3:]
    if with_part:
        part_send, part_keep = refs[:2]
        refs = refs[2:]
    send, keep = refs[:2]
    refs = refs[2:]
    if is_last:
        grad_keep, grad_send, vec = refs[:3]
        refs = refs[3:]
    else:
        fc_out, proj_out, vec = refs[:3]
        refs = refs[3:]
    xs, cs, fc, proj, sec_s, hid_s, gp_s, send_s, keep_s, acc_fc, acc_proj, sem, sem_w, sem_p, sem_o = refs[:15]
    if is_last:
        stage_keep, stage_send = refs[15:]
    f = me_ref[1]
    blocks, rows, features = xs.shape
    hidden = fc.shape[1]
    third, half = features // 2, proj_a.shape[0]
    tokens_in = bring(token_pairs(s, token_refs, xs, cs), sem)
    weights_in = bring(
        [
            (fc_a.at[0:third], fc.at[pl.ds(pl.multiple_of(f * third, 16), third), :]),
            (fc_b.at[0:third], fc.at[pl.ds(pl.multiple_of((1 - f) * third, 16), third), :]),
            (proj_a, proj.at[pl.ds(pl.multiple_of(f * half, 16), half), :]),
            (proj_b, proj.at[pl.ds(pl.multiple_of((1 - f) * half, 16), half), :]),
        ],
        sem_w,
    )
    later = []
    if with_part:
        later += [(part_send, send_s), (part_keep, keep_s)]
    if with_acc:
        later += [(acc_fc_in, acc_fc), (acc_proj_in, acc_proj)]
    later = bring(later, sem_p)
    for copy in weights_in + tokens_in:
        copy.wait()
    gain, shift, bias = vecs[2:3, :], vecs[3:4, :], vecs[5:6, 0:hidden]
    dgain = jnp.zeros((1, features), wide)
    dshift = jnp.zeros((1, features), wide)
    dbias = jnp.zeros((1, hidden), wide)
    if with_part:
        later[0].wait()
        later[1].wait()
    for j in range(blocks):
        here = pl.ds(j * rows, rows)
        n = row_norm(xs[j])
        second = (n * gain + shift).astype(low)
        sec_s[here, :] = second
        cot = cs[j]
        pre = nn(second, fc[...]) + bias
        phi, slope = gelu_parts(pre)
        hid = (pre * phi).astype(low)
        gp = nt(cot, proj[...]) * slope
        dbias = dbias + jnp.sum(gp, axis=0, keepdims=True)
        gp = gp.astype(low)
        hid_s[here, :] = hid
        gp_s[here, :] = gp
        out = nn(hid, proj[...])
        dsec = nt(gp, fc[...])
        dgain = dgain + jnp.sum(dsec * n, axis=0, keepdims=True)
        dshift = dshift + jnp.sum(dsec, axis=0, keepdims=True)
        e = dsec * gain
        to = send_s if j % 2 else keep_s
        if with_part:
            out = out + to[j // 2 * 2].astype(wide)
            e = e + to[j // 2 * 2 + 1].astype(wide)
        to[j // 2 * 2] = out.astype(low)
        to[j // 2 * 2 + 1] = e.astype(low)
    results = bring([(send_s, send), (keep_s, keep)], sem_o)
    dcot = jnp.sum(cs[0].astype(wide), axis=0, keepdims=True)
    if with_acc:
        for copy in later[-2:]:
            copy.wait()
        dgain = dgain + acc_vec_in[0:1, :]
        dshift = dshift + acc_vec_in[1:2, :]
        dbias = dbias + acc_vec_in[2:3, 0:hidden]
        dcot = dcot + acc_vec_in[3:4, :]
    every_cot = cs[...].reshape(blocks * rows, features)
    for k, (acc, a, b, own) in enumerate(((acc_fc, sec_s, gp_s[...], third), (acc_proj, hid_s, every_cot, half))):
        grad = nn(jnp.transpose(a[...]), b)
        acc[...] = grad + acc[...] if with_acc else grad
        if is_last:
            lo = k * third
            stage_keep[lo : lo + own, :] = acc[pl.ds(pl.multiple_of(f * own, 16), own), :].astype(low)
            stage_send[lo : lo + own, :] = acc[pl.ds(pl.multiple_of((1 - f) * own, 16), own), :].astype(low)
            moves = [(stage_keep, grad_keep), (stage_send, grad_send)]
            moves = [(x.at[lo : lo + own], y.at[lo : lo + own]) for x, y in moves]
        else:
            moves = [(acc, (fc_out, proj_out)[k])]
        for x, y in moves:
            results.append(pltpu.make_async_copy(x, y, sem_o.at[len(results)]))
            results[-1].start()
    vec[0:1, :] = dgain
    vec[1:2, :] = dshift
    vec[2:3, 0:hidden] = dbias
    vec[3:4, :] = dcot
    for copy in results:
        copy.wait()


def ff_call(s, me, token_args, fc_a, fc_b, proj_a, proj_b, vecs, acc, part, is_last):
    rows, features = token_args[0].shape[1:]
    hidden, blocks = fc_a.shape[1], 4
    total = blocks * rows
    third = features // 2
    operands = [me, *token_args, fc_a, fc_b, proj_a, proj_b, vecs]
    specs = [in_smem] + [anywhere] * 10 + [in_vmem]
    aliases = {}
    if acc is not None:
        if not is_last:
            aliases = {len(operands): 2, len(operands) + 1: 3}
        operands += list(acc)
        specs += [anywhere, anywhere, in_vmem]
    if part is not None:
        aliases[len(operands)] = 0
        aliases[len(operands) + 1] = 1
        operands += list(part)
        specs += [anywhere, anywhere]
    shared = jax.ShapeDtypeStruct((4, rows, features), low)
    vec = jax.ShapeDtypeStruct((8, features), wide)
    if is_last:
        rows_out = third + proj_a.shape[0]
        grads = (
            jax.ShapeDtypeStruct((rows_out, features), low),
            jax.ShapeDtypeStruct((rows_out, features), low),
        )
        grad_specs = (anywhere,) * 2
        more = [pltpu.VMEM((rows_out, features), low)] * 2
    else:
        grads = (
            jax.ShapeDtypeStruct((features, hidden), wide),
            jax.ShapeDtypeStruct((hidden, features), wide),
        )
        grad_specs, more = (anywhere,) * 2, []
    return pl.pallas_call(
        partial(ff_kernel, s, acc is not None, part is not None, is_last),
        out_shape=(shared, shared, *grads, vec),
        in_specs=specs,
        out_specs=(anywhere, anywhere, *grad_specs, in_vmem),
        scratch_shapes=[
            pltpu.VMEM((blocks, rows, features), low),
            pltpu.VMEM((blocks, rows, features), low),
            pltpu.VMEM((features, hidden), low),
            pltpu.VMEM((hidden, features), low),
            pltpu.VMEM((total, features), low),
            pltpu.VMEM((total, hidden), low),
            pltpu.VMEM((total, hidden), low),
            pltpu.VMEM((4, rows, features), low),
            pltpu.VMEM((4, rows, features), low),
            pltpu.VMEM((features, hidden), wide),
            pltpu.VMEM((hidden, features), wide),
            pltpu.SemaphoreType.DMA((8,)),
            pltpu.SemaphoreType.DMA((4,)),
            pltpu.SemaphoreType.DMA((4,)),
            pltpu.SemaphoreType.DMA((8,)),
            *more,
        ],
        input_output_aliases=aliases,
        compiler_params=pltpu.CompilerParams(vmem_limit_bytes=50 * 2**20),
        cost_estimate=pl.CostEstimate(flops=1, bytes_accessed=1, transcendentals=0),
        name="feed_forward",
    )(*operands)


def turn(block, cosine, sine):
    half = ROT // 2
    a, b = block[0:half], block[half:ROT]
    return jnp.concatenate([a * cosine - b * sine, b * cosine + a * sine, block[ROT:]], axis=0)


def att_kernel(s, heads, with_acc, with_part, is_last, *refs):
    me_ref, refs = refs[0], refs[1:]
    token_refs, refs = refs[:6], refs[6:]
    w_a, w_b, bias, wout_a, wout_b, vecs, segs, cosine, sine = refs[:9]
    refs = refs[9:]
    if is_last:
        ff_vec, refs = refs[0], refs[1:]
    if with_acc:
        acc_w_in, acc_o_in, acc_vec_in = refs[:3]
        refs = refs[3:]
    if with_part:
        part_send, part_keep = refs[:2]
        refs = refs[2:]
    send, keep = refs[:2]
    refs = refs[2:]
    if is_last:
        messages, (o_keep, o_send, o_send_far) = refs[:8], refs[8:11]
        refs = refs[11:]
    else:
        w_out, o_out, vec = refs[:3]
        refs = refs[3:]
    xs, cs, wt_s, wout, first_s, n_s, cot_s, qt_s, kt_s, vt_s, k_s, v_s, dot_s, mask_s, att_s, d_s, dk_s, dv_s = refs[:18]
    send_s, keep_s, acc_w, acc_o, sem, sem_p, sem_o = refs[18:25]
    if is_last:
        by_rows = refs[25]
    me, f, core = me_ref[0], me_ref[1], me_ref[2]
    blocks, rows, features = xs.shape
    part = heads * HEAD
    length = blocks * rows
    reach = length // 2
    scale = 1.0 / math.sqrt(HEAD)
    tokens_in = bring(token_pairs(s, token_refs, xs, cs), sem)
    gain, shift = vecs[0:1, :], vecs[1:2, :]
    share = w_a.shape[0]
    wt_s[:, pl.ds(pl.multiple_of(f * share, 128), share)] = jnp.transpose(w_a[...])
    wt_s[:, pl.ds(pl.multiple_of((1 - f) * share, 128), share)] = jnp.transpose(w_b[...])
    owned = wout_a.shape[0]
    wout[pl.ds(pl.multiple_of(core * owned, 16), owned), :] = wout_a[...]
    wout[pl.ds(pl.multiple_of((1 - core) * owned, 16), owned), :] = wout_b[...]

    seg_row = segs[s : s + 1, :]
    seg_col = jnp.transpose(jnp.broadcast_to(seg_row, (128, length)))
    spans, place = [], 0
    for i in range(blocks):
        start = max(0, i * rows - reach)
        count = (i + 1) * rows - start
        spans.append((start, count, place))
        ours = seg_row[:, i * rows : (i + 1) * rows]
        theirs = seg_col[start : start + count]
        theirs = jnp.concatenate([theirs] * (rows // 128), axis=1)
        key = start + lax.broadcasted_iota(jnp.int32, (count, rows), 0)
        query = i * rows + lax.broadcasted_iota(jnp.int32, (count, rows), 1)
        allowed = (theirs == ours) & (key <= query)
        mask_s[place : place + count, :] = jnp.where(allowed, 0.0, far_below)
        place += count

    for copy in tokens_in:
        copy.wait()
    wide_bias = jnp.concatenate([bias[...]] * (rows // 128), axis=1)
    for j in range(blocks):
        off = pl.multiple_of((me ^ j) * rows, rows)
        n = row_norm(xs[j])
        n_s[pl.ds(off, rows), :] = n.astype(low)
        first = (n * gain + shift).astype(low)
        first_s[pl.ds(off, rows), :] = first
        cot = cs[j]
        cot_s[pl.ds(off, rows), :] = cot
        cos_b, sin_b = cosine[:, pl.ds(off, rows)], sine[:, pl.ds(off, rows)]
        made = nt(wt_s[...], first) + wide_bias
        for h in range(heads):
            lo, hi = h * HEAD, (h + 1) * HEAD
            query = turn(made[lo:hi], cos_b, sin_b).astype(low)
            qt_s[lo:hi, pl.ds(off, rows)] = (query.astype(wide) * scale).astype(low)
            key = turn(made[part + lo : part + hi], cos_b, sin_b).astype(low)
            kt_s[lo:hi, pl.ds(off, rows)] = key
            value = made[2 * part + lo : 2 * part + hi].astype(low)
            vt_s[lo:hi, pl.ds(off, rows)] = value
            k_s[h, pl.ds(off, rows), :] = jnp.transpose(key)
            v_s[h, pl.ds(off, rows), :] = jnp.transpose(value)
        dot_s[:, pl.ds(off, rows)] = nt(wout[...], cot).astype(low)

    later = []
    if with_part:
        later += [(part_send, send_s), (part_keep, keep_s)]
    if with_acc:
        later += [(acc_w_in, acc_w), (acc_o_in, acc_o)]
    later = bring(later, sem_p)
    dk_s[...] = jnp.zeros_like(dk_s)
    dv_s[...] = jnp.zeros_like(dv_s)

    def one_head(h, carry):
        base = pl.multiple_of(h * HEAD, HEAD)
        mine = pl.ds(base, HEAD)
        for i in range(blocks):
            start, count, place = spans[i]
            here, there = slice(i * rows, (i + 1) * rows), slice(start, start + count)
            query, grad = qt_s[mine, here], dot_s[mine, here]
            score = nn(k_s[h, there, :], query) + mask_s[place : place + count, :]
            top = jnp.max(score, axis=0, keepdims=True)
            lifted = jnp.exp2((score - top) * log2e)
            total = jnp.sum(lifted, axis=0, keepdims=True)
            prob = lifted * (1.0 / total)
            prob_low = prob.astype(low)
            att_s[mine, here] = nn(vt_s[mine, there], prob_low).astype(low)
            dprob = nn(v_s[h, there, :], grad)
            inner = jnp.sum(prob * dprob, axis=0, keepdims=True)
            dscore = (prob * (dprob - inner)).astype(low)
            dv_s[mine, there] += nt(grad, prob_low)
            dk_s[mine, there] += nt(query, dscore)
            dq = nn(kt_s[mine, there], dscore) * scale
            cos_b, sin_b = cosine[:, here], sine[:, here]
            d_s[mine, here] = turn(dq, cos_b, -sin_b).astype(low)
        return carry

    lax.fori_loop(0, heads, one_head, 0)
    for h in range(heads):
        lo, hi = h * HEAD, (h + 1) * HEAD
        d_s[part + lo : part + hi, :] = turn(dk_s[lo:hi, :], cosine[...], -sine[...]).astype(low)
    d_s[2 * part : 3 * part, :] = dv_s[...].astype(low)

    g_w = nn(d_s[...], first_s[...])
    g_o = nn(att_s[...], cot_s[...])
    if with_part:
        later[0].wait()
        later[1].wait()
    if with_acc:
        later[-2].wait()
        later[-1].wait()
        g_w = g_w + acc_w[...]
        g_o = g_o + acc_o[...]
    acc_w[...] = g_w
    results = []
    if is_last:
        by_rows[...] = jnp.transpose(acc_w[...])
        for k, message in enumerate(messages):
            shard = (f ^ (k // 4)) * 4 + (me ^ (k % 4))
            block = by_rows[pl.ds(pl.multiple_of(shard * owned, 8), owned), :]
            message[0:owned, :] = block.astype(message.dtype)
        acc_o[...] = g_o
        mine = acc_o[pl.ds(pl.multiple_of(f * owned, 16), owned), :]
        o_keep[...] = jnp.where(f == core, mine, 0.0)
        o_send[...] = acc_o[pl.ds(pl.multiple_of((1 - f) * owned, 16), owned), :].astype(low)
        o_send_far[...] = mine.astype(low)
    else:
        acc_o[...] = g_o
        results = [
            pltpu.make_async_copy(acc_w, w_out, sem_o.at[2]),
            pltpu.make_async_copy(acc_o, o_out, sem_o.at[3]),
        ]
        for copy in results:
            copy.start()
    dgain = jnp.zeros((1, features), wide)
    dshift = jnp.zeros((1, features), wide)
    dbias = jnp.zeros((8, 3 * part), wide)
    for j in range(blocks):
        off = pl.multiple_of((me ^ j) * rows, rows)
        att = jnp.transpose(att_s[:, pl.ds(off, rows)])
        out = nn(att, wout[...])
        dqkv = jnp.transpose(d_s[:, pl.ds(off, rows)])
        dbias = dbias + nn(jnp.ones((8, rows), low), dqkv)
        dfirst = nn(dqkv, wt_s[...])
        n = n_s[pl.ds(off, rows), :].astype(wide)
        dgain = dgain + jnp.sum(dfirst * n, axis=0, keepdims=True)
        dshift = dshift + jnp.sum(dfirst, axis=0, keepdims=True)
        e = dfirst * gain
        to, first = send_s if j % 2 else keep_s, j // 2 * 2
        if with_part:
            out = out + to[first].astype(wide)
            e = e + to[first + 1].astype(wide)
        to[first] = out.astype(low)
        to[first + 1] = e.astype(low)
    results += bring([(send_s, send), (keep_s, keep)], sem_o)
    dbias = dbias[0:1]
    if with_acc:
        dgain = dgain + acc_vec_in[0:1, :]
        dshift = dshift + acc_vec_in[1:2, :]
        dbias = dbias + acc_vec_in[2:3, 0 : 3 * part]
    if is_last:
        cols = 3 * part
        rest = jnp.zeros((1, features - cols), wide)
        vec = jnp.concatenate(
            [dgain, dshift, ff_vec[0:2, :], ff_vec[3:4, :], ff_vec[2:3, :], jnp.concatenate([dbias, rest], axis=1)]
            + [jnp.zeros((1, features), wide)]
        )
        for message in messages:
            message[owned : owned + 8, :] = vec[:, 0:cols].astype(message.dtype)
            message[owned + 8 : owned + 16, 0 : features - cols] = vec[:, cols:].astype(message.dtype)
            message[owned + 8 : owned + 16, features - cols :] = jnp.zeros((8, 2 * cols - features), message.dtype)
    else:
        vec[0:1, :] = dgain
        vec[1:2, :] = dshift
        vec[2:3, 0 : 3 * part] = dbias
    for copy in results:
        copy.wait()


def att_call(s, me, token_args, w_a, w_b, bias, wout_a, wout_b, vecs, segs, cosine, sine, acc, part_in, ff_vec):
    rows, features = token_args[0].shape[1:]
    part, blocks = w_a.shape[1] // 3, 4
    heads = part // HEAD
    length = blocks * rows
    is_last = ff_vec is not None
    operands = [me, *token_args, w_a, w_b, bias, wout_a, wout_b, vecs, segs, cosine, sine]
    operands += [ff_vec] if is_last else []
    specs = [in_smem] + [anywhere] * 6 + [in_vmem] * (len(operands) - 7)
    aliases = {}
    if acc is not None:
        if not is_last:
            aliases = {len(operands): 2, len(operands) + 1: 3}
        operands += list(acc)
        specs += [anywhere, anywhere, in_vmem]
    if part_in is not None:
        aliases[len(operands)] = 0
        aliases[len(operands) + 1] = 1
        operands += list(part_in)
        specs += [anywhere, anywhere]
    shared = jax.ShapeDtypeStruct((4, rows, features), low)
    if is_last:
        message = (part // 2 + 16, 3 * part)
        grads = (jax.ShapeDtypeStruct(message, wide),) + (jax.ShapeDtypeStruct(message, low),) * 7
        grads += (
            jax.ShapeDtypeStruct((part // 2, features), wide),
            jax.ShapeDtypeStruct((part // 2, features), low),
            jax.ShapeDtypeStruct((part // 2, features), low),
        )
        grad_specs = (in_vmem,) * 11
        last_vec, vec_specs = (), ()
        more = [pltpu.VMEM((features, 3 * part), wide)]
    else:
        grads = (
            jax.ShapeDtypeStruct((3 * part, features), wide),
            jax.ShapeDtypeStruct((part, features), wide),
        )
        grad_specs = (anywhere,) * 2
        last_vec, vec_specs, more = (jax.ShapeDtypeStruct((8, features), wide),), (in_vmem,), []
    reach = length // 2
    masked = sum((i + 1) * rows - max(0, i * rows - reach) for i in range(blocks))
    return pl.pallas_call(
        partial(att_kernel, s, heads, acc is not None, part_in is not None, is_last),
        out_shape=(shared, shared, *grads, *last_vec),
        in_specs=specs,
        out_specs=(anywhere, anywhere, *grad_specs, *vec_specs),
        scratch_shapes=[
            pltpu.VMEM((blocks, rows, features), low),
            pltpu.VMEM((blocks, rows, features), low),
            pltpu.VMEM((3 * part, features), low),
            pltpu.VMEM((part, features), low),
            pltpu.VMEM((length, features), low),
            pltpu.VMEM((length, features), low),
            pltpu.VMEM((length, features), low),
            pltpu.VMEM((part, length), low),
            pltpu.VMEM((part, length), low),
            pltpu.VMEM((part, length), low),
            pltpu.VMEM((heads, length, HEAD), low),
            pltpu.VMEM((heads, length, HEAD), low),
            pltpu.VMEM((part, length), low),
            pltpu.VMEM((masked, rows), wide),
            pltpu.VMEM((part, length), low),
            pltpu.VMEM((3 * part, length), low),
            pltpu.VMEM((part, length), wide),
            pltpu.VMEM((part, length), wide),
            pltpu.VMEM((4, rows, features), low),
            pltpu.VMEM((4, rows, features), low),
            pltpu.VMEM((3 * part, features), wide),
            pltpu.VMEM((part, features), wide),
            pltpu.SemaphoreType.DMA((8,)),
            pltpu.SemaphoreType.DMA((4,)),
            pltpu.SemaphoreType.DMA((8,)),
            *more,
        ],
        input_output_aliases=aliases,
        compiler_params=pltpu.CompilerParams(vmem_limit_bytes=50 * 2**20),
        cost_estimate=pl.CostEstimate(flops=1, bytes_accessed=1, transcendentals=0),
        name="attention",
    )(*operands)


def split_kernel(me_ref, keep, got, *refs):
    pieces, both = refs[:4], refs[4]
    r = me_ref[3]
    half = both.shape[0] // 2
    fine, short = half // 16, half // 4
    both[...] = keep[...].astype(wide) + got[...].astype(wide)
    for k, piece in enumerate(pieces):
        cut = r ^ k
        parts = [both[pl.ds(pl.multiple_of(b * 4 * fine + cut * fine, 8), fine), :] for b in range(4)]
        piece[0 : 4 * fine, :] = jnp.concatenate(parts).astype(piece.dtype)
        piece[4 * fine :, :] = both[pl.ds(pl.multiple_of(half + cut * short, 8), short), :].astype(piece.dtype)


def split_call(me, keep, got):
    shape = (keep.shape[0] // 4, keep.shape[1])
    return pl.pallas_call(
        split_kernel,
        out_shape=(jax.ShapeDtypeStruct(shape, wide),) + (jax.ShapeDtypeStruct(shape, low),) * 3,
        in_specs=[in_smem] + [in_vmem] * 2,
        out_specs=(in_vmem,) * 4,
        scratch_shapes=[pltpu.VMEM(keep.shape, wide)],
        name="split_gradients",
    )(me, keep, got)


def meet_kernel(me_ref, *refs):
    messages, (o_keep, o_near, o_far), pieces, (came, rows) = refs[:8], refs[8:11], refs[11:15], refs[15:]
    c, r = me_ref[0], me_ref[3]
    owned, features = o_keep.shape
    cols = came.shape[2]
    part, fine = cols // 3, owned // 4
    for k, message in enumerate(messages):
        came[k] = message[...].astype(wide)
    by_ctx = []
    for k in range(4):
        both = came[c ^ k] + came[4 + (c ^ k)]
        by_ctx.append(both)
        for t in range(3):
            lo = (4 * t + head_block(k)) * part
            rows[:, lo : lo + part] = both[0:owned, t * part : (t + 1) * part]
    rows[:, 3 * features :] = o_keep[...] + o_near[...].astype(wide) + o_far[...].astype(wide)
    vecs = [
        jnp.concatenate([b[owned : owned + 8, :], b[owned + 8 : owned + 16, 0 : features - cols]], axis=1)
        for b in by_ctx
    ]
    shared = (vecs[0] + vecs[1]) + (vecs[2] + vecs[3])
    vec = jnp.concatenate([shared[0:5]] + [v[5:6] for v in vecs] + [v[6:7] for v in vecs] + [shared[7:8]] * 3)
    for k, piece in enumerate(pieces):
        cut = r ^ k
        own = vec[0:4]
        for m in range(1, 4):
            own = jnp.where(cut == m, vec[4 * m : 4 * m + 4], own)
        piece[:, 0 : 4 * features] = rows[pl.ds(pl.multiple_of(cut * fine, 8), fine), :].astype(piece.dtype)
        lanes = [own[i // 6 : i // 6 + 1, i % 6 * 128 : i % 6 * 128 + 128] for i in range(24)]
        piece[:, 4 * features :] = jnp.concatenate(lanes).astype(piece.dtype)


def meet_call(me, messages, outs):
    owned, features = outs[0].shape
    assert features == 6 * 128 and owned == 96
    shape = (owned // 4, 4 * features + 128)
    return pl.pallas_call(
        meet_kernel,
        out_shape=(jax.ShapeDtypeStruct(shape, wide),) + (jax.ShapeDtypeStruct(shape, low),) * 3,
        in_specs=[in_smem] + [in_vmem] * 11,
        out_specs=(in_vmem,) * 4,
        scratch_shapes=[
            pltpu.VMEM((8, *messages[0].shape), wide),
            pltpu.VMEM((owned, 4 * features), wide),
        ],
        name="meet_gradients",
    )(me, *messages, *outs)


def spread_kernel(me_ref, p0, p1, p2, p3, b0, b1, b2, b3, rows_out, scratch):
    c, r = me_ref[0], me_ref[3]
    owned = b0.shape[0]
    fine, short = owned // 4, rows_out.shape[0] // 4
    for k, p in enumerate((p0, p1, p2, p3)):
        cut = r ^ k
        value = p[...].astype(wide)
        for b in range(4):
            scratch[b, pl.ds(pl.multiple_of(cut * fine, 8), fine), :] = value[b * fine : (b + 1) * fine]
        rows_out[pl.ds(pl.multiple_of(cut * short, 8), short), :] = value[owned:]
    for k, out in enumerate((b0, b1, b2, b3)):
        out[...] = scratch[c ^ k].astype(low)


def spread_call(me, owned, row_rows, pieces):
    features = pieces[0].shape[1]
    return pl.pallas_call(
        spread_kernel,
        out_shape=(jax.ShapeDtypeStruct((owned, features), low),) * 4
        + (jax.ShapeDtypeStruct((row_rows, features), wide),),
        in_specs=[in_smem] + [in_vmem] * 4,
        out_specs=(in_vmem,) * 5,
        scratch_shapes=[pltpu.VMEM((4, owned, features), wide)],
        name="spread_gradients",
    )(me, *pieces)


def join_ff_kernel(me_ref, b0, b1, b2, b3, out):
    c = me_ref[0]
    unit = out.shape[1] // 8
    for k, b in enumerate((b0, b1, b2, b3)):
        for t in range(2):
            lo = pl.multiple_of((4 * t + (c ^ k)) * unit, 128)
            out[:, pl.ds(lo, unit)] = b[:, t * unit : (t + 1) * unit].astype(wide)


def join_ff_call(me, blocks):
    owned, hidden = blocks[0].shape
    return pl.pallas_call(
        join_ff_kernel,
        out_shape=jax.ShapeDtypeStruct((owned, 4 * hidden), wide),
        in_specs=[in_smem] + [in_vmem] * 4,
        out_specs=in_vmem,
        name="join_fc_gradient",
    )(me, *blocks)


def join_att_kernel(me_ref, p0, p1, p2, p3, qkv_out, rows_out, *refs):
    outs, (vec, row) = refs[:8], refs[8:]
    c, f, r = me_ref[0], me_ref[1], me_ref[3]
    features, fine = rows_out.shape[1], p0.shape[0]
    part = features // 4
    for k, p in enumerate((p0, p1, p2, p3)):
        cut = r ^ k
        rows = pl.ds(pl.multiple_of(cut * fine, 8), fine)
        value = p[...].astype(wide)
        qkv_out[rows, :] = value[:, 0 : 3 * features]
        rows_out[rows, :] = value[:, 3 * features : 4 * features]
        vec[cut] = value[:, 4 * features :]

    mine = f * 4 + c
    total = [
        jnp.concatenate([vec[k // 4, k % 4 * 6 + i : k % 4 * 6 + i + 1, :] for i in range(6)], axis=1) for k in range(13)
    ]

    def choose(values, index):
        value = values[0]
        for k in range(1, len(values)):
            value = jnp.where(index == k, values[k], value)
        return value

    for i in (0, 1, 2, 3, 4, 7):
        size = outs[i].shape[0]
        source = total[min(i, 4)]
        outs[i][...] = choose([source[:, k * size : (k + 1) * size] for k in range(8)], mine).reshape(size)
    size = outs[5].shape[0]
    for k in range(4):
        for t in range(3):
            lo = (4 * t + head_block(k)) * part
            row[0:1, lo : lo + part] = total[9 + k][:, t * part : (t + 1) * part]
    outs[5][...] = choose([row[0:1, k * size : (k + 1) * size] for k in range(8)], mine).reshape(size)
    size = outs[6].shape[0]
    pieces = [total[5 + k][:, t * size : (t + 1) * size] for t in range(2) for k in range(4)]
    outs[6][...] = choose(pieces, mine).reshape(size)


def join_att_call(me, owned, features, pieces):
    sizes = (features // 8,) * 5 + (3 * features // 8, features // 2, features // 8)
    return pl.pallas_call(
        join_att_kernel,
        out_shape=(
            jax.ShapeDtypeStruct((owned, 3 * features), wide),
            jax.ShapeDtypeStruct((owned, features), wide),
        )
        + tuple(jax.ShapeDtypeStruct((n,), wide) for n in sizes),
        in_specs=[in_smem] + [in_vmem] * 4,
        out_specs=(in_vmem,) * 10,
        scratch_shapes=[pltpu.VMEM((4, owned // 4, 128), wide), pltpu.VMEM((8, 3 * features), wide)],
        name="join_qkv_gradient",
    )(me, *pieces)


def finish_kernel(seqs, x_ref, cot_ref, vecs, *refs):
    nears, overs, (out, grad) = refs[:seqs], refs[seqs : 2 * seqs], refs[2 * seqs :]
    for s, (near, over) in enumerate(zip(nears, overs)):
        x = x_ref[s].astype(wide)
        total = near[0].astype(wide) + over[0].astype(wide)
        out[s] = (x + total + vecs[4:5, :]).astype(low)
        e = near[1].astype(wide) + over[1].astype(wide)
        center = x - jnp.mean(x, axis=-1, keepdims=True)
        spread = jnp.mean(center * center, axis=-1, keepdims=True)
        root = lax.rsqrt(spread + epsilon)
        n = center * root
        back = root * (e - jnp.mean(e, axis=-1, keepdims=True) - n * jnp.mean(e * n, axis=-1, keepdims=True))
        grad[s] = (cot_ref[s].astype(wide) + back).astype(low)


def finish_call(tokens, cotangent, vecs, nears, overs):
    seqs = len(nears)
    shape = jax.ShapeDtypeStruct(tokens.shape, low)
    return pl.pallas_call(
        partial(finish_kernel, seqs),
        out_shape=(shape, shape),
        in_specs=[in_vmem] * (3 + 2 * seqs),
        out_specs=(in_vmem,) * 2,
        name="finish_tokens",
    )(tokens, cotangent, vecs, *nears, *overs)


def shards(
    tokens,
    segment,
    ln1_gain,
    ln1_bias,
    qkv_weight,
    qkv_bias,
    out_weight,
    out_bias,
    ln2_gain,
    ln2_bias,
    fc_weight,
    fc_bias,
    proj_weight,
    proj_bias,
    cotangent,
):
    ctx, fsdp, rep = lax.axis_size("ctx"), lax.axis_size("fsdp"), lax.axis_size("rep")
    c, f, r = lax.axis_index("ctx"), lax.axis_index("fsdp"), lax.axis_index("rep")
    paired = fsdp == 2 and ctx == 4 and rep == 4
    seqs, local_len, features = tokens.shape
    length = local_len * ctx
    owned = qkv_weight.shape[0]
    hidden_own = proj_weight.shape[0]
    hidden_all = fc_weight.shape[1]
    hidden = hidden_all // ctx
    part = features // ctx
    me = f * ctx + c
    core = c & 1

    half = ROT // 2
    inverse = (1.0 / np.float32(10000.0) ** (np.arange(0, ROT, 2, dtype=np.float32) / ROT)).astype(np.float32)
    angles = inverse[:, None] * np.arange(length, dtype=np.float32)[None, :]
    cosine, sine = jnp.asarray(np.cos(angles)), jnp.asarray(np.sin(angles))

    def far_rows(s, *before):
        both = jnp.stack([tokens[s], cotangent[s]])
        return swap(after(both, *before) if before else both, "ctx", 2)

    near = (swap(tokens, "ctx", 1), swap(cotangent, "ctx", 1))

    if paired:
        where = jnp.stack([c, f, core, r]).astype(jnp.int32)
        vectors = (ln1_gain, ln1_bias, ln2_gain, ln2_bias, out_bias, proj_bias, qkv_bias, fc_bias)
        proj_x = swap(proj_weight, "fsdp", 1)
        q0, q1, q2, q3, f0, f1, f2, f3 = pack_call(where, qkv_weight, fc_weight, segment, vectors)
        f_got = [swap(f1, "ctx", 1), swap(f2, "ctx", 2), swap(f3, "ctx", 3)]
        far_send = [jnp.stack([tokens[s], cotangent[s]]) for s in range(seqs)]
        f_got, far_send = lax.optimization_barrier((f_got, far_send))
        far = [swap(far_send[0], "ctx", 2)]
        f_half = rows_call(where, owned, (f0, *f_got))
        f_half, proj_x = lax.optimization_barrier((f_half, proj_x))
        f_other = swap(f_half, "fsdp", 1)
        far1 = swap(after(far_send[1], f_half), "ctx", 2)
        far[0], f_other = lax.optimization_barrier((far[0], f_other))
        far_core = [swap(far[0], "ctx", 1)]
        vecs, bias, segs = prep_call(where, owned, part, seqs, length, f_half, f_other)
        proj_pair, fc_pair = (proj_weight, proj_x), (f_half, f_other)
    else:
        zero = jnp.zeros_like(c)
        where = jnp.stack([c, zero, zero, zero]).astype(jnp.int32)

        def whole(v, axes=("fsdp", "ctx")):
            return lax.all_gather(v, axes, axis=0, tiled=True)

        far = [far_rows(s) for s in range(seqs)]
        far_core = [swap(v, "ctx", 1) for v in far]
        bias = pick(whole(qkv_bias).reshape(3, ctx, part).transpose(1, 0, 2), c).astype(wide)
        bias = jnp.broadcast_to(bias.reshape(3 * part, 1), (3 * part, 128))
        b_sum = (whole(out_bias).astype(wide) + whole(proj_bias).astype(wide)).reshape(1, features)
        vecs = [whole(v).astype(wide) for v in (ln1_gain, ln1_bias, ln2_gain, ln2_bias)]
        vecs += [b_sum.reshape(features), pick(whole(fc_bias).reshape(ctx, hidden), c).astype(wide)]
        vecs = jnp.concatenate([jnp.stack(vecs), jnp.zeros((2, features), wide)])
        segs = lax.all_gather(segment.astype(low), "ctx", axis=1, tiled=True).astype(wide)
        segs = jnp.concatenate([segs, jnp.zeros((8 - seqs, length), wide)])

        def halves(v):
            return v[: v.shape[0] // 2], v[v.shape[0] // 2 :]

        out_pair = halves(pick(whole(out_weight).reshape(ctx, part, features), c))
        proj_pair = halves(pick(whole(proj_weight).reshape(ctx, hidden, features), c))
        qkv_pair = pick(whole(qkv_weight).reshape(features, 3, ctx, part).transpose(2, 0, 1, 3), c)
        qkv_pair = halves(qkv_pair.reshape(features, 3 * part))
        fc_pair = halves(pick(whole(fc_weight).reshape(features, ctx, hidden).transpose(1, 0, 2), c))

    def run_ff(s, args, acc, part_in, is_last):
        send, keep, *grads = ff_call(s, where, args, *fc_pair, *proj_pair, vecs, acc, part_in, is_last)
        return (send, keep), grads

    def run_att(s, args, weights, acc, part_in, vec=None):
        send, keep, *grads = att_call(
            s, where, args, *weights[0], bias, *weights[1], vecs, segs, cosine, sine, acc, part_in, vec
        )
        return (send, keep), grads

    def near_rows(send, keep):
        got = swap(send, "ctx", 1)
        return [(keep[k : k + 2].astype(wide) + got[k : k + 2].astype(wide)).astype(low) for k in (0, 2)]

    def to_rep(pieces):
        return [swap(piece, "rep", k) for k, piece in zip(range(1, rep), pieces)]

    def to_ctx(pieces):
        return [swap(piece, "ctx", k) for k, piece in zip(range(1, ctx), pieces)]

    def add_up(first, others):
        total = first
        for value in others:
            total = total + value.astype(wide)
        return total.astype(low)

    phase = lax.optimization_barrier
    if paired:
        args = (tokens, cotangent, *near, far[0], far_core[0])
        far_send, q1, q2, q3, out_send, args = phase((far_send, q1, q2, q3, out_weight, args))
        q_got = [swap(q1, "ctx", 1), swap(q2, "ctx", 2), swap(q3, "ctx", 3)]
        out_x = swap(out_send, "fsdp", 1)
        part0, acc = run_ff(0, args, None, None, False)

        part0, acc, far1, q_got, far_send, out_x = phase((part0, acc, far1, q_got, far_send, out_x))
        far2 = swap(far_send[2], "ctx", 2)
        out_keep = jnp.where(core == f, out_weight, out_x)
        out_got = swap(jnp.where(core == f, out_x, out_weight), "ctx", 1)
        far1_core = swap(far1, "ctx", 1)
        part1, acc = run_ff(1, (tokens, cotangent, *near, far1, far1_core), acc, None, False)

        part1, acc, far2, q_got, out_got, out_keep = phase((part1, acc, far2, q_got, out_got, out_keep))
        q_half = rows_call(where, owned, (q0, *q_got))
        far2_core = swap(far2, "ctx", 1)
        far2_core, q_half, acc = phase((far2_core, q_half, acc))
        q_other = swap(q_half, "fsdp", 1)
        part2, ff_last = run_ff(2, (tokens, cotangent, *near, far2, far2_core), acc, None, True)

        part0, ff_last, q_other = phase((part0, ff_last, q_other))
        att_weights = ((q_half, q_other), (out_keep, out_got))
        ff_got = swap(ff_last[1], "fsdp", 1)
        args = (tokens, cotangent, *near, far[0], far_core[0])
        part0, att_acc = run_att(0, args, att_weights, None, part0)

        part0, att_acc, ff_got = phase((part0, att_acc, ff_got))
        ff_pieces = split_call(where, ff_last[0], ff_got)
        near0, away = near_rows(*part0)
        ff_pieces, near0, away, part1, att_acc = phase((ff_pieces, near0, away, part1, att_acc))
        ff_got = to_rep(ff_pieces[1:])
        over0 = swap(away, "ctx", 2)
        args = (tokens, cotangent, *near, far1, far1_core)
        part1, att_acc = run_att(1, args, att_weights, att_acc, part1)

        part1, att_acc, ff_got, over0 = phase((part1, att_acc, ff_got, over0))
        ff_total = add_up(ff_pieces[0], ff_got)
        near1, away = near_rows(*part1)
        ff_total, near1, away, part2, att_acc = phase((ff_total, near1, away, part2, att_acc))
        ff_got = to_rep([ff_total] * (rep - 1))
        over1 = swap(away, "ctx", 2)
        args = (tokens, cotangent, *near, far2, far2_core)
        part2, att_last = run_att(2, args, att_weights, att_acc, part2, ff_last[2])

        part2, att_last, ff_got, over1 = phase((part2, att_last, ff_got, over1))
        flat = [(k, i) for k in range(fsdp) for i in range(ctx)]
        messages = [att_last[0]]
        for g, h in flat[1:]:
            peers = [(k * ctx + i, (k ^ g) * ctx + (i ^ h)) for k, i in flat]
            messages.append(lax.ppermute(att_last[g * ctx + h], ("fsdp", "ctx"), peers))
        pairs = [(k, i, 1 - k, i) if (i & 1) != k else (k, i, k, i ^ 1) for k, i in flat]
        near_got = lax.ppermute(att_last[9], ("fsdp", "ctx"), [(a * ctx + b, d * ctx + e) for a, b, d, e in pairs])
        pairs = [(k * ctx + i, (1 - k) * ctx + (i ^ 1)) for k, i in flat if (i & 1) != k]
        far_got = lax.ppermute(att_last[10], ("fsdp", "ctx"), pairs)
        near2, away = near_rows(*part2)
        messages, near_got, far_got, near2, away, ff_got = phase(
            (messages, near_got, far_got, near2, away, ff_got)
        )

        pieces = meet_call(where, messages, (att_last[8], near_got, far_got))
        pieces, away = phase((pieces, away))
        got = to_rep(pieces[1:])
        over2 = swap(away, "ctx", 2)
        *ff_blocks, g_proj = spread_call(where, owned, hidden_own, (ff_total, *ff_got))
        got, over2, ff_blocks = phase((got, over2, ff_blocks))

        piece = add_up(pieces[0], got)
        piece, over2, ff_blocks = phase((piece, over2, ff_blocks))
        others = to_rep([piece] * (rep - 1))
        ff_blocks_got = to_ctx(ff_blocks[1:])
        output, grad_tokens = finish_call(tokens, cotangent, vecs, (near0, near1, near2), (over0, over1, over2))
        g_fc = join_ff_call(where, (ff_blocks[0], *ff_blocks_got))
        g_qkv, g_out, *vector_grads = join_att_call(where, owned, features, (piece, *others))
    else:
        att_acc = ff_acc = None
        nears, overs = [], []
        for s in range(seqs):
            args = (tokens, cotangent, *near, far[s], far_core[s])
            parts, ff_acc = run_ff(s, args, ff_acc, None, s == seqs - 1)
            vec = ff_acc[2] if s == seqs - 1 else None
            parts, att_acc = run_att(s, args, (qkv_pair, out_pair), att_acc, parts, vec)
            near_sum, away = near_rows(*parts)
            nears.append(near_sum)
            overs.append(swap(away, "ctx", 2))
        output, grad_tokens = finish_call(tokens, cotangent, vecs, nears, overs)

        def any_columns(kept, sent):
            grad = jnp.concatenate([kept.astype(low), sent])
            grad = lax.psum_scatter(grad, "fsdp", scatter_dimension=0, tiled=True)
            grad = lax.psum(grad, "rep").reshape(ctx, owned, -1)
            return lax.all_to_all(grad, "ctx", split_axis=0, concat_axis=0)

        def any_rows(kept, sent):
            grad = jnp.concatenate([kept.astype(low), sent])
            grad = jnp.where(jnp.arange(ctx)[:, None, None] == c, grad[None], 0).reshape(-1, features)
            return lax.psum(
                lax.psum_scatter(grad, ("fsdp", "ctx"), scatter_dimension=0, tiled=True), "rep"
            )

        cut = features // 2
        g_fc = any_columns(ff_acc[0][:cut], ff_acc[1][:cut])
        g_fc = g_fc.transpose(1, 0, 2).reshape(owned, hidden_all)
        g_proj = any_rows(ff_acc[0][cut:], ff_acc[1][cut:])
        sent = jnp.concatenate([att_acc[0][None].astype(low), jnp.stack(att_acc[1:8])])
        whole_w = jnp.concatenate(in_order([v[: part // 2] for v in sent], c))
        g_qkv = any_columns(whole_w[: features // 2], whole_w[features // 2 :]).reshape(ctx, owned, 3, part)
        g_qkv = g_qkv.transpose(1, 2, 0, 3).reshape(owned, 3 * features)
        g_out = any_rows(*att_acc[8:10])
        vec = att_acc[0][part // 2 :]
        vec = jnp.concatenate([vec[:8], vec[8:, : features - 3 * part]], axis=1)
        total_vec = jnp.zeros((16, features), wide).at[0:5].set(vec[0:5])
        total_vec = lax.dynamic_update_slice(total_vec, vec[5:6], (5 + c, 0))
        total_vec = lax.dynamic_update_slice(total_vec, vec[6:7], (9 + c, 0))
        total_vec = lax.psum(total_vec, ("ctx", "fsdp", "rep"))
        grads = [total_vec[k] for k in range(5)]
        grads.append(total_vec[9 : 9 + ctx, : 3 * part].reshape(ctx, 3, part).transpose(1, 0, 2).reshape(-1))
        grads.append(total_vec[5 : 5 + ctx, :hidden].reshape(-1))
        grads.append(total_vec[4])
        vector_grads = []
        for v in grads:
            size = v.shape[0] // (fsdp * ctx)
            vector_grads.append(lax.dynamic_slice(v, (me * size,), (size,)))
    g_gain_one, g_shift_one, g_gain_two, g_shift_two, g_b_out, g_b_qkv, g_b_fc, g_b_proj = vector_grads
    return (
        output,
        grad_tokens,
        g_gain_one,
        g_shift_one,
        g_qkv.astype(wide),
        g_b_qkv,
        g_out.astype(wide),
        g_b_out,
        g_gain_two,
        g_shift_two,
        g_fc.astype(wide),
        g_b_fc,
        g_proj.astype(wide),
        g_b_proj,
    )


def solution(mesh):
    rows, row = P(("rep", "fsdp"), "ctx", None), P(("rep", "fsdp"), "ctx")
    vector, matrix = P(("fsdp", "ctx")), P(("fsdp", "ctx"), None)
    params = (
        vector, vector, matrix, vector, matrix, vector,
        vector, vector, matrix, vector, matrix, vector,
    )
    return jax.shard_map(
        shards,
        mesh=mesh,
        in_specs=(rows, row, *params, rows),
        out_specs=(rows, rows, *params),
        check_vma=False,
    )
```

```python
from functools import partial
import math

import jax
import jax.numpy as jnp
import numpy as np
from jax import lax
from jax.experimental import pallas as pl
from jax.experimental.pallas import tpu as pltpu
from jax.sharding import PartitionSpec as P

HEADS = 12
HEAD = 64
ROT = 16

epsilon = 1e-05
far_below = -1e30
low = jnp.bfloat16
wide = jnp.float32
log2e = math.log2(math.e)


def nn(a, b):
    return lax.dot_general(a, b, (((1,), (0,)), ((), ())), preferred_element_type=wide)


def nt(a, b):
    return lax.dot_general(a, b, (((1,), (1,)), ((), ())), preferred_element_type=wide)


def swap(value, axis, bits):
    size = lax.axis_size(axis)
    return lax.ppermute(value, axis, [(i, i ^ bits) for i in range(size)])


def in_order(rel, me):
    out = []
    for k in range(len(rel)):
        value = rel[k]
        for m in range(1, len(rel)):
            value = jnp.where(me == m, rel[k ^ m], value)
        out.append(value)
    return out


def pick(stacked, index):
    return lax.dynamic_index_in_dim(stacked, index, 0, keepdims=False)


def after(value, *before):
    return lax.optimization_barrier((value, before))[0]


anywhere = pl.BlockSpec(memory_space=pltpu.HBM)
in_vmem = pl.BlockSpec(memory_space=pltpu.VMEM)
in_smem = pl.BlockSpec(memory_space=pltpu.SMEM)
extra_rows = 16


def head_block(index):
    return ((index & 1) << 1) | (index >> 1)


def pack_kernel(vectors, me_ref, qkv, fc, segment, *refs):
    vector_refs, refs = refs[:vectors], refs[vectors:]
    q0, q1, q2, q3, f0, f1, f2, f3, scratch, extra = refs
    c = me_ref[0]
    owned, part, unit = qkv.shape[0], qkv.shape[1] // 12, fc.shape[1] // 8
    extra[...] = jnp.zeros_like(extra)
    for row, ref in enumerate(vector_refs):
        extra[row : row + 1, 0 : ref.shape[0]] = ref[...].astype(wide).reshape(1, -1)
    extra[8 : 8 + segment.shape[0], 0 : segment.shape[1]] = segment[...].astype(wide)
    for k in range(4):
        block = head_block(k)
        for t in range(3):
            lo = (4 * t + block) * part
            scratch[k ^ c, :, t * part : (t + 1) * part] = qkv[:, lo : lo + part]
    for k, (q, g) in enumerate(((q0, f0), (q1, f1), (q2, f2), (q3, f3))):
        q[...] = scratch[k]
        for t in range(2):
            lo = pl.multiple_of((4 * t + (c ^ k)) * unit, 128)
            g[0:owned, t * unit : (t + 1) * unit] = fc[:, pl.ds(lo, unit)]
        g[owned:, :] = extra[...].astype(low)


def pack_call(me, qkv, fc, segment, vectors):
    owned = qkv.shape[0]
    narrow, broad = (owned, qkv.shape[1] // 4), (owned + extra_rows, fc.shape[1] // 4)
    shapes = (narrow,) * 4 + (broad,) * 4
    return pl.pallas_call(
        partial(pack_kernel, len(vectors)),
        out_shape=tuple(jax.ShapeDtypeStruct(s, low) for s in shapes),
        in_specs=[in_smem] + [in_vmem] * (3 + len(vectors)),
        out_specs=(in_vmem,) * 8,
        scratch_shapes=[
            pltpu.VMEM((4, owned, narrow[1]), low),
            pltpu.VMEM((extra_rows, broad[1]), wide),
        ],
        name="pack_columns",
    )(me, qkv, fc, segment, *vectors)


def rows_kernel(owned, me_ref, p0, p1, p2, p3, half):
    c = me_ref[0]
    tail = p0.shape[0] - owned
    for k, p in enumerate((p0, p1, p2, p3)):
        half[pl.ds(pl.multiple_of((c ^ k) * owned, 16), owned), :] = p[0:owned, :]
        if tail:
            half[pl.ds(pl.multiple_of(4 * owned + (c ^ k) * tail, 16), tail), :] = p[owned:, :]


def rows_call(me, owned, pieces):
    rows, cols = pieces[0].shape
    return pl.pallas_call(
        partial(rows_kernel, owned),
        out_shape=jax.ShapeDtypeStruct((4 * rows, cols), low),
        in_specs=[in_smem] + [in_vmem] * 4,
        out_specs=in_vmem,
        name="rows_by_ctx",
    )(me, *pieces)


def prep_kernel(owned, part, seqs, me_ref, mine, other, vecs, bias, seg):
    c, f = me_ref[0], me_ref[1]
    extra_mine, extra_other = mine[...].astype(wide), other[...].astype(wide)
    first = jnp.where(f == 0, extra_mine, extra_other)
    last = jnp.where(f == 0, extra_other, extra_mine)

    def vector(row, size):
        pieces = [
            e[k * extra_rows + row : k * extra_rows + row + 1, 0:size]
            for e in (first, last)
            for k in range(4)
        ]
        return jnp.concatenate(pieces, axis=1)

    block = head_block(c)
    vecs[...] = jnp.zeros_like(vecs)
    for row in range(4):
        vecs[row : row + 1, :] = vector(row, owned)
    vecs[4:5, :] = vector(4, owned) + vector(5, owned)
    unit = mine.shape[1] // 2
    for t, e in enumerate((first, last)):
        chosen = e[7:8, 0:unit]
        for k in range(1, 4):
            chosen = jnp.where(c == k, e[k * extra_rows + 7 : k * extra_rows + 8, 0:unit], chosen)
        vecs[5:6, t * unit : (t + 1) * unit] = chosen
    all_qkv = vector(6, 3 * owned)
    picked = []
    for t in range(3):
        chosen = all_qkv[:, 4 * t * part : (4 * t + 1) * part]
        for k in range(1, 4):
            chosen = jnp.where(block == k, all_qkv[:, (4 * t + k) * part : (4 * t + k + 1) * part], chosen)
        picked.append(chosen)
    row_bias = jnp.concatenate(picked, axis=1)
    bias[...] = jnp.transpose(jnp.broadcast_to(row_bias, (128, 3 * part)))
    seg[...] = jnp.zeros_like(seg)
    width = seg.shape[1] // 4
    for s in range(seqs):
        for k in range(4):
            row = k * extra_rows + 8 + s
            seg[s : s + 1, k * width : (k + 1) * width] = extra_mine[row : row + 1, 0:width]


def prep_call(me, owned, part, seqs, length, mine, other):
    tail = pl.BlockSpec((4 * extra_rows, mine.shape[1]), lambda i: (4 * owned // (4 * extra_rows), 0))
    assert 4 * owned % (4 * extra_rows) == 0
    shapes = ((8, 8 * owned), (3 * part, 128), (8, length))
    return pl.pallas_call(
        partial(prep_kernel, owned, part, seqs),
        grid=(1,),
        out_shape=tuple(jax.ShapeDtypeStruct(s, wide) for s in shapes),
        in_specs=[in_smem, tail, tail],
        out_specs=tuple(pl.BlockSpec(s, lambda i: (0, 0)) for s in shapes),
        name="prepare_vectors",
    )(me, mine, other)


def row_norm(block):
    values = block.astype(wide)
    center = values - jnp.mean(values, axis=-1, keepdims=True)
    spread = jnp.mean(center * center, axis=-1, keepdims=True)
    return center * lax.rsqrt(spread + epsilon)


def gelu_parts(v):
    bell = jnp.exp2(v * v * (-0.5 * log2e))
    base = 1.0 + (0.3275911 / math.sqrt(2.0)) * jnp.abs(v)
    t = pl.reciprocal(base, approx=True)
    t = t * (2.0 - base * t)
    poly = 0.5 * 1.061405429
    for coef in (-1.453152027, 1.421413741, -0.284496736, 0.254829592):
        poly = poly * t + 0.5 * coef
    tail = poly * t * bell
    phi = jnp.where(v >= 0, 1.0 - tail, tail)
    return phi, phi + v * bell * (1.0 / math.sqrt(2.0 * math.pi))


def bring(pairs, sem):
    copies = [pltpu.make_async_copy(a, b, sem.at[k]) for k, (a, b) in enumerate(pairs)]
    for copy in copies:
        copy.start()
    return copies


def token_pairs(s, refs, xs, cs):
    tok, cot, tok1, cot1, far, far1 = refs
    pairs = []
    for j, (t, c) in enumerate(
        ((tok.at[s], cot.at[s]), (tok1.at[s], cot1.at[s]), (far.at[0], far.at[1]), (far1.at[0], far1.at[1]))
    ):
        pairs += [(t, xs.at[j]), (c, cs.at[j])]
    return pairs


def ff_kernel(s, with_acc, with_part, is_last, *refs):
    me_ref, refs = refs[0], refs[1:]
    token_refs, refs = refs[:6], refs[6:]
    fc_a, fc_b, proj_a, proj_b, vecs = refs[:5]
    refs = refs[5:]
    if with_acc:
        acc_fc_in, acc_proj_in, acc_vec_in = refs[:3]
        refs = refs[3:]
    if with_part:
        part_send, part_keep = refs[:2]
        refs = refs[2:]
    send, keep = refs[:2]
    refs = refs[2:]
    if is_last:
        grad_keep, grad_send, vec = refs[:3]
        refs = refs[3:]
    else:
        fc_out, proj_out, vec = refs[:3]
        refs = refs[3:]
    xs, cs, fc, proj, sec_s, hid_s, gp_s, send_s, keep_s, acc_fc, acc_proj, sem, sem_w, sem_p, sem_o = refs[:15]
    if is_last:
        stage_keep, stage_send = refs[15:]
    f = me_ref[1]
    blocks, rows, features = xs.shape
    hidden = fc.shape[1]
    third, half = features // 2, proj_a.shape[0]
    tokens_in = bring(token_pairs(s, token_refs, xs, cs), sem)
    weights_in = bring(
        [
            (fc_a.at[0:third], fc.at[pl.ds(pl.multiple_of(f * third, 16), third), :]),
            (fc_b.at[0:third], fc.at[pl.ds(pl.multiple_of((1 - f) * third, 16), third), :]),
            (proj_a, proj.at[pl.ds(pl.multiple_of(f * half, 16), half), :]),
            (proj_b, proj.at[pl.ds(pl.multiple_of((1 - f) * half, 16), half), :]),
        ],
        sem_w,
    )
    later = []
    if with_part:
        later += [(part_send, send_s), (part_keep, keep_s)]
    if with_acc:
        later += [(acc_fc_in, acc_fc), (acc_proj_in, acc_proj)]
    later = bring(later, sem_p)
    for copy in weights_in + tokens_in:
        copy.wait()
    gain, shift, bias = vecs[2:3, :], vecs[3:4, :], vecs[5:6, 0:hidden]
    dgain = jnp.zeros((1, features), wide)
    dshift = jnp.zeros((1, features), wide)
    dbias = jnp.zeros((1, hidden), wide)
    if with_part:
        later[0].wait()
        later[1].wait()
    for j in range(blocks):
        here = pl.ds(j * rows, rows)
        n = row_norm(xs[j])
        second = (n * gain + shift).astype(low)
        sec_s[here, :] = second
        cot = cs[j]
        pre = nn(second, fc[...]) + bias
        phi, slope = gelu_parts(pre)
        hid = (pre * phi).astype(low)
        gp = nt(cot, proj[...]) * slope
        dbias = dbias + jnp.sum(gp, axis=0, keepdims=True)
        gp = gp.astype(low)
        hid_s[here, :] = hid
        gp_s[here, :] = gp
        out = nn(hid, proj[...])
        dsec = nt(gp, fc[...])
        dgain = dgain + jnp.sum(dsec * n, axis=0, keepdims=True)
        dshift = dshift + jnp.sum(dsec, axis=0, keepdims=True)
        e = dsec * gain
        to = send_s if j % 2 else keep_s
        if with_part:
            out = out + to[j // 2 * 2].astype(wide)
            e = e + to[j // 2 * 2 + 1].astype(wide)
        to[j // 2 * 2] = out.astype(low)
        to[j // 2 * 2 + 1] = e.astype(low)
    results = bring([(send_s, send), (keep_s, keep)], sem_o)
    dcot = jnp.sum(cs[0].astype(wide), axis=0, keepdims=True)
    if with_acc:
        for copy in later[-2:]:
            copy.wait()
        dgain = dgain + acc_vec_in[0:1, :]
        dshift = dshift + acc_vec_in[1:2, :]
        dbias = dbias + acc_vec_in[2:3, 0:hidden]
        dcot = dcot + acc_vec_in[3:4, :]
    every_cot = cs[...].reshape(blocks * rows, features)
    for k, (acc, a, b, own) in enumerate(((acc_fc, sec_s, gp_s[...], third), (acc_proj, hid_s, every_cot, half))):
        grad = nn(jnp.transpose(a[...]), b)
        acc[...] = grad + acc[...] if with_acc else grad
        if is_last:
            lo = k * third
            stage_keep[lo : lo + own, :] = acc[pl.ds(pl.multiple_of(f * own, 16), own), :].astype(low)
            stage_send[lo : lo + own, :] = acc[pl.ds(pl.multiple_of((1 - f) * own, 16), own), :].astype(low)
            moves = [(stage_keep, grad_keep), (stage_send, grad_send)]
            moves = [(x.at[lo : lo + own], y.at[lo : lo + own]) for x, y in moves]
        else:
            moves = [(acc, (fc_out, proj_out)[k])]
        for x, y in moves:
            results.append(pltpu.make_async_copy(x, y, sem_o.at[len(results)]))
            results[-1].start()
    vec[0:1, :] = dgain
    vec[1:2, :] = dshift
    vec[2:3, 0:hidden] = dbias
    vec[3:4, :] = dcot
    for copy in results:
        copy.wait()


def ff_call(s, me, token_args, fc_a, fc_b, proj_a, proj_b, vecs, acc, part, is_last):
    rows, features = token_args[0].shape[1:]
    hidden, blocks = fc_a.shape[1], 4
    total = blocks * rows
    third = features // 2
    operands = [me, *token_args, fc_a, fc_b, proj_a, proj_b, vecs]
    specs = [in_smem] + [anywhere] * 10 + [in_vmem]
    aliases = {}
    if acc is not None:
        if not is_last:
            aliases = {len(operands): 2, len(operands) + 1: 3}
        operands += list(acc)
        specs += [anywhere, anywhere, in_vmem]
    if part is not None:
        aliases[len(operands)] = 0
        aliases[len(operands) + 1] = 1
        operands += list(part)
        specs += [anywhere, anywhere]
    shared = jax.ShapeDtypeStruct((4, rows, features), low)
    vec = jax.ShapeDtypeStruct((8, features), wide)
    if is_last:
        rows_out = third + proj_a.shape[0]
        grads = (
            jax.ShapeDtypeStruct((rows_out, features), low),
            jax.ShapeDtypeStruct((rows_out, features), low),
        )
        grad_specs = (anywhere,) * 2
        more = [pltpu.VMEM((rows_out, features), low)] * 2
    else:
        grads = (
            jax.ShapeDtypeStruct((features, hidden), wide),
            jax.ShapeDtypeStruct((hidden, features), wide),
        )
        grad_specs, more = (anywhere,) * 2, []
    return pl.pallas_call(
        partial(ff_kernel, s, acc is not None, part is not None, is_last),
        out_shape=(shared, shared, *grads, vec),
        in_specs=specs,
        out_specs=(anywhere, anywhere, *grad_specs, in_vmem),
        scratch_shapes=[
            pltpu.VMEM((blocks, rows, features), low),
            pltpu.VMEM((blocks, rows, features), low),
            pltpu.VMEM((features, hidden), low),
            pltpu.VMEM((hidden, features), low),
            pltpu.VMEM((total, features), low),
            pltpu.VMEM((total, hidden), low),
            pltpu.VMEM((total, hidden), low),
            pltpu.VMEM((4, rows, features), low),
            pltpu.VMEM((4, rows, features), low),
            pltpu.VMEM((features, hidden), wide),
            pltpu.VMEM((hidden, features), wide),
            pltpu.SemaphoreType.DMA((8,)),
            pltpu.SemaphoreType.DMA((4,)),
            pltpu.SemaphoreType.DMA((4,)),
            pltpu.SemaphoreType.DMA((8,)),
            *more,
        ],
        input_output_aliases=aliases,
        compiler_params=pltpu.CompilerParams(vmem_limit_bytes=50 * 2**20),
        cost_estimate=pl.CostEstimate(flops=1, bytes_accessed=1, transcendentals=0),
        name="feed_forward",
    )(*operands)


def turn(block, cosine, sine):
    half = ROT // 2
    a, b = block[0:half], block[half:ROT]
    return jnp.concatenate([a * cosine - b * sine, b * cosine + a * sine, block[ROT:]], axis=0)


def att_kernel(s, heads, with_acc, with_part, is_last, *refs):
    me_ref, refs = refs[0], refs[1:]
    token_refs, refs = refs[:6], refs[6:]
    w_a, w_b, bias, wout_a, wout_b, vecs, segs, cosine, sine = refs[:9]
    refs = refs[9:]
    if is_last:
        ff_vec, refs = refs[0], refs[1:]
    if with_acc:
        acc_w_in, acc_o_in, acc_vec_in = refs[:3]
        refs = refs[3:]
    if with_part:
        part_send, part_keep = refs[:2]
        refs = refs[2:]
    homes, refs = refs[:4], refs[4:]
    if is_last:
        messages, (o_keep, o_send, o_send_far) = refs[:8], refs[8:11]
        refs = refs[11:]
    else:
        w_out, o_out, vec = refs[:3]
        refs = refs[3:]
    xs, cs, wt_s, wout, first_s, n_s, cot_s, qt_s, kt_s, vt_s, k_s, v_s, dot_s, mask_s, att_s, d_s, dk_s, dv_s = refs[:18]
    send_s, keep_s, acc_w, acc_o, sem, sem_p, sem_o = refs[18:25]
    if is_last:
        by_rows = refs[25]
    me, f, core = me_ref[0], me_ref[1], me_ref[2]
    blocks, rows, features = xs.shape
    part = heads * HEAD
    length = blocks * rows
    reach = length // 2
    scale = 1.0 / math.sqrt(HEAD)
    tokens_in = bring(token_pairs(s, token_refs, xs, cs), sem)
    gain, shift = vecs[0:1, :], vecs[1:2, :]
    share = w_a.shape[0]
    wt_s[:, pl.ds(pl.multiple_of(f * share, 128), share)] = jnp.transpose(w_a[...])
    wt_s[:, pl.ds(pl.multiple_of((1 - f) * share, 128), share)] = jnp.transpose(w_b[...])
    owned = wout_a.shape[0]
    wout[pl.ds(pl.multiple_of(core * owned, 16), owned), :] = wout_a[...]
    wout[pl.ds(pl.multiple_of((1 - core) * owned, 16), owned), :] = wout_b[...]

    seg_row = segs[s : s + 1, :]
    seg_col = jnp.transpose(jnp.broadcast_to(seg_row, (128, length)))
    spans, place = [], 0
    for i in range(blocks):
        start = max(0, i * rows - reach)
        count = (i + 1) * rows - start
        spans.append((start, count, place))
        ours = seg_row[:, i * rows : (i + 1) * rows]
        theirs = seg_col[start : start + count]
        theirs = jnp.concatenate([theirs] * (rows // 128), axis=1)
        key = start + lax.broadcasted_iota(jnp.int32, (count, rows), 0)
        query = i * rows + lax.broadcasted_iota(jnp.int32, (count, rows), 1)
        allowed = (theirs == ours) & (key <= query)
        mask_s[place : place + count, :] = jnp.where(allowed, 0.0, far_below)
        place += count

    for copy in tokens_in:
        copy.wait()
    wide_bias = jnp.concatenate([bias[...]] * (rows // 128), axis=1)
    for j in range(blocks):
        off = pl.multiple_of((me ^ j) * rows, rows)
        n = row_norm(xs[j])
        n_s[pl.ds(off, rows), :] = n.astype(low)
        first = (n * gain + shift).astype(low)
        first_s[pl.ds(off, rows), :] = first
        cot = cs[j]
        cot_s[pl.ds(off, rows), :] = cot
        cos_b, sin_b = cosine[:, pl.ds(off, rows)], sine[:, pl.ds(off, rows)]
        made = nt(wt_s[...], first) + wide_bias
        for h in range(heads):
            lo, hi = h * HEAD, (h + 1) * HEAD
            query = turn(made[lo:hi], cos_b, sin_b).astype(low)
            qt_s[lo:hi, pl.ds(off, rows)] = (query.astype(wide) * scale).astype(low)
            key = turn(made[part + lo : part + hi], cos_b, sin_b).astype(low)
            kt_s[lo:hi, pl.ds(off, rows)] = key
            value = made[2 * part + lo : 2 * part + hi].astype(low)
            vt_s[lo:hi, pl.ds(off, rows)] = value
            k_s[h, pl.ds(off, rows), :] = jnp.transpose(key)
            v_s[h, pl.ds(off, rows), :] = jnp.transpose(value)
        dot_s[:, pl.ds(off, rows)] = nt(wout[...], cot).astype(low)

    later = []
    if with_part:
        later += [(part_send, send_s), (part_keep, keep_s)]
    if with_acc:
        later += [(acc_w_in, acc_w), (acc_o_in, acc_o)]
    later = bring(later, sem_p)
    dk_s[...] = jnp.zeros_like(dk_s)
    dv_s[...] = jnp.zeros_like(dv_s)

    def one_head(h, carry):
        base = pl.multiple_of(h * HEAD, HEAD)
        mine = pl.ds(base, HEAD)
        for i in range(blocks):
            start, count, place = spans[i]
            here, there = slice(i * rows, (i + 1) * rows), slice(start, start + count)
            query, grad = qt_s[mine, here], dot_s[mine, here]
            score = nn(k_s[h, there, :], query) + mask_s[place : place + count, :]
            top = jnp.max(score, axis=0, keepdims=True)
            lifted = jnp.exp2((score - top) * log2e)
            total = jnp.sum(lifted, axis=0, keepdims=True)
            prob = lifted * (1.0 / total)
            prob_low = prob.astype(low)
            att_s[mine, here] = nn(vt_s[mine, there], prob_low).astype(low)
            dprob = nn(v_s[h, there, :], grad)
            inner = jnp.sum(prob * dprob, axis=0, keepdims=True)
            dscore = (prob * (dprob - inner)).astype(low)
            dv_s[mine, there] += nt(grad, prob_low)
            dk_s[mine, there] += nt(query, dscore)
            dq = nn(kt_s[mine, there], dscore) * scale
            cos_b, sin_b = cosine[:, here], sine[:, here]
            d_s[mine, here] = turn(dq, cos_b, -sin_b).astype(low)
        return carry

    lax.fori_loop(0, heads, one_head, 0)
    for h in range(heads):
        lo, hi = h * HEAD, (h + 1) * HEAD
        d_s[part + lo : part + hi, :] = turn(dk_s[lo:hi, :], cosine[...], -sine[...]).astype(low)
    d_s[2 * part : 3 * part, :] = dv_s[...].astype(low)

    g_w = nn(d_s[...], first_s[...])
    g_o = nn(att_s[...], cot_s[...])
    if with_part:
        later[0].wait()
        later[1].wait()
    if with_acc:
        later[-2].wait()
        later[-1].wait()
        g_w = g_w + acc_w[...]
        g_o = g_o + acc_o[...]
    acc_w[...] = g_w
    results = []
    if is_last:
        by_rows[...] = jnp.transpose(acc_w[...])
        for k, message in enumerate(messages):
            shard = (f ^ (k // 4)) * 4 + (me ^ (k % 4))
            block = by_rows[pl.ds(pl.multiple_of(shard * owned, 8), owned), :]
            message[0:owned, :] = block.astype(message.dtype)
        acc_o[...] = g_o
        mine = acc_o[pl.ds(pl.multiple_of(f * owned, 16), owned), :]
        o_keep[...] = jnp.where(f == core, mine, 0.0)
        o_send[...] = acc_o[pl.ds(pl.multiple_of((1 - f) * owned, 16), owned), :].astype(low)
        o_send_far[...] = mine.astype(low)
    else:
        acc_o[...] = g_o
        results = [
            pltpu.make_async_copy(acc_w, w_out, sem_o.at[2]),
            pltpu.make_async_copy(acc_o, o_out, sem_o.at[3]),
        ]
        for copy in results:
            copy.start()
    dgain = jnp.zeros((1, features), wide)
    dshift = jnp.zeros((1, features), wide)
    dbias = jnp.zeros((8, 3 * part), wide)
    for j in range(blocks):
        off = pl.multiple_of((me ^ j) * rows, rows)
        att = jnp.transpose(att_s[:, pl.ds(off, rows)])
        out = nn(att, wout[...])
        dqkv = jnp.transpose(d_s[:, pl.ds(off, rows)])
        dbias = dbias + nn(jnp.ones((8, rows), low), dqkv)
        dfirst = nn(dqkv, wt_s[...])
        n = n_s[pl.ds(off, rows), :].astype(wide)
        dgain = dgain + jnp.sum(dfirst * n, axis=0, keepdims=True)
        dshift = dshift + jnp.sum(dfirst, axis=0, keepdims=True)
        e = dfirst * gain
        to, first = send_s if j % 2 else keep_s, j // 2 * 2
        if with_part:
            out = out + to[first].astype(wide)
            e = e + to[first + 1].astype(wide)
        to[first] = out.astype(low)
        to[first + 1] = e.astype(low)
        if j % 2:
            for k, (a, b) in enumerate(((send_s, homes[first]), (keep_s, homes[first + 1]))):
                results.append(pltpu.make_async_copy(a.at[first : first + 2], b, sem_o.at[4 + first + k]))
                results[-1].start()
    dbias = dbias[0:1]
    if with_acc:
        dgain = dgain + acc_vec_in[0:1, :]
        dshift = dshift + acc_vec_in[1:2, :]
        dbias = dbias + acc_vec_in[2:3, 0 : 3 * part]
    if is_last:
        cols = 3 * part
        rest = jnp.zeros((1, features - cols), wide)
        vec = jnp.concatenate(
            [dgain, dshift, ff_vec[0:2, :], ff_vec[3:4, :], ff_vec[2:3, :], jnp.concatenate([dbias, rest], axis=1)]
            + [jnp.zeros((1, features), wide)]
        )
        for message in messages:
            message[owned : owned + 8, :] = vec[:, 0:cols].astype(message.dtype)
            message[owned + 8 : owned + 16, 0 : features - cols] = vec[:, cols:].astype(message.dtype)
            message[owned + 8 : owned + 16, features - cols :] = jnp.zeros((8, 2 * cols - features), message.dtype)
    else:
        vec[0:1, :] = dgain
        vec[1:2, :] = dshift
        vec[2:3, 0 : 3 * part] = dbias
    for copy in results:
        copy.wait()


def att_call(s, me, token_args, w_a, w_b, bias, wout_a, wout_b, vecs, segs, cosine, sine, acc, part_in, ff_vec):
    rows, features = token_args[0].shape[1:]
    part, blocks = w_a.shape[1] // 3, 4
    heads = part // HEAD
    length = blocks * rows
    is_last = ff_vec is not None
    operands = [me, *token_args, w_a, w_b, bias, wout_a, wout_b, vecs, segs, cosine, sine]
    operands += [ff_vec] if is_last else []
    specs = [in_smem] + [anywhere] * 6 + [in_vmem] * (len(operands) - 7)
    aliases = {}
    if acc is not None:
        if not is_last:
            aliases = {len(operands): 4, len(operands) + 1: 5}
        operands += list(acc)
        specs += [anywhere, anywhere, in_vmem]
    if part_in is not None:
        operands += list(part_in)
        specs += [anywhere, anywhere]
    shared = jax.ShapeDtypeStruct((2, rows, features), low)
    if is_last:
        message = (part // 2 + 16, 3 * part)
        grads = (jax.ShapeDtypeStruct(message, wide),) + (jax.ShapeDtypeStruct(message, low),) * 7
        grads += (
            jax.ShapeDtypeStruct((part // 2, features), wide),
            jax.ShapeDtypeStruct((part // 2, features), low),
            jax.ShapeDtypeStruct((part // 2, features), low),
        )
        grad_specs = (in_vmem,) * 11
        last_vec, vec_specs = (), ()
        more = [pltpu.VMEM((features, 3 * part), wide)]
    else:
        grads = (
            jax.ShapeDtypeStruct((3 * part, features), wide),
            jax.ShapeDtypeStruct((part, features), wide),
        )
        grad_specs = (anywhere,) * 2
        last_vec, vec_specs, more = (jax.ShapeDtypeStruct((8, features), wide),), (in_vmem,), []
    reach = length // 2
    masked = sum((i + 1) * rows - max(0, i * rows - reach) for i in range(blocks))
    return pl.pallas_call(
        partial(att_kernel, s, heads, acc is not None, part_in is not None, is_last),
        out_shape=(shared,) * 4 + (*grads, *last_vec),
        in_specs=specs,
        out_specs=(anywhere,) * 4 + (*grad_specs, *vec_specs),
        scratch_shapes=[
            pltpu.VMEM((blocks, rows, features), low),
            pltpu.VMEM((blocks, rows, features), low),
            pltpu.VMEM((3 * part, features), low),
            pltpu.VMEM((part, features), low),
            pltpu.VMEM((length, features), low),
            pltpu.VMEM((length, features), low),
            pltpu.VMEM((length, features), low),
            pltpu.VMEM((part, length), low),
            pltpu.VMEM((part, length), low),
            pltpu.VMEM((part, length), low),
            pltpu.VMEM((heads, length, HEAD), low),
            pltpu.VMEM((heads, length, HEAD), low),
            pltpu.VMEM((part, length), low),
            pltpu.VMEM((masked, rows), wide),
            pltpu.VMEM((part, length), low),
            pltpu.VMEM((3 * part, length), low),
            pltpu.VMEM((part, length), wide),
            pltpu.VMEM((part, length), wide),
            pltpu.VMEM((4, rows, features), low),
            pltpu.VMEM((4, rows, features), low),
            pltpu.VMEM((3 * part, features), wide),
            pltpu.VMEM((part, features), wide),
            pltpu.SemaphoreType.DMA((8,)),
            pltpu.SemaphoreType.DMA((4,)),
            pltpu.SemaphoreType.DMA((8,)),
            *more,
        ],
        input_output_aliases=aliases,
        compiler_params=pltpu.CompilerParams(vmem_limit_bytes=50 * 2**20),
        cost_estimate=pl.CostEstimate(flops=1, bytes_accessed=1, transcendentals=0),
        name="attention",
    )(*operands)


def split_kernel(me_ref, keep, got, *refs):
    pieces, both = refs[:4], refs[4]
    r = me_ref[3]
    half = both.shape[0] // 2
    fine, short = half // 16, half // 4
    both[...] = keep[...].astype(wide) + got[...].astype(wide)
    for k, piece in enumerate(pieces):
        cut = r ^ k
        parts = [both[pl.ds(pl.multiple_of(b * 4 * fine + cut * fine, 8), fine), :] for b in range(4)]
        piece[0 : 4 * fine, :] = jnp.concatenate(parts).astype(piece.dtype)
        piece[4 * fine :, :] = both[pl.ds(pl.multiple_of(half + cut * short, 8), short), :].astype(piece.dtype)


def split_call(me, keep, got):
    shape = (keep.shape[0] // 4, keep.shape[1])
    return pl.pallas_call(
        split_kernel,
        out_shape=(jax.ShapeDtypeStruct(shape, wide),) + (jax.ShapeDtypeStruct(shape, low),) * 3,
        in_specs=[in_smem] + [in_vmem] * 2,
        out_specs=(in_vmem,) * 4,
        scratch_shapes=[pltpu.VMEM(keep.shape, wide)],
        name="split_gradients",
    )(me, keep, got)


def meet_kernel(me_ref, *refs):
    messages, (o_keep, o_near, o_far), pieces, (came, rows) = refs[:8], refs[8:11], refs[11:15], refs[15:]
    c, r = me_ref[0], me_ref[3]
    owned, features = o_keep.shape
    cols = came.shape[2]
    part, fine = cols // 3, owned // 4
    for k, message in enumerate(messages):
        came[k] = message[...].astype(wide)
    by_ctx = []
    for k in range(4):
        both = came[c ^ k] + came[4 + (c ^ k)]
        by_ctx.append(both)
        for t in range(3):
            lo = (4 * t + head_block(k)) * part
            rows[:, lo : lo + part] = both[0:owned, t * part : (t + 1) * part]
    rows[:, 3 * features :] = o_keep[...] + o_near[...].astype(wide) + o_far[...].astype(wide)
    vecs = [
        jnp.concatenate([b[owned : owned + 8, :], b[owned + 8 : owned + 16, 0 : features - cols]], axis=1)
        for b in by_ctx
    ]
    shared = (vecs[0] + vecs[1]) + (vecs[2] + vecs[3])
    vec = jnp.concatenate([shared[0:5]] + [v[5:6] for v in vecs] + [v[6:7] for v in vecs] + [shared[7:8]] * 3)
    for k, piece in enumerate(pieces):
        cut = r ^ k
        own = vec[0:4]
        for m in range(1, 4):
            own = jnp.where(cut == m, vec[4 * m : 4 * m + 4], own)
        piece[:, 0 : 4 * features] = rows[pl.ds(pl.multiple_of(cut * fine, 8), fine), :].astype(piece.dtype)
        lanes = [own[i // 6 : i // 6 + 1, i % 6 * 128 : i % 6 * 128 + 128] for i in range(24)]
        piece[:, 4 * features :] = jnp.concatenate(lanes).astype(piece.dtype)


def meet_call(me, messages, outs):
    owned, features = outs[0].shape
    assert features == 6 * 128 and owned == 96
    shape = (owned // 4, 4 * features + 128)
    return pl.pallas_call(
        meet_kernel,
        out_shape=(jax.ShapeDtypeStruct(shape, wide),) + (jax.ShapeDtypeStruct(shape, low),) * 3,
        in_specs=[in_smem] + [in_vmem] * 11,
        out_specs=(in_vmem,) * 4,
        scratch_shapes=[
            pltpu.VMEM((8, *messages[0].shape), wide),
            pltpu.VMEM((owned, 4 * features), wide),
        ],
        name="meet_gradients",
    )(me, *messages, *outs)


def spread_kernel(me_ref, p0, p1, p2, p3, b0, b1, b2, b3, rows_out, scratch):
    c, r = me_ref[0], me_ref[3]
    owned = b0.shape[0]
    fine, short = owned // 4, rows_out.shape[0] // 4
    for k, p in enumerate((p0, p1, p2, p3)):
        cut = r ^ k
        value = p[...].astype(wide)
        for b in range(4):
            scratch[b, pl.ds(pl.multiple_of(cut * fine, 8), fine), :] = value[b * fine : (b + 1) * fine]
        rows_out[pl.ds(pl.multiple_of(cut * short, 8), short), :] = value[owned:]
    for k, out in enumerate((b0, b1, b2, b3)):
        out[...] = scratch[c ^ k].astype(low)


def spread_call(me, owned, row_rows, pieces):
    features = pieces[0].shape[1]
    return pl.pallas_call(
        spread_kernel,
        out_shape=(jax.ShapeDtypeStruct((owned, features), low),) * 4
        + (jax.ShapeDtypeStruct((row_rows, features), wide),),
        in_specs=[in_smem] + [in_vmem] * 4,
        out_specs=(in_vmem,) * 5,
        scratch_shapes=[pltpu.VMEM((4, owned, features), wide)],
        name="spread_gradients",
    )(me, *pieces)


def join_ff_kernel(me_ref, b0, b1, b2, b3, out):
    c = me_ref[0]
    unit = out.shape[1] // 8
    for k, b in enumerate((b0, b1, b2, b3)):
        for t in range(2):
            lo = pl.multiple_of((4 * t + (c ^ k)) * unit, 128)
            out[:, pl.ds(lo, unit)] = b[:, t * unit : (t + 1) * unit].astype(wide)


def join_ff_call(me, blocks):
    owned, hidden = blocks[0].shape
    return pl.pallas_call(
        join_ff_kernel,
        out_shape=jax.ShapeDtypeStruct((owned, 4 * hidden), wide),
        in_specs=[in_smem] + [in_vmem] * 4,
        out_specs=in_vmem,
        name="join_fc_gradient",
    )(me, *blocks)


def join_att_kernel(me_ref, p0, p1, p2, p3, qkv_out, rows_out, *refs):
    outs, (vec, row) = refs[:8], refs[8:]
    c, f, r = me_ref[0], me_ref[1], me_ref[3]
    features, fine = rows_out.shape[1], p0.shape[0]
    part = features // 4
    for k, p in enumerate((p0, p1, p2, p3)):
        cut = r ^ k
        rows = pl.ds(pl.multiple_of(cut * fine, 8), fine)
        value = p[...].astype(wide)
        qkv_out[rows, :] = value[:, 0 : 3 * features]
        rows_out[rows, :] = value[:, 3 * features : 4 * features]
        vec[cut] = value[:, 4 * features :]

    mine = f * 4 + c
    total = [
        jnp.concatenate([vec[k // 4, k % 4 * 6 + i : k % 4 * 6 + i + 1, :] for i in range(6)], axis=1) for k in range(13)
    ]

    def choose(values, index):
        value = values[0]
        for k in range(1, len(values)):
            value = jnp.where(index == k, values[k], value)
        return value

    for i in (0, 1, 2, 3, 4, 7):
        size = outs[i].shape[0]
        source = total[min(i, 4)]
        outs[i][...] = choose([source[:, k * size : (k + 1) * size] for k in range(8)], mine).reshape(size)
    size = outs[5].shape[0]
    for k in range(4):
        for t in range(3):
            lo = (4 * t + head_block(k)) * part
            row[0:1, lo : lo + part] = total[9 + k][:, t * part : (t + 1) * part]
    outs[5][...] = choose([row[0:1, k * size : (k + 1) * size] for k in range(8)], mine).reshape(size)
    size = outs[6].shape[0]
    pieces = [total[5 + k][:, t * size : (t + 1) * size] for t in range(2) for k in range(4)]
    outs[6][...] = choose(pieces, mine).reshape(size)


def join_att_call(me, owned, features, pieces):
    sizes = (features // 8,) * 5 + (3 * features // 8, features // 2, features // 8)
    return pl.pallas_call(
        join_att_kernel,
        out_shape=(
            jax.ShapeDtypeStruct((owned, 3 * features), wide),
            jax.ShapeDtypeStruct((owned, features), wide),
        )
        + tuple(jax.ShapeDtypeStruct((n,), wide) for n in sizes),
        in_specs=[in_smem] + [in_vmem] * 4,
        out_specs=(in_vmem,) * 10,
        scratch_shapes=[pltpu.VMEM((4, owned // 4, 128), wide), pltpu.VMEM((8, 3 * features), wide)],
        name="join_qkv_gradient",
    )(me, *pieces)


def finish_kernel(first, count, x_ref, cot_ref, vecs, *refs):
    out, grad = refs[-2:]
    for k in range(count):
        mine, got, over = refs[3 * k : 3 * k + 3]
        s = first + k
        spot = k if x_ref.shape[0] == count else s
        x = x_ref[spot].astype(wide)
        total = mine[0].astype(wide) + got[0].astype(wide) + over[0].astype(wide)
        out[spot] = (x + total + vecs[4:5, :]).astype(low)
        e = mine[1].astype(wide) + got[1].astype(wide) + over[1].astype(wide)
        center = x - jnp.mean(x, axis=-1, keepdims=True)
        spread = jnp.mean(center * center, axis=-1, keepdims=True)
        root = lax.rsqrt(spread + epsilon)
        n = center * root
        back = root * (e - jnp.mean(e, axis=-1, keepdims=True) - n * jnp.mean(e * n, axis=-1, keepdims=True))
        grad[spot] = (cot_ref[spot].astype(wide) + back).astype(low)


def finish_call(first, tokens, cotangent, vecs, triples, before=None):
    count, shape = len(triples), jax.ShapeDtypeStruct(tokens.shape, low)
    block = pl.BlockSpec((count, *tokens.shape[1:]), lambda i: (first // count, 0, 0))
    assert first % count == 0
    whole = [pl.BlockSpec(v.shape, lambda i, d=v.ndim: (0,) * d) for v in (vecs, *sum(triples, ()))]
    operands = [tokens, cotangent, vecs, *sum(triples, ())]
    specs = [block, block, *whole]
    aliases = {}
    if before is not None:
        aliases = {len(operands): 0, len(operands) + 1: 1}
        operands += list(before)
        specs += [anywhere, anywhere]
    return pl.pallas_call(
        partial(finish_kernel, first, count),
        grid=(1,),
        out_shape=(shape, shape),
        in_specs=specs,
        out_specs=(block, block),
        input_output_aliases=aliases,
        name="finish_tokens",
    )(*operands)


def shards(
    tokens,
    segment,
    ln1_gain,
    ln1_bias,
    qkv_weight,
    qkv_bias,
    out_weight,
    out_bias,
    ln2_gain,
    ln2_bias,
    fc_weight,
    fc_bias,
    proj_weight,
    proj_bias,
    cotangent,
):
    ctx, fsdp, rep = lax.axis_size("ctx"), lax.axis_size("fsdp"), lax.axis_size("rep")
    c, f, r = lax.axis_index("ctx"), lax.axis_index("fsdp"), lax.axis_index("rep")
    paired = fsdp == 2 and ctx == 4 and rep == 4
    seqs, local_len, features = tokens.shape
    length = local_len * ctx
    owned = qkv_weight.shape[0]
    hidden_own = proj_weight.shape[0]
    hidden_all = fc_weight.shape[1]
    hidden = hidden_all // ctx
    part = features // ctx
    me = f * ctx + c
    core = c & 1

    half = ROT // 2
    inverse = (1.0 / np.float32(10000.0) ** (np.arange(0, ROT, 2, dtype=np.float32) / ROT)).astype(np.float32)
    angles = inverse[:, None] * np.arange(length, dtype=np.float32)[None, :]
    cosine, sine = jnp.asarray(np.cos(angles)), jnp.asarray(np.sin(angles))

    def far_rows(s, *before):
        both = jnp.stack([tokens[s], cotangent[s]])
        return swap(after(both, *before) if before else both, "ctx", 2)

    near = (swap(tokens, "ctx", 1), swap(cotangent, "ctx", 1))

    if paired:
        where = jnp.stack([c, f, core, r]).astype(jnp.int32)
        vectors = (ln1_gain, ln1_bias, ln2_gain, ln2_bias, out_bias, proj_bias, qkv_bias, fc_bias)
        proj_x = swap(proj_weight, "fsdp", 1)
        q0, q1, q2, q3, f0, f1, f2, f3 = pack_call(where, qkv_weight, fc_weight, segment, vectors)
        f_got = [swap(f1, "ctx", 1), swap(f2, "ctx", 2), swap(f3, "ctx", 3)]
        far_send = [jnp.stack([tokens[s], cotangent[s]]) for s in range(seqs)]
        f_got, far_send = lax.optimization_barrier((f_got, far_send))
        far = [swap(far_send[0], "ctx", 2)]
        f_half = rows_call(where, owned, (f0, *f_got))
        f_half, proj_x = lax.optimization_barrier((f_half, proj_x))
        f_other = swap(f_half, "fsdp", 1)
        far1 = swap(after(far_send[1], f_half), "ctx", 2)
        far[0], f_other = lax.optimization_barrier((far[0], f_other))
        far_core = [swap(far[0], "ctx", 1)]
        vecs, bias, segs = prep_call(where, owned, part, seqs, length, f_half, f_other)
        proj_pair, fc_pair = (proj_weight, proj_x), (f_half, f_other)
    else:
        zero = jnp.zeros_like(c)
        where = jnp.stack([c, zero, zero, zero]).astype(jnp.int32)

        def whole(v, axes=("fsdp", "ctx")):
            return lax.all_gather(v, axes, axis=0, tiled=True)

        far = [far_rows(s) for s in range(seqs)]
        far_core = [swap(v, "ctx", 1) for v in far]
        bias = pick(whole(qkv_bias).reshape(3, ctx, part).transpose(1, 0, 2), c).astype(wide)
        bias = jnp.broadcast_to(bias.reshape(3 * part, 1), (3 * part, 128))
        b_sum = (whole(out_bias).astype(wide) + whole(proj_bias).astype(wide)).reshape(1, features)
        vecs = [whole(v).astype(wide) for v in (ln1_gain, ln1_bias, ln2_gain, ln2_bias)]
        vecs += [b_sum.reshape(features), pick(whole(fc_bias).reshape(ctx, hidden), c).astype(wide)]
        vecs = jnp.concatenate([jnp.stack(vecs), jnp.zeros((2, features), wide)])
        segs = lax.all_gather(segment.astype(low), "ctx", axis=1, tiled=True).astype(wide)
        segs = jnp.concatenate([segs, jnp.zeros((8 - seqs, length), wide)])

        def halves(v):
            return v[: v.shape[0] // 2], v[v.shape[0] // 2 :]

        out_pair = halves(pick(whole(out_weight).reshape(ctx, part, features), c))
        proj_pair = halves(pick(whole(proj_weight).reshape(ctx, hidden, features), c))
        qkv_pair = pick(whole(qkv_weight).reshape(features, 3, ctx, part).transpose(2, 0, 1, 3), c)
        qkv_pair = halves(qkv_pair.reshape(features, 3 * part))
        fc_pair = halves(pick(whole(fc_weight).reshape(features, ctx, hidden).transpose(1, 0, 2), c))

    def run_ff(s, args, acc, part_in, is_last):
        send, keep, *grads = ff_call(s, where, args, *fc_pair, *proj_pair, vecs, acc, part_in, is_last)
        return (send, keep), grads

    def run_att(s, args, weights, acc, part_in, vec=None):
        send_near, keep_near, send_far, keep_far, *grads = att_call(
            s, where, args, *weights[0], bias, *weights[1], vecs, segs, cosine, sine, acc, part_in, vec
        )
        return (send_near, keep_near, send_far, keep_far), grads

    def chip_sum(send, keep):
        return (keep.astype(wide) + swap(send, "ctx", 1).astype(wide)).astype(low)

    def to_rep(pieces):
        return [swap(piece, "rep", k) for k, piece in zip(range(1, rep), pieces)]

    def to_ctx(pieces):
        return [swap(piece, "ctx", k) for k, piece in zip(range(1, ctx), pieces)]

    def add_up(first, others):
        total = first
        for value in others:
            total = total + value.astype(wide)
        return total.astype(low)

    phase = lax.optimization_barrier
    if paired:
        args = (tokens, cotangent, *near, far[0], far_core[0])
        far_send, q1, q2, q3, out_send, args = phase((far_send, q1, q2, q3, out_weight, args))
        q_got = [swap(q1, "ctx", 1), swap(q2, "ctx", 2), swap(q3, "ctx", 3)]
        out_x = swap(out_send, "fsdp", 1)
        part0, acc = run_ff(0, args, None, None, False)

        part0, acc, far1, q_got, far_send, out_x = phase((part0, acc, far1, q_got, far_send, out_x))
        far2 = swap(far_send[2], "ctx", 2)
        out_keep = jnp.where(core == f, out_weight, out_x)
        out_got = swap(jnp.where(core == f, out_x, out_weight), "ctx", 1)
        far1_core = swap(far1, "ctx", 1)
        part1, acc = run_ff(1, (tokens, cotangent, *near, far1, far1_core), acc, None, False)

        part1, acc, far2, q_got, out_got, out_keep = phase((part1, acc, far2, q_got, out_got, out_keep))
        q_half = rows_call(where, owned, (q0, *q_got))
        far2_core = swap(far2, "ctx", 1)
        far2_core, q_half, acc = phase((far2_core, q_half, acc))
        q_other = swap(q_half, "fsdp", 1)
        part2, ff_last = run_ff(2, (tokens, cotangent, *near, far2, far2_core), acc, None, True)

        part0, ff_last, q_other = phase((part0, ff_last, q_other))
        att_weights = ((q_half, q_other), (out_keep, out_got))
        ff_got = swap(ff_last[1], "fsdp", 1)
        args = (tokens, cotangent, *near, far[0], far_core[0])
        part0, att_acc = run_att(0, args, att_weights, None, part0)

        part0, att_acc, ff_got = phase((part0, att_acc, ff_got))
        ff_pieces = split_call(where, ff_last[0], ff_got)
        away = chip_sum(*part0[2:])
        ff_pieces, part0, away, part1, att_acc = phase((ff_pieces, part0, away, part1, att_acc))
        ff_got = to_rep(ff_pieces[1:])
        over0 = swap(away, "ctx", 2)
        got0 = swap(part0[0], "ctx", 1)
        args = (tokens, cotangent, *near, far1, far1_core)
        part1, att_acc = run_att(1, args, att_weights, att_acc, part1)

        part1, att_acc, ff_got, over0, got0 = phase((part1, att_acc, ff_got, over0, got0))
        ff_total = add_up(ff_pieces[0], ff_got)
        away = chip_sum(*part1[2:])
        ff_total, part1, away, part2, att_acc = phase((ff_total, part1, away, part2, att_acc))
        ff_got = to_rep([ff_total] * (rep - 1))
        over1 = swap(away, "ctx", 2)
        got1 = swap(part1[0], "ctx", 1)
        args = (tokens, cotangent, *near, far2, far2_core)
        part2, att_last = run_att(2, args, att_weights, att_acc, part2, ff_last[2])

        part2, att_last, ff_got, over1, got1 = phase((part2, att_last, ff_got, over1, got1))
        flat = [(k, i) for k in range(fsdp) for i in range(ctx)]
        messages = [att_last[0]]
        for g, h in flat[1:]:
            peers = [(k * ctx + i, (k ^ g) * ctx + (i ^ h)) for k, i in flat]
            messages.append(lax.ppermute(att_last[g * ctx + h], ("fsdp", "ctx"), peers))
        pairs = [(k, i, 1 - k, i) if (i & 1) != k else (k, i, k, i ^ 1) for k, i in flat]
        near_got = lax.ppermute(att_last[9], ("fsdp", "ctx"), [(a * ctx + b, d * ctx + e) for a, b, d, e in pairs])
        pairs = [(k * ctx + i, (1 - k) * ctx + (i ^ 1)) for k, i in flat if (i & 1) != k]
        far_got = lax.ppermute(att_last[10], ("fsdp", "ctx"), pairs)
        away = chip_sum(*part2[2:])
        messages, near_got, far_got, part2, away, ff_got = phase(
            (messages, near_got, far_got, part2, away, ff_got)
        )

        pieces = meet_call(where, messages, (att_last[8], near_got, far_got))
        pieces, away, part2 = phase((pieces, away, part2))
        got = to_rep(pieces[1:])
        over2 = swap(away, "ctx", 2)
        got2 = swap(part2[0], "ctx", 1)
        *ff_blocks, g_proj = spread_call(where, owned, hidden_own, (ff_total, *ff_got))
        done = finish_call(0, tokens, cotangent, vecs, [(part0[1], got0, over0), (part1[1], got1, over1)])
        got, over2, got2, ff_blocks, done = phase((got, over2, got2, ff_blocks, done))

        piece = add_up(pieces[0], got)
        piece, over2, got2, ff_blocks, done = phase((piece, over2, got2, ff_blocks, done))
        others = to_rep([piece] * (rep - 1))
        ff_blocks_got = to_ctx(ff_blocks[1:])
        output, grad_tokens = finish_call(2, tokens, cotangent, vecs, [(part2[1], got2, over2)], done)
        g_fc = join_ff_call(where, (ff_blocks[0], *ff_blocks_got))
        g_qkv, g_out, *vector_grads = join_att_call(where, owned, features, (piece, *others))
    else:
        att_acc = ff_acc = None
        done = None
        for s in range(seqs):
            args = (tokens, cotangent, *near, far[s], far_core[s])
            parts, ff_acc = run_ff(s, args, ff_acc, None, s == seqs - 1)
            vec = ff_acc[2] if s == seqs - 1 else None
            parts, att_acc = run_att(s, args, (qkv_pair, out_pair), att_acc, parts, vec)
            over = swap(chip_sum(*parts[2:]), "ctx", 2)
            done = finish_call(s, tokens, cotangent, vecs, [(parts[1], swap(parts[0], "ctx", 1), over)], done)
        output, grad_tokens = done

        def any_columns(kept, sent):
            grad = jnp.concatenate([kept.astype(low), sent])
            grad = lax.psum_scatter(grad, "fsdp", scatter_dimension=0, tiled=True)
            grad = lax.psum(grad, "rep").reshape(ctx, owned, -1)
            return lax.all_to_all(grad, "ctx", split_axis=0, concat_axis=0)

        def any_rows(kept, sent):
            grad = jnp.concatenate([kept.astype(low), sent])
            grad = jnp.where(jnp.arange(ctx)[:, None, None] == c, grad[None], 0).reshape(-1, features)
            return lax.psum(
                lax.psum_scatter(grad, ("fsdp", "ctx"), scatter_dimension=0, tiled=True), "rep"
            )

        cut = features // 2
        g_fc = any_columns(ff_acc[0][:cut], ff_acc[1][:cut])
        g_fc = g_fc.transpose(1, 0, 2).reshape(owned, hidden_all)
        g_proj = any_rows(ff_acc[0][cut:], ff_acc[1][cut:])
        sent = jnp.concatenate([att_acc[0][None].astype(low), jnp.stack(att_acc[1:8])])
        whole_w = jnp.concatenate(in_order([v[: part // 2] for v in sent], c))
        g_qkv = any_columns(whole_w[: features // 2], whole_w[features // 2 :]).reshape(ctx, owned, 3, part)
        g_qkv = g_qkv.transpose(1, 2, 0, 3).reshape(owned, 3 * features)
        g_out = any_rows(*att_acc[8:10])
        vec = att_acc[0][part // 2 :]
        vec = jnp.concatenate([vec[:8], vec[8:, : features - 3 * part]], axis=1)
        total_vec = jnp.zeros((16, features), wide).at[0:5].set(vec[0:5])
        total_vec = lax.dynamic_update_slice(total_vec, vec[5:6], (5 + c, 0))
        total_vec = lax.dynamic_update_slice(total_vec, vec[6:7], (9 + c, 0))
        total_vec = lax.psum(total_vec, ("ctx", "fsdp", "rep"))
        grads = [total_vec[k] for k in range(5)]
        grads.append(total_vec[9 : 9 + ctx, : 3 * part].reshape(ctx, 3, part).transpose(1, 0, 2).reshape(-1))
        grads.append(total_vec[5 : 5 + ctx, :hidden].reshape(-1))
        grads.append(total_vec[4])
        vector_grads = []
        for v in grads:
            size = v.shape[0] // (fsdp * ctx)
            vector_grads.append(lax.dynamic_slice(v, (me * size,), (size,)))
    g_gain_one, g_shift_one, g_gain_two, g_shift_two, g_b_out, g_b_qkv, g_b_fc, g_b_proj = vector_grads
    return (
        output,
        grad_tokens,
        g_gain_one,
        g_shift_one,
        g_qkv.astype(wide),
        g_b_qkv,
        g_out.astype(wide),
        g_b_out,
        g_gain_two,
        g_shift_two,
        g_fc.astype(wide),
        g_b_fc,
        g_proj.astype(wide),
        g_b_proj,
    )


def solution(mesh):
    rows, row = P(("rep", "fsdp"), "ctx", None), P(("rep", "fsdp"), "ctx")
    vector, matrix = P(("fsdp", "ctx")), P(("fsdp", "ctx"), None)
    params = (
        vector, vector, matrix, vector, matrix, vector,
        vector, vector, matrix, vector, matrix, vector,
    )
    return jax.shard_map(
        shards,
        mesh=mesh,
        in_specs=(rows, row, *params, rows),
        out_specs=(rows, rows, *params),
        check_vma=False,
    )
```

```python
from functools import partial
import math

import jax
import jax.numpy as jnp
import numpy as np
from jax import lax
from jax.experimental import pallas as pl
from jax.experimental.pallas import tpu as pltpu
from jax.sharding import PartitionSpec as P

HEADS = 12
HEAD = 64
ROT = 16

epsilon = 1e-05
far_below = -1e30
low = jnp.bfloat16
wide = jnp.float32
log2e = math.log2(math.e)


def nn(a, b):
    return lax.dot_general(a, b, (((1,), (0,)), ((), ())), preferred_element_type=wide)


def nt(a, b):
    return lax.dot_general(a, b, (((1,), (1,)), ((), ())), preferred_element_type=wide)


def swap(value, axis, bits):
    size = lax.axis_size(axis)
    return lax.ppermute(value, axis, [(i, i ^ bits) for i in range(size)])


def in_order(rel, me):
    out = []
    for k in range(len(rel)):
        value = rel[k]
        for m in range(1, len(rel)):
            value = jnp.where(me == m, rel[k ^ m], value)
        out.append(value)
    return out


def pick(stacked, index):
    return lax.dynamic_index_in_dim(stacked, index, 0, keepdims=False)


def after(value, *before):
    return lax.optimization_barrier((value, before))[0]


anywhere = pl.BlockSpec(memory_space=pltpu.HBM)
in_vmem = pl.BlockSpec(memory_space=pltpu.VMEM)
in_smem = pl.BlockSpec(memory_space=pltpu.SMEM)
extra_rows = 16


def head_block(index):
    return ((index & 1) << 1) | (index >> 1)


def pack_kernel(vectors, me_ref, qkv, fc, segment, *refs):
    vector_refs, refs = refs[:vectors], refs[vectors:]
    q0, q1, q2, q3, f0, f1, f2, f3, scratch, extra = refs
    c = me_ref[0]
    owned, part, unit = qkv.shape[0], qkv.shape[1] // 12, fc.shape[1] // 8
    extra[...] = jnp.zeros_like(extra)
    for row, ref in enumerate(vector_refs):
        extra[row : row + 1, 0 : ref.shape[0]] = ref[...].astype(wide).reshape(1, -1)
    extra[8 : 8 + segment.shape[0], 0 : segment.shape[1]] = segment[...].astype(wide)
    for k in range(4):
        block = head_block(k)
        for t in range(3):
            lo = (4 * t + block) * part
            scratch[k ^ c, :, t * part : (t + 1) * part] = qkv[:, lo : lo + part]
    for k, (q, g) in enumerate(((q0, f0), (q1, f1), (q2, f2), (q3, f3))):
        q[...] = scratch[k]
        for t in range(2):
            lo = pl.multiple_of((4 * t + (c ^ k)) * unit, 128)
            g[0:owned, t * unit : (t + 1) * unit] = fc[:, pl.ds(lo, unit)]
        g[owned:, :] = extra[...].astype(low)


def pack_call(me, qkv, fc, segment, vectors):
    owned = qkv.shape[0]
    narrow, broad = (owned, qkv.shape[1] // 4), (owned + extra_rows, fc.shape[1] // 4)
    shapes = (narrow,) * 4 + (broad,) * 4
    return pl.pallas_call(
        partial(pack_kernel, len(vectors)),
        out_shape=tuple(jax.ShapeDtypeStruct(s, low) for s in shapes),
        in_specs=[in_smem] + [in_vmem] * (3 + len(vectors)),
        out_specs=(in_vmem,) * 8,
        scratch_shapes=[
            pltpu.VMEM((4, owned, narrow[1]), low),
            pltpu.VMEM((extra_rows, broad[1]), wide),
        ],
        name="pack_columns",
    )(me, qkv, fc, segment, *vectors)


def rows_kernel(owned, me_ref, p0, p1, p2, p3, half):
    c = me_ref[0]
    tail = p0.shape[0] - owned
    for k, p in enumerate((p0, p1, p2, p3)):
        half[pl.ds(pl.multiple_of((c ^ k) * owned, 16), owned), :] = p[0:owned, :]
        if tail:
            half[pl.ds(pl.multiple_of(4 * owned + (c ^ k) * tail, 16), tail), :] = p[owned:, :]


def rows_call(me, owned, pieces):
    rows, cols = pieces[0].shape
    return pl.pallas_call(
        partial(rows_kernel, owned),
        out_shape=jax.ShapeDtypeStruct((4 * rows, cols), low),
        in_specs=[in_smem] + [in_vmem] * 4,
        out_specs=in_vmem,
        name="rows_by_ctx",
    )(me, *pieces)


def prep_kernel(owned, part, seqs, me_ref, mine, other, vecs, bias, seg):
    c, f = me_ref[0], me_ref[1]
    extra_mine, extra_other = mine[...].astype(wide), other[...].astype(wide)
    first = jnp.where(f == 0, extra_mine, extra_other)
    last = jnp.where(f == 0, extra_other, extra_mine)

    def vector(row, size):
        pieces = [
            e[k * extra_rows + row : k * extra_rows + row + 1, 0:size]
            for e in (first, last)
            for k in range(4)
        ]
        return jnp.concatenate(pieces, axis=1)

    block = head_block(c)
    vecs[...] = jnp.zeros_like(vecs)
    for row in range(4):
        vecs[row : row + 1, :] = vector(row, owned)
    vecs[4:5, :] = vector(4, owned) + vector(5, owned)
    unit = mine.shape[1] // 2
    for t, e in enumerate((first, last)):
        chosen = e[7:8, 0:unit]
        for k in range(1, 4):
            chosen = jnp.where(c == k, e[k * extra_rows + 7 : k * extra_rows + 8, 0:unit], chosen)
        vecs[5:6, t * unit : (t + 1) * unit] = chosen
    all_qkv = vector(6, 3 * owned)
    picked = []
    for t in range(3):
        chosen = all_qkv[:, 4 * t * part : (4 * t + 1) * part]
        for k in range(1, 4):
            chosen = jnp.where(block == k, all_qkv[:, (4 * t + k) * part : (4 * t + k + 1) * part], chosen)
        picked.append(chosen)
    row_bias = jnp.concatenate(picked, axis=1)
    bias[...] = jnp.transpose(jnp.broadcast_to(row_bias, (128, 3 * part)))
    seg[...] = jnp.zeros_like(seg)
    width = seg.shape[1] // 4
    for s in range(seqs):
        for k in range(4):
            row = k * extra_rows + 8 + s
            seg[s : s + 1, k * width : (k + 1) * width] = extra_mine[row : row + 1, 0:width]


def prep_call(me, owned, part, seqs, length, mine, other):
    tail = pl.BlockSpec((4 * extra_rows, mine.shape[1]), lambda i: (4 * owned // (4 * extra_rows), 0))
    assert 4 * owned % (4 * extra_rows) == 0
    shapes = ((8, 8 * owned), (3 * part, 128), (8, length))
    return pl.pallas_call(
        partial(prep_kernel, owned, part, seqs),
        grid=(1,),
        out_shape=tuple(jax.ShapeDtypeStruct(s, wide) for s in shapes),
        in_specs=[in_smem, tail, tail],
        out_specs=tuple(pl.BlockSpec(s, lambda i: (0, 0)) for s in shapes),
        name="prepare_vectors",
    )(me, mine, other)


def row_norm(block):
    values = block.astype(wide)
    center = values - jnp.mean(values, axis=-1, keepdims=True)
    spread = jnp.mean(center * center, axis=-1, keepdims=True)
    return center * lax.rsqrt(spread + epsilon)


def gelu_parts(v):
    bell = jnp.exp2(v * v * (-0.5 * log2e))
    base = 1.0 + (0.3275911 / math.sqrt(2.0)) * jnp.abs(v)
    t = pl.reciprocal(base, approx=True)
    t = t * (2.0 - base * t)
    poly = 0.5 * 1.061405429
    for coef in (-1.453152027, 1.421413741, -0.284496736, 0.254829592):
        poly = poly * t + 0.5 * coef
    tail = poly * t * bell
    phi = jnp.where(v >= 0, 1.0 - tail, tail)
    return phi, phi + v * bell * (1.0 / math.sqrt(2.0 * math.pi))


def bring(pairs, sem):
    copies = [pltpu.make_async_copy(a, b, sem.at[k]) for k, (a, b) in enumerate(pairs)]
    for copy in copies:
        copy.start()
    return copies


def token_pairs(s, refs, xs, cs):
    tok, cot, tok1, cot1, far, far1 = refs
    pairs = []
    for j, (t, c) in enumerate(
        ((tok.at[s], cot.at[s]), (tok1.at[s], cot1.at[s]), (far.at[0], far.at[1]), (far1.at[0], far1.at[1]))
    ):
        pairs += [(t, xs.at[j]), (c, cs.at[j])]
    return pairs


def ff_kernel(s, with_acc, with_part, is_last, *refs):
    me_ref, refs = refs[0], refs[1:]
    token_refs, refs = refs[:6], refs[6:]
    fc_a, fc_b, proj_a, proj_b, vecs = refs[:5]
    refs = refs[5:]
    if with_acc:
        acc_fc_in, acc_proj_in, acc_vec_in = refs[:3]
        refs = refs[3:]
    if with_part:
        part_send, part_keep = refs[:2]
        refs = refs[2:]
    send, keep = refs[:2]
    refs = refs[2:]
    if is_last:
        grad_keep, grad_send, vec = refs[:3]
        refs = refs[3:]
    else:
        fc_out, proj_out, vec = refs[:3]
        refs = refs[3:]
    xs, cs, fc, proj, sec_s, hid_s, gp_s, send_s, keep_s, acc_fc, acc_proj, sem, sem_w, sem_p, sem_o = refs[:15]
    if is_last:
        stage_keep, stage_send = refs[15:]
    f = me_ref[1]
    blocks, rows, features = xs.shape
    hidden = fc.shape[1]
    third, half = features // 2, proj_a.shape[0]
    tokens_in = bring(token_pairs(s, token_refs, xs, cs), sem)
    weights_in = bring(
        [
            (fc_a.at[0:third], fc.at[pl.ds(pl.multiple_of(f * third, 16), third), :]),
            (fc_b.at[0:third], fc.at[pl.ds(pl.multiple_of((1 - f) * third, 16), third), :]),
            (proj_a, proj.at[pl.ds(pl.multiple_of(f * half, 16), half), :]),
            (proj_b, proj.at[pl.ds(pl.multiple_of((1 - f) * half, 16), half), :]),
        ],
        sem_w,
    )
    later = []
    if with_part:
        later += [(part_send, send_s), (part_keep, keep_s)]
    if with_acc:
        later += [(acc_fc_in, acc_fc), (acc_proj_in, acc_proj)]
    later = bring(later, sem_p)
    for copy in weights_in + tokens_in:
        copy.wait()
    gain, shift, bias = vecs[2:3, :], vecs[3:4, :], vecs[5:6, 0:hidden]
    dgain = jnp.zeros((1, features), wide)
    dshift = jnp.zeros((1, features), wide)
    dbias = jnp.zeros((1, hidden), wide)
    if with_part:
        later[0].wait()
        later[1].wait()
    for j in range(blocks):
        here = pl.ds(j * rows, rows)
        n = row_norm(xs[j])
        second = (n * gain + shift).astype(low)
        sec_s[here, :] = second
        cot = cs[j]
        pre = nn(second, fc[...]) + bias
        phi, slope = gelu_parts(pre)
        hid = (pre * phi).astype(low)
        gp = nt(cot, proj[...]) * slope
        dbias = dbias + jnp.sum(gp, axis=0, keepdims=True)
        gp = gp.astype(low)
        hid_s[here, :] = hid
        gp_s[here, :] = gp
        out = nn(hid, proj[...])
        dsec = nt(gp, fc[...])
        dgain = dgain + jnp.sum(dsec * n, axis=0, keepdims=True)
        dshift = dshift + jnp.sum(dsec, axis=0, keepdims=True)
        e = dsec * gain
        to = send_s if j % 2 else keep_s
        if with_part:
            out = out + to[j // 2 * 2].astype(wide)
            e = e + to[j // 2 * 2 + 1].astype(wide)
        to[j // 2 * 2] = out.astype(low)
        to[j // 2 * 2 + 1] = e.astype(low)
    results = bring([(send_s, send), (keep_s, keep)], sem_o)
    dcot = jnp.sum(cs[0].astype(wide), axis=0, keepdims=True)
    if with_acc:
        for copy in later[-2:]:
            copy.wait()
        dgain = dgain + acc_vec_in[0:1, :]
        dshift = dshift + acc_vec_in[1:2, :]
        dbias = dbias + acc_vec_in[2:3, 0:hidden]
        dcot = dcot + acc_vec_in[3:4, :]
    every_cot = cs[...].reshape(blocks * rows, features)
    for k, (acc, a, b, own) in enumerate(((acc_fc, sec_s, gp_s[...], third), (acc_proj, hid_s, every_cot, half))):
        grad = nn(jnp.transpose(a[...]), b)
        acc[...] = grad + acc[...] if with_acc else grad
        if is_last:
            lo = k * third
            stage_keep[lo : lo + own, :] = acc[pl.ds(pl.multiple_of(f * own, 16), own), :].astype(low)
            stage_send[lo : lo + own, :] = acc[pl.ds(pl.multiple_of((1 - f) * own, 16), own), :].astype(low)
            moves = [(stage_keep, grad_keep), (stage_send, grad_send)]
            moves = [(x.at[lo : lo + own], y.at[lo : lo + own]) for x, y in moves]
        else:
            moves = [(acc, (fc_out, proj_out)[k])]
        for x, y in moves:
            results.append(pltpu.make_async_copy(x, y, sem_o.at[len(results)]))
            results[-1].start()
    vec[0:1, :] = dgain
    vec[1:2, :] = dshift
    vec[2:3, 0:hidden] = dbias
    vec[3:4, :] = dcot
    for copy in results:
        copy.wait()


def ff_call(s, me, token_args, fc_a, fc_b, proj_a, proj_b, vecs, acc, part, is_last):
    rows, features = token_args[0].shape[1:]
    hidden, blocks = fc_a.shape[1], 4
    total = blocks * rows
    third = features // 2
    operands = [me, *token_args, fc_a, fc_b, proj_a, proj_b, vecs]
    specs = [in_smem] + [anywhere] * 10 + [in_vmem]
    aliases = {}
    if acc is not None:
        if not is_last:
            aliases = {len(operands): 2, len(operands) + 1: 3}
        operands += list(acc)
        specs += [anywhere, anywhere, in_vmem]
    if part is not None:
        aliases[len(operands)] = 0
        aliases[len(operands) + 1] = 1
        operands += list(part)
        specs += [anywhere, anywhere]
    shared = jax.ShapeDtypeStruct((4, rows, features), low)
    vec = jax.ShapeDtypeStruct((8, features), wide)
    if is_last:
        rows_out = third + proj_a.shape[0]
        grads = (
            jax.ShapeDtypeStruct((rows_out, features), low),
            jax.ShapeDtypeStruct((rows_out, features), low),
        )
        grad_specs = (anywhere,) * 2
        more = [pltpu.VMEM((rows_out, features), low)] * 2
    else:
        grads = (
            jax.ShapeDtypeStruct((features, hidden), wide),
            jax.ShapeDtypeStruct((hidden, features), wide),
        )
        grad_specs, more = (anywhere,) * 2, []
    return pl.pallas_call(
        partial(ff_kernel, s, acc is not None, part is not None, is_last),
        out_shape=(shared, shared, *grads, vec),
        in_specs=specs,
        out_specs=(anywhere, anywhere, *grad_specs, in_vmem),
        scratch_shapes=[
            pltpu.VMEM((blocks, rows, features), low),
            pltpu.VMEM((blocks, rows, features), low),
            pltpu.VMEM((features, hidden), low),
            pltpu.VMEM((hidden, features), low),
            pltpu.VMEM((total, features), low),
            pltpu.VMEM((total, hidden), low),
            pltpu.VMEM((total, hidden), low),
            pltpu.VMEM((4, rows, features), low),
            pltpu.VMEM((4, rows, features), low),
            pltpu.VMEM((features, hidden), wide),
            pltpu.VMEM((hidden, features), wide),
            pltpu.SemaphoreType.DMA((8,)),
            pltpu.SemaphoreType.DMA((4,)),
            pltpu.SemaphoreType.DMA((4,)),
            pltpu.SemaphoreType.DMA((8,)),
            *more,
        ],
        input_output_aliases=aliases,
        compiler_params=pltpu.CompilerParams(vmem_limit_bytes=50 * 2**20),
        cost_estimate=pl.CostEstimate(flops=1, bytes_accessed=1, transcendentals=0),
        name="feed_forward",
    )(*operands)


def turn(block, cosine, sine):
    half = ROT // 2
    a, b = block[0:half], block[half:ROT]
    return jnp.concatenate([a * cosine - b * sine, b * cosine + a * sine, block[ROT:]], axis=0)


def att_kernel(s, heads, with_acc, with_part, is_last, *refs):
    me_ref, refs = refs[0], refs[1:]
    token_refs, refs = refs[:6], refs[6:]
    w_a, w_b, bias, wout_a, wout_b, vecs, segs, cosine, sine = refs[:9]
    refs = refs[9:]
    if is_last:
        ff_vec, refs = refs[0], refs[1:]
    if with_acc:
        acc_w_in, acc_o_in, acc_vec_in = refs[:3]
        refs = refs[3:]
    if with_part:
        part_send, part_keep = refs[:2]
        refs = refs[2:]
    homes, refs = refs[:4], refs[4:]
    if is_last:
        messages, (o_keep, o_send, o_send_far) = refs[:8], refs[8:11]
        refs = refs[11:]
    else:
        w_out, o_out, vec = refs[:3]
        refs = refs[3:]
    xs, cs, wt_s, wout, first_s, n_s, cot_s, qt_s, kt_s, vt_s, k_s, v_s, dot_s, mask_s, att_s, d_s, dk_s, dv_s = refs[:18]
    send_s, keep_s, acc_w, acc_o, sem, sem_p, sem_o = refs[18:25]
    if is_last:
        by_rows = refs[25]
    me, f, core = me_ref[0], me_ref[1], me_ref[2]
    blocks, rows, features = xs.shape
    part = heads * HEAD
    length = blocks * rows
    reach = length // 2
    scale = 1.0 / math.sqrt(HEAD)
    tokens_in = bring(token_pairs(s, token_refs, xs, cs), sem)
    gain, shift = vecs[0:1, :], vecs[1:2, :]
    share = w_a.shape[0]
    wt_s[:, pl.ds(pl.multiple_of(f * share, 128), share)] = jnp.transpose(w_a[...])
    wt_s[:, pl.ds(pl.multiple_of((1 - f) * share, 128), share)] = jnp.transpose(w_b[...])
    owned = wout_a.shape[0]
    wout[pl.ds(pl.multiple_of(core * owned, 16), owned), :] = wout_a[...]
    wout[pl.ds(pl.multiple_of((1 - core) * owned, 16), owned), :] = wout_b[...]

    seg_row = segs[s : s + 1, :]
    seg_col = jnp.transpose(jnp.broadcast_to(seg_row, (128, length)))
    spans, place = [], 0
    for i in range(blocks):
        start = max(0, i * rows - reach)
        count = (i + 1) * rows - start
        spans.append((start, count, place))
        ours = seg_row[:, i * rows : (i + 1) * rows]
        theirs = seg_col[start : start + count]
        theirs = jnp.concatenate([theirs] * (rows // 128), axis=1)
        key = start + lax.broadcasted_iota(jnp.int32, (count, rows), 0)
        query = i * rows + lax.broadcasted_iota(jnp.int32, (count, rows), 1)
        allowed = (theirs == ours) & (key <= query)
        mask_s[place : place + count, :] = jnp.where(allowed, 0.0, far_below)
        place += count

    for copy in tokens_in:
        copy.wait()
    wide_bias = jnp.concatenate([bias[...]] * (rows // 128), axis=1)
    for j in range(blocks):
        off = pl.multiple_of((me ^ j) * rows, rows)
        n = row_norm(xs[j])
        n_s[pl.ds(off, rows), :] = n.astype(low)
        first = (n * gain + shift).astype(low)
        first_s[pl.ds(off, rows), :] = first
        cot = cs[j]
        cot_s[pl.ds(off, rows), :] = cot
        cos_b, sin_b = cosine[:, pl.ds(off, rows)], sine[:, pl.ds(off, rows)]
        made = nt(wt_s[...], first) + wide_bias
        for h in range(heads):
            lo, hi = h * HEAD, (h + 1) * HEAD
            query = turn(made[lo:hi], cos_b, sin_b).astype(low)
            qt_s[lo:hi, pl.ds(off, rows)] = (query.astype(wide) * scale).astype(low)
            key = turn(made[part + lo : part + hi], cos_b, sin_b).astype(low)
            kt_s[lo:hi, pl.ds(off, rows)] = key
            value = made[2 * part + lo : 2 * part + hi].astype(low)
            vt_s[lo:hi, pl.ds(off, rows)] = value
            k_s[h, pl.ds(off, rows), :] = jnp.transpose(key)
            v_s[h, pl.ds(off, rows), :] = jnp.transpose(value)
        dot_s[:, pl.ds(off, rows)] = nt(wout[...], cot).astype(low)

    later = []
    if with_part:
        later += [(part_send, send_s), (part_keep, keep_s)]
    if with_acc:
        later += [(acc_w_in, acc_w), (acc_o_in, acc_o)]
    later = bring(later, sem_p)
    dk_s[...] = jnp.zeros_like(dk_s)
    dv_s[...] = jnp.zeros_like(dv_s)

    def one_head(h, carry):
        base = pl.multiple_of(h * HEAD, HEAD)
        mine = pl.ds(base, HEAD)
        for i in range(blocks):
            start, count, place = spans[i]
            here, there = slice(i * rows, (i + 1) * rows), slice(start, start + count)
            query, grad = qt_s[mine, here], dot_s[mine, here]
            score = nn(k_s[h, there, :], query) + mask_s[place : place + count, :]
            top = jnp.max(score, axis=0, keepdims=True)
            lifted = jnp.exp2((score - top) * log2e)
            total = jnp.sum(lifted, axis=0, keepdims=True)
            prob = lifted * (1.0 / total)
            prob_low = prob.astype(low)
            att_s[mine, here] = nn(vt_s[mine, there], prob_low).astype(low)
            dprob = nn(v_s[h, there, :], grad)
            inner = jnp.sum(prob * dprob, axis=0, keepdims=True)
            dscore = (prob * (dprob - inner)).astype(low)
            dv_s[mine, there] += nt(grad, prob_low)
            dk_s[mine, there] += nt(query, dscore)
            dq = nn(kt_s[mine, there], dscore) * scale
            cos_b, sin_b = cosine[:, here], sine[:, here]
            d_s[mine, here] = turn(dq, cos_b, -sin_b).astype(low)
        return carry

    lax.fori_loop(0, heads, one_head, 0)
    for h in range(heads):
        lo, hi = h * HEAD, (h + 1) * HEAD
        d_s[part + lo : part + hi, :] = turn(dk_s[lo:hi, :], cosine[...], -sine[...]).astype(low)
    d_s[2 * part : 3 * part, :] = dv_s[...].astype(low)

    g_w = nn(d_s[...], first_s[...])
    g_o = nn(att_s[...], cot_s[...])
    if with_part:
        later[0].wait()
        later[1].wait()
    if with_acc:
        later[-2].wait()
        later[-1].wait()
        g_w = g_w + acc_w[...]
        g_o = g_o + acc_o[...]
    acc_w[...] = g_w
    results = []
    if is_last:
        by_rows[...] = jnp.transpose(acc_w[...])
        for k, message in enumerate(messages):
            shard = (f ^ (k // 4)) * 4 + (me ^ (k % 4))
            block = by_rows[pl.ds(pl.multiple_of(shard * owned, 8), owned), :]
            message[0:owned, :] = block.astype(message.dtype)
        acc_o[...] = g_o
        mine = acc_o[pl.ds(pl.multiple_of(f * owned, 16), owned), :]
        o_keep[...] = jnp.where(f == core, mine, 0.0)
        o_send[...] = acc_o[pl.ds(pl.multiple_of((1 - f) * owned, 16), owned), :].astype(low)
        o_send_far[...] = mine.astype(low)
    else:
        acc_o[...] = g_o
        results = [
            pltpu.make_async_copy(acc_w, w_out, sem_o.at[2]),
            pltpu.make_async_copy(acc_o, o_out, sem_o.at[3]),
        ]
        for copy in results:
            copy.start()
    dgain = jnp.zeros((1, features), wide)
    dshift = jnp.zeros((1, features), wide)
    dbias = jnp.zeros((8, 3 * part), wide)
    for j in range(blocks):
        off = pl.multiple_of((me ^ j) * rows, rows)
        att = jnp.transpose(att_s[:, pl.ds(off, rows)])
        out = nn(att, wout[...])
        dqkv = jnp.transpose(d_s[:, pl.ds(off, rows)])
        dbias = dbias + nn(jnp.ones((8, rows), low), dqkv)
        dfirst = nn(dqkv, wt_s[...])
        n = n_s[pl.ds(off, rows), :].astype(wide)
        dgain = dgain + jnp.sum(dfirst * n, axis=0, keepdims=True)
        dshift = dshift + jnp.sum(dfirst, axis=0, keepdims=True)
        e = dfirst * gain
        to, first = send_s if j % 2 else keep_s, j // 2 * 2
        if with_part:
            out = out + to[first].astype(wide)
            e = e + to[first + 1].astype(wide)
        to[first] = out.astype(low)
        to[first + 1] = e.astype(low)
        if j % 2:
            for k, (a, b) in enumerate(((send_s, homes[first]), (keep_s, homes[first + 1]))):
                results.append(pltpu.make_async_copy(a.at[first : first + 2], b, sem_o.at[4 + first + k]))
                results[-1].start()
    dbias = dbias[0:1]
    if with_acc:
        dgain = dgain + acc_vec_in[0:1, :]
        dshift = dshift + acc_vec_in[1:2, :]
        dbias = dbias + acc_vec_in[2:3, 0 : 3 * part]
    if is_last:
        cols = 3 * part
        rest = jnp.zeros((1, features - cols), wide)
        vec = jnp.concatenate(
            [dgain, dshift, ff_vec[0:2, :], ff_vec[3:4, :], ff_vec[2:3, :], jnp.concatenate([dbias, rest], axis=1)]
            + [jnp.zeros((1, features), wide)]
        )
        for message in messages:
            message[owned : owned + 8, :] = vec[:, 0:cols].astype(message.dtype)
            message[owned + 8 : owned + 16, 0 : features - cols] = vec[:, cols:].astype(message.dtype)
            message[owned + 8 : owned + 16, features - cols :] = jnp.zeros((8, 2 * cols - features), message.dtype)
    else:
        vec[0:1, :] = dgain
        vec[1:2, :] = dshift
        vec[2:3, 0 : 3 * part] = dbias
    for copy in results:
        copy.wait()


def att_call(s, me, token_args, w_a, w_b, bias, wout_a, wout_b, vecs, segs, cosine, sine, acc, part_in, ff_vec):
    rows, features = token_args[0].shape[1:]
    part, blocks = w_a.shape[1] // 3, 4
    heads = part // HEAD
    length = blocks * rows
    is_last = ff_vec is not None
    operands = [me, *token_args, w_a, w_b, bias, wout_a, wout_b, vecs, segs, cosine, sine]
    operands += [ff_vec] if is_last else []
    specs = [in_smem] + [anywhere] * 6 + [in_vmem] * (len(operands) - 7)
    aliases = {}
    if acc is not None:
        if not is_last:
            aliases = {len(operands): 4, len(operands) + 1: 5}
        operands += list(acc)
        specs += [anywhere, anywhere, in_vmem]
    if part_in is not None:
        operands += list(part_in)
        specs += [anywhere, anywhere]
    shared = jax.ShapeDtypeStruct((2, rows, features), low)
    if is_last:
        message = (part // 2 + 16, 3 * part)
        grads = (jax.ShapeDtypeStruct(message, wide),) + (jax.ShapeDtypeStruct(message, low),) * 7
        grads += (
            jax.ShapeDtypeStruct((part // 2, features), wide),
            jax.ShapeDtypeStruct((part // 2, features), low),
            jax.ShapeDtypeStruct((part // 2, features), low),
        )
        grad_specs = (in_vmem,) * 11
        last_vec, vec_specs = (), ()
        more = [pltpu.VMEM((features, 3 * part), wide)]
    else:
        grads = (
            jax.ShapeDtypeStruct((3 * part, features), wide),
            jax.ShapeDtypeStruct((part, features), wide),
        )
        grad_specs = (anywhere,) * 2
        last_vec, vec_specs, more = (jax.ShapeDtypeStruct((8, features), wide),), (in_vmem,), []
    reach = length // 2
    masked = sum((i + 1) * rows - max(0, i * rows - reach) for i in range(blocks))
    return pl.pallas_call(
        partial(att_kernel, s, heads, acc is not None, part_in is not None, is_last),
        out_shape=(shared,) * 4 + (*grads, *last_vec),
        in_specs=specs,
        out_specs=(anywhere,) * 4 + (*grad_specs, *vec_specs),
        scratch_shapes=[
            pltpu.VMEM((blocks, rows, features), low),
            pltpu.VMEM((blocks, rows, features), low),
            pltpu.VMEM((3 * part, features), low),
            pltpu.VMEM((part, features), low),
            pltpu.VMEM((length, features), low),
            pltpu.VMEM((length, features), low),
            pltpu.VMEM((length, features), low),
            pltpu.VMEM((part, length), low),
            pltpu.VMEM((part, length), low),
            pltpu.VMEM((part, length), low),
            pltpu.VMEM((heads, length, HEAD), low),
            pltpu.VMEM((heads, length, HEAD), low),
            pltpu.VMEM((part, length), low),
            pltpu.VMEM((masked, rows), wide),
            pltpu.VMEM((part, length), low),
            pltpu.VMEM((3 * part, length), low),
            pltpu.VMEM((part, length), wide),
            pltpu.VMEM((part, length), wide),
            pltpu.VMEM((4, rows, features), low),
            pltpu.VMEM((4, rows, features), low),
            pltpu.VMEM((3 * part, features), wide),
            pltpu.VMEM((part, features), wide),
            pltpu.SemaphoreType.DMA((8,)),
            pltpu.SemaphoreType.DMA((4,)),
            pltpu.SemaphoreType.DMA((8,)),
            *more,
        ],
        input_output_aliases=aliases,
        compiler_params=pltpu.CompilerParams(vmem_limit_bytes=56 * 2**20),
        cost_estimate=pl.CostEstimate(flops=1, bytes_accessed=1, transcendentals=0),
        name="attention",
    )(*operands)


def split_kernel(me_ref, keep, got, *refs):
    pieces, both = refs[:4], refs[4]
    r = me_ref[3]
    half = both.shape[0] // 2
    fine, short = half // 16, half // 4
    both[...] = keep[...].astype(wide) + got[...].astype(wide)
    for k, piece in enumerate(pieces):
        cut = r ^ k
        parts = [both[pl.ds(pl.multiple_of(b * 4 * fine + cut * fine, 8), fine), :] for b in range(4)]
        piece[0 : 4 * fine, :] = jnp.concatenate(parts).astype(piece.dtype)
        piece[4 * fine :, :] = both[pl.ds(pl.multiple_of(half + cut * short, 8), short), :].astype(piece.dtype)


def split_call(me, keep, got):
    shape = (keep.shape[0] // 4, keep.shape[1])
    return pl.pallas_call(
        split_kernel,
        out_shape=(jax.ShapeDtypeStruct(shape, wide),) + (jax.ShapeDtypeStruct(shape, low),) * 3,
        in_specs=[in_smem] + [in_vmem] * 2,
        out_specs=(in_vmem,) * 4,
        scratch_shapes=[pltpu.VMEM(keep.shape, wide)],
        name="split_gradients",
    )(me, keep, got)


def meet_kernel(me_ref, *refs):
    messages, (o_keep, o_near, o_far), pieces, (came, rows) = refs[:8], refs[8:11], refs[11:15], refs[15:]
    c, r = me_ref[0], me_ref[3]
    owned, features = o_keep.shape
    cols = came.shape[2]
    part, fine = cols // 3, owned // 4
    for k, message in enumerate(messages):
        came[k] = message[...].astype(wide)
    by_ctx = []
    for k in range(4):
        both = came[c ^ k] + came[4 + (c ^ k)]
        by_ctx.append(both)
        for t in range(3):
            lo = (4 * t + head_block(k)) * part
            rows[:, lo : lo + part] = both[0:owned, t * part : (t + 1) * part]
    rows[:, 3 * features :] = o_keep[...] + o_near[...].astype(wide) + o_far[...].astype(wide)
    vecs = [
        jnp.concatenate([b[owned : owned + 8, :], b[owned + 8 : owned + 16, 0 : features - cols]], axis=1)
        for b in by_ctx
    ]
    shared = (vecs[0] + vecs[1]) + (vecs[2] + vecs[3])
    vec = jnp.concatenate([shared[0:5]] + [v[5:6] for v in vecs] + [v[6:7] for v in vecs] + [shared[7:8]] * 3)
    for k, piece in enumerate(pieces):
        cut = r ^ k
        own = vec[0:4]
        for m in range(1, 4):
            own = jnp.where(cut == m, vec[4 * m : 4 * m + 4], own)
        piece[:, 0 : 4 * features] = rows[pl.ds(pl.multiple_of(cut * fine, 8), fine), :].astype(piece.dtype)
        lanes = [own[i // 6 : i // 6 + 1, i % 6 * 128 : i % 6 * 128 + 128] for i in range(24)]
        piece[:, 4 * features :] = jnp.concatenate(lanes).astype(piece.dtype)


def meet_call(me, messages, outs):
    owned, features = outs[0].shape
    assert features == 6 * 128 and owned == 96
    shape = (owned // 4, 4 * features + 128)
    return pl.pallas_call(
        meet_kernel,
        out_shape=(jax.ShapeDtypeStruct(shape, wide),) + (jax.ShapeDtypeStruct(shape, low),) * 3,
        in_specs=[in_smem] + [in_vmem] * 11,
        out_specs=(in_vmem,) * 4,
        scratch_shapes=[
            pltpu.VMEM((8, *messages[0].shape), wide),
            pltpu.VMEM((owned, 4 * features), wide),
        ],
        name="meet_gradients",
    )(me, *messages, *outs)


def spread_kernel(me_ref, p0, p1, p2, p3, b0, b1, b2, b3, rows_out, scratch):
    c, r = me_ref[0], me_ref[3]
    owned = b0.shape[0]
    fine, short = owned // 4, rows_out.shape[0] // 4
    for k, p in enumerate((p0, p1, p2, p3)):
        cut = r ^ k
        value = p[...].astype(wide)
        for b in range(4):
            scratch[b, pl.ds(pl.multiple_of(cut * fine, 8), fine), :] = value[b * fine : (b + 1) * fine]
        rows_out[pl.ds(pl.multiple_of(cut * short, 8), short), :] = value[owned:]
    for k, out in enumerate((b0, b1, b2, b3)):
        out[...] = scratch[c ^ k].astype(low)


def spread_call(me, owned, row_rows, pieces):
    features = pieces[0].shape[1]
    return pl.pallas_call(
        spread_kernel,
        out_shape=(jax.ShapeDtypeStruct((owned, features), low),) * 4
        + (jax.ShapeDtypeStruct((row_rows, features), wide),),
        in_specs=[in_smem] + [in_vmem] * 4,
        out_specs=(in_vmem,) * 5,
        scratch_shapes=[pltpu.VMEM((4, owned, features), wide)],
        name="spread_gradients",
    )(me, *pieces)


def join_ff_kernel(me_ref, b0, b1, b2, b3, out):
    c = me_ref[0]
    unit = out.shape[1] // 8
    for k, b in enumerate((b0, b1, b2, b3)):
        for t in range(2):
            lo = pl.multiple_of((4 * t + (c ^ k)) * unit, 128)
            out[:, pl.ds(lo, unit)] = b[:, t * unit : (t + 1) * unit].astype(wide)


def join_ff_call(me, blocks):
    owned, hidden = blocks[0].shape
    return pl.pallas_call(
        join_ff_kernel,
        out_shape=jax.ShapeDtypeStruct((owned, 4 * hidden), wide),
        in_specs=[in_smem] + [in_vmem] * 4,
        out_specs=in_vmem,
        name="join_fc_gradient",
    )(me, *blocks)


def join_att_kernel(me_ref, p0, p1, p2, p3, qkv_out, rows_out, *refs):
    outs, (vec, row) = refs[:8], refs[8:]
    c, f, r = me_ref[0], me_ref[1], me_ref[3]
    features, fine = rows_out.shape[1], p0.shape[0]
    part = features // 4
    for k, p in enumerate((p0, p1, p2, p3)):
        cut = r ^ k
        rows = pl.ds(pl.multiple_of(cut * fine, 8), fine)
        value = p[...].astype(wide)
        qkv_out[rows, :] = value[:, 0 : 3 * features]
        rows_out[rows, :] = value[:, 3 * features : 4 * features]
        vec[cut] = value[:, 4 * features :]

    mine = f * 4 + c
    total = [
        jnp.concatenate([vec[k // 4, k % 4 * 6 + i : k % 4 * 6 + i + 1, :] for i in range(6)], axis=1) for k in range(13)
    ]

    def choose(values, index):
        value = values[0]
        for k in range(1, len(values)):
            value = jnp.where(index == k, values[k], value)
        return value

    for i in (0, 1, 2, 3, 4, 7):
        size = outs[i].shape[0]
        source = total[min(i, 4)]
        outs[i][...] = choose([source[:, k * size : (k + 1) * size] for k in range(8)], mine).reshape(size)
    size = outs[5].shape[0]
    for k in range(4):
        for t in range(3):
            lo = (4 * t + head_block(k)) * part
            row[0:1, lo : lo + part] = total[9 + k][:, t * part : (t + 1) * part]
    outs[5][...] = choose([row[0:1, k * size : (k + 1) * size] for k in range(8)], mine).reshape(size)
    size = outs[6].shape[0]
    pieces = [total[5 + k][:, t * size : (t + 1) * size] for t in range(2) for k in range(4)]
    outs[6][...] = choose(pieces, mine).reshape(size)


def join_att_call(me, owned, features, pieces):
    sizes = (features // 8,) * 5 + (3 * features // 8, features // 2, features // 8)
    return pl.pallas_call(
        join_att_kernel,
        out_shape=(
            jax.ShapeDtypeStruct((owned, 3 * features), wide),
            jax.ShapeDtypeStruct((owned, features), wide),
        )
        + tuple(jax.ShapeDtypeStruct((n,), wide) for n in sizes),
        in_specs=[in_smem] + [in_vmem] * 4,
        out_specs=(in_vmem,) * 10,
        scratch_shapes=[pltpu.VMEM((4, owned // 4, 128), wide), pltpu.VMEM((8, 3 * features), wide)],
        name="join_qkv_gradient",
    )(me, *pieces)


def finish_kernel(first, count, x_ref, cot_ref, vecs, *refs):
    out, grad = refs[-2:]
    for k in range(count):
        mine, got, over = refs[3 * k : 3 * k + 3]
        s = first + k
        spot = k if x_ref.shape[0] == count else s
        x = x_ref[spot].astype(wide)
        total = mine[0].astype(wide) + got[0].astype(wide) + over[0].astype(wide)
        out[spot] = (x + total + vecs[4:5, :]).astype(low)
        e = mine[1].astype(wide) + got[1].astype(wide) + over[1].astype(wide)
        center = x - jnp.mean(x, axis=-1, keepdims=True)
        spread = jnp.mean(center * center, axis=-1, keepdims=True)
        root = lax.rsqrt(spread + epsilon)
        n = center * root
        back = root * (e - jnp.mean(e, axis=-1, keepdims=True) - n * jnp.mean(e * n, axis=-1, keepdims=True))
        grad[spot] = (cot_ref[spot].astype(wide) + back).astype(low)


def finish_call(first, tokens, cotangent, vecs, triples, before=None):
    count, shape = len(triples), jax.ShapeDtypeStruct(tokens.shape, low)
    block = pl.BlockSpec((count, *tokens.shape[1:]), lambda i: (first // count, 0, 0))
    assert first % count == 0
    whole = [pl.BlockSpec(v.shape, lambda i, d=v.ndim: (0,) * d) for v in (vecs, *sum(triples, ()))]
    operands = [tokens, cotangent, vecs, *sum(triples, ())]
    specs = [block, block, *whole]
    aliases = {}
    if before is not None:
        aliases = {len(operands): 0, len(operands) + 1: 1}
        operands += list(before)
        specs += [anywhere, anywhere]
    return pl.pallas_call(
        partial(finish_kernel, first, count),
        grid=(1,),
        out_shape=(shape, shape),
        in_specs=specs,
        out_specs=(block, block),
        input_output_aliases=aliases,
        name="finish_tokens",
    )(*operands)


def shards(
    tokens,
    segment,
    ln1_gain,
    ln1_bias,
    qkv_weight,
    qkv_bias,
    out_weight,
    out_bias,
    ln2_gain,
    ln2_bias,
    fc_weight,
    fc_bias,
    proj_weight,
    proj_bias,
    cotangent,
):
    ctx, fsdp, rep = lax.axis_size("ctx"), lax.axis_size("fsdp"), lax.axis_size("rep")
    c, f, r = lax.axis_index("ctx"), lax.axis_index("fsdp"), lax.axis_index("rep")
    paired = fsdp == 2 and ctx == 4 and rep == 4
    seqs, local_len, features = tokens.shape
    length = local_len * ctx
    owned = qkv_weight.shape[0]
    hidden_own = proj_weight.shape[0]
    hidden_all = fc_weight.shape[1]
    hidden = hidden_all // ctx
    part = features // ctx
    me = f * ctx + c
    core = c & 1

    half = ROT // 2
    inverse = (1.0 / np.float32(10000.0) ** (np.arange(0, ROT, 2, dtype=np.float32) / ROT)).astype(np.float32)
    angles = inverse[:, None] * np.arange(length, dtype=np.float32)[None, :]
    cosine, sine = jnp.asarray(np.cos(angles)), jnp.asarray(np.sin(angles))

    def far_rows(s, *before):
        both = jnp.stack([tokens[s], cotangent[s]])
        return swap(after(both, *before) if before else both, "ctx", 2)

    near = (swap(tokens, "ctx", 1), swap(cotangent, "ctx", 1))

    if paired:
        where = jnp.stack([c, f, core, r]).astype(jnp.int32)
        vectors = (ln1_gain, ln1_bias, ln2_gain, ln2_bias, out_bias, proj_bias, qkv_bias, fc_bias)
        proj_x = swap(proj_weight, "fsdp", 1)
        q0, q1, q2, q3, f0, f1, f2, f3 = pack_call(where, qkv_weight, fc_weight, segment, vectors)
        f_got = [swap(f1, "ctx", 1), swap(f2, "ctx", 2), swap(f3, "ctx", 3)]
        far_send = [jnp.stack([tokens[s], cotangent[s]]) for s in range(seqs)]
        f_got, far_send = lax.optimization_barrier((f_got, far_send))
        far = [swap(far_send[0], "ctx", 2)]
        f_half = rows_call(where, owned, (f0, *f_got))
        f_half, proj_x = lax.optimization_barrier((f_half, proj_x))
        f_other = swap(f_half, "fsdp", 1)
        far1 = swap(after(far_send[1], f_half), "ctx", 2)
        far[0], f_other = lax.optimization_barrier((far[0], f_other))
        far_core = [swap(far[0], "ctx", 1)]
        vecs, bias, segs = prep_call(where, owned, part, seqs, length, f_half, f_other)
        proj_pair, fc_pair = (proj_weight, proj_x), (f_half, f_other)
    else:
        zero = jnp.zeros_like(c)
        where = jnp.stack([c, zero, zero, zero]).astype(jnp.int32)

        def whole(v, axes=("fsdp", "ctx")):
            return lax.all_gather(v, axes, axis=0, tiled=True)

        far = [far_rows(s) for s in range(seqs)]
        far_core = [swap(v, "ctx", 1) for v in far]
        bias = pick(whole(qkv_bias).reshape(3, ctx, part).transpose(1, 0, 2), c).astype(wide)
        bias = jnp.broadcast_to(bias.reshape(3 * part, 1), (3 * part, 128))
        b_sum = (whole(out_bias).astype(wide) + whole(proj_bias).astype(wide)).reshape(1, features)
        vecs = [whole(v).astype(wide) for v in (ln1_gain, ln1_bias, ln2_gain, ln2_bias)]
        vecs += [b_sum.reshape(features), pick(whole(fc_bias).reshape(ctx, hidden), c).astype(wide)]
        vecs = jnp.concatenate([jnp.stack(vecs), jnp.zeros((2, features), wide)])
        segs = lax.all_gather(segment.astype(low), "ctx", axis=1, tiled=True).astype(wide)
        segs = jnp.concatenate([segs, jnp.zeros((8 - seqs, length), wide)])

        def halves(v):
            return v[: v.shape[0] // 2], v[v.shape[0] // 2 :]

        out_pair = halves(pick(whole(out_weight).reshape(ctx, part, features), c))
        proj_pair = halves(pick(whole(proj_weight).reshape(ctx, hidden, features), c))
        qkv_pair = pick(whole(qkv_weight).reshape(features, 3, ctx, part).transpose(2, 0, 1, 3), c)
        qkv_pair = halves(qkv_pair.reshape(features, 3 * part))
        fc_pair = halves(pick(whole(fc_weight).reshape(features, ctx, hidden).transpose(1, 0, 2), c))

    def run_ff(s, args, acc, part_in, is_last):
        send, keep, *grads = ff_call(s, where, args, *fc_pair, *proj_pair, vecs, acc, part_in, is_last)
        return (send, keep), grads

    def run_att(s, args, weights, acc, part_in, vec=None):
        send_near, keep_near, send_far, keep_far, *grads = att_call(
            s, where, args, *weights[0], bias, *weights[1], vecs, segs, cosine, sine, acc, part_in, vec
        )
        return (send_near, keep_near, send_far, keep_far), grads

    def chip_sum(send, keep):
        return (keep.astype(wide) + swap(send, "ctx", 1).astype(wide)).astype(low)

    def to_rep(pieces):
        return [swap(piece, "rep", k) for k, piece in zip(range(1, rep), pieces)]

    def to_ctx(pieces):
        return [swap(piece, "ctx", k) for k, piece in zip(range(1, ctx), pieces)]

    def add_up(first, others):
        total = first
        for value in others:
            total = total + value.astype(wide)
        return total.astype(low)

    phase = lax.optimization_barrier
    if paired:
        args = (tokens, cotangent, *near, far[0], far_core[0])
        far_send, q1, q2, q3, out_send, args = phase((far_send, q1, q2, q3, out_weight, args))
        q_got = [swap(q1, "ctx", 1), swap(q2, "ctx", 2), swap(q3, "ctx", 3)]
        out_x = swap(out_send, "fsdp", 1)
        part0, acc = run_ff(0, args, None, None, False)

        part0, acc, far1, q_got, far_send, out_x = phase((part0, acc, far1, q_got, far_send, out_x))
        far2 = swap(far_send[2], "ctx", 2)
        out_keep = jnp.where(core == f, out_weight, out_x)
        out_got = swap(jnp.where(core == f, out_x, out_weight), "ctx", 1)
        far1_core = swap(far1, "ctx", 1)
        part1, acc = run_ff(1, (tokens, cotangent, *near, far1, far1_core), acc, None, False)

        part1, acc, far2, q_got, out_got, out_keep = phase((part1, acc, far2, q_got, out_got, out_keep))
        q_half = rows_call(where, owned, (q0, *q_got))
        far2_core = swap(far2, "ctx", 1)
        far2_core, q_half, acc = phase((far2_core, q_half, acc))
        q_other = swap(q_half, "fsdp", 1)
        part2, ff_last = run_ff(2, (tokens, cotangent, *near, far2, far2_core), acc, None, True)

        part0, ff_last, q_other = phase((part0, ff_last, q_other))
        att_weights = ((q_half, q_other), (out_keep, out_got))
        ff_got = swap(ff_last[1], "fsdp", 1)
        args = (tokens, cotangent, *near, far[0], far_core[0])
        part0, att_acc = run_att(0, args, att_weights, None, part0)

        part0, att_acc, ff_got = phase((part0, att_acc, ff_got))
        ff_pieces = split_call(where, ff_last[0], ff_got)
        away = chip_sum(*part0[2:])
        ff_pieces, part0, away, part1, att_acc = phase((ff_pieces, part0, away, part1, att_acc))
        ff_got = to_rep(ff_pieces[1:])
        over0 = swap(away, "ctx", 2)
        got0 = swap(part0[0], "ctx", 1)
        args = (tokens, cotangent, *near, far1, far1_core)
        part1, att_acc = run_att(1, args, att_weights, att_acc, part1)

        part1, att_acc, ff_got, over0, got0 = phase((part1, att_acc, ff_got, over0, got0))
        ff_total = add_up(ff_pieces[0], ff_got)
        away = chip_sum(*part1[2:])
        ff_total, part1, away, part2, att_acc = phase((ff_total, part1, away, part2, att_acc))
        ff_got = to_rep([ff_total] * (rep - 1))
        over1 = swap(away, "ctx", 2)
        got1 = swap(part1[0], "ctx", 1)
        args = (tokens, cotangent, *near, far2, far2_core)
        part2, att_last = run_att(2, args, att_weights, att_acc, part2, ff_last[2])

        part2, att_last, ff_got, over1, got1 = phase((part2, att_last, ff_got, over1, got1))
        flat = [(k, i) for k in range(fsdp) for i in range(ctx)]
        messages = [att_last[0]]
        for g, h in flat[1:]:
            peers = [(k * ctx + i, (k ^ g) * ctx + (i ^ h)) for k, i in flat]
            messages.append(lax.ppermute(att_last[g * ctx + h], ("fsdp", "ctx"), peers))
        pairs = [(k, i, 1 - k, i) if (i & 1) != k else (k, i, k, i ^ 1) for k, i in flat]
        near_got = lax.ppermute(att_last[9], ("fsdp", "ctx"), [(a * ctx + b, d * ctx + e) for a, b, d, e in pairs])
        pairs = [(k * ctx + i, (1 - k) * ctx + (i ^ 1)) for k, i in flat if (i & 1) != k]
        far_got = lax.ppermute(att_last[10], ("fsdp", "ctx"), pairs)
        away = chip_sum(*part2[2:])
        messages, near_got, far_got, part2, away, ff_got = phase(
            (messages, near_got, far_got, part2, away, ff_got)
        )

        pieces = meet_call(where, messages, (att_last[8], near_got, far_got))
        pieces, away, part2 = phase((pieces, away, part2))
        got = to_rep(pieces[1:])
        over2 = swap(away, "ctx", 2)
        got2 = swap(part2[0], "ctx", 1)
        *ff_blocks, g_proj = spread_call(where, owned, hidden_own, (ff_total, *ff_got))
        done = finish_call(0, tokens, cotangent, vecs, [(part0[1], got0, over0), (part1[1], got1, over1)])
        got, over2, got2, ff_blocks, done = phase((got, over2, got2, ff_blocks, done))

        piece = add_up(pieces[0], got)
        piece, over2, got2, ff_blocks, done = phase((piece, over2, got2, ff_blocks, done))
        others = to_rep([piece] * (rep - 1))
        ff_blocks_got = to_ctx(ff_blocks[1:])
        output, grad_tokens = finish_call(2, tokens, cotangent, vecs, [(part2[1], got2, over2)], done)
        g_fc = join_ff_call(where, (ff_blocks[0], *ff_blocks_got))
        g_qkv, g_out, *vector_grads = join_att_call(where, owned, features, (piece, *others))
    else:
        att_acc = ff_acc = None
        done = None
        for s in range(seqs):
            args = (tokens, cotangent, *near, far[s], far_core[s])
            parts, ff_acc = run_ff(s, args, ff_acc, None, s == seqs - 1)
            vec = ff_acc[2] if s == seqs - 1 else None
            parts, att_acc = run_att(s, args, (qkv_pair, out_pair), att_acc, parts, vec)
            over = swap(chip_sum(*parts[2:]), "ctx", 2)
            done = finish_call(s, tokens, cotangent, vecs, [(parts[1], swap(parts[0], "ctx", 1), over)], done)
        output, grad_tokens = done

        def any_columns(kept, sent):
            grad = jnp.concatenate([kept.astype(low), sent])
            grad = lax.psum_scatter(grad, "fsdp", scatter_dimension=0, tiled=True)
            grad = lax.psum(grad, "rep").reshape(ctx, owned, -1)
            return lax.all_to_all(grad, "ctx", split_axis=0, concat_axis=0)

        def any_rows(kept, sent):
            grad = jnp.concatenate([kept.astype(low), sent])
            grad = jnp.where(jnp.arange(ctx)[:, None, None] == c, grad[None], 0).reshape(-1, features)
            return lax.psum(
                lax.psum_scatter(grad, ("fsdp", "ctx"), scatter_dimension=0, tiled=True), "rep"
            )

        cut = features // 2
        g_fc = any_columns(ff_acc[0][:cut], ff_acc[1][:cut])
        g_fc = g_fc.transpose(1, 0, 2).reshape(owned, hidden_all)
        g_proj = any_rows(ff_acc[0][cut:], ff_acc[1][cut:])
        sent = jnp.concatenate([att_acc[0][None].astype(low), jnp.stack(att_acc[1:8])])
        whole_w = jnp.concatenate(in_order([v[: part // 2] for v in sent], c))
        g_qkv = any_columns(whole_w[: features // 2], whole_w[features // 2 :]).reshape(ctx, owned, 3, part)
        g_qkv = g_qkv.transpose(1, 2, 0, 3).reshape(owned, 3 * features)
        g_out = any_rows(*att_acc[8:10])
        vec = att_acc[0][part // 2 :]
        vec = jnp.concatenate([vec[:8], vec[8:, : features - 3 * part]], axis=1)
        total_vec = jnp.zeros((16, features), wide).at[0:5].set(vec[0:5])
        total_vec = lax.dynamic_update_slice(total_vec, vec[5:6], (5 + c, 0))
        total_vec = lax.dynamic_update_slice(total_vec, vec[6:7], (9 + c, 0))
        total_vec = lax.psum(total_vec, ("ctx", "fsdp", "rep"))
        grads = [total_vec[k] for k in range(5)]
        grads.append(total_vec[9 : 9 + ctx, : 3 * part].reshape(ctx, 3, part).transpose(1, 0, 2).reshape(-1))
        grads.append(total_vec[5 : 5 + ctx, :hidden].reshape(-1))
        grads.append(total_vec[4])
        vector_grads = []
        for v in grads:
            size = v.shape[0] // (fsdp * ctx)
            vector_grads.append(lax.dynamic_slice(v, (me * size,), (size,)))
    g_gain_one, g_shift_one, g_gain_two, g_shift_two, g_b_out, g_b_qkv, g_b_fc, g_b_proj = vector_grads
    return (
        output,
        grad_tokens,
        g_gain_one,
        g_shift_one,
        g_qkv.astype(wide),
        g_b_qkv,
        g_out.astype(wide),
        g_b_out,
        g_gain_two,
        g_shift_two,
        g_fc.astype(wide),
        g_b_fc,
        g_proj.astype(wide),
        g_b_proj,
    )


def solution(mesh):
    rows, row = P(("rep", "fsdp"), "ctx", None), P(("rep", "fsdp"), "ctx")
    vector, matrix = P(("fsdp", "ctx")), P(("fsdp", "ctx"), None)
    params = (
        vector, vector, matrix, vector, matrix, vector,
        vector, vector, matrix, vector, matrix, vector,
    )
    return jax.shard_map(
        shards,
        mesh=mesh,
        in_specs=(rows, row, *params, rows),
        out_specs=(rows, rows, *params),
        check_vma=False,
    )
```

```python
from functools import partial
import math

import jax
import jax.numpy as jnp
import numpy as np
from jax import lax
from jax.experimental import pallas as pl
from jax.experimental.pallas import tpu as pltpu
from jax.sharding import PartitionSpec as P

HEADS = 12
HEAD = 64
ROT = 16

epsilon = 1e-05
far_below = -1e30
low = jnp.bfloat16
wide = jnp.float32
log2e = math.log2(math.e)


def nn(a, b):
    return lax.dot_general(a, b, (((1,), (0,)), ((), ())), preferred_element_type=wide)


def nt(a, b):
    return lax.dot_general(a, b, (((1,), (1,)), ((), ())), preferred_element_type=wide)


def swap(value, axis, bits):
    size = lax.axis_size(axis)
    return lax.ppermute(value, axis, [(i, i ^ bits) for i in range(size)])


def in_order(rel, me):
    out = []
    for k in range(len(rel)):
        value = rel[k]
        for m in range(1, len(rel)):
            value = jnp.where(me == m, rel[k ^ m], value)
        out.append(value)
    return out


def pick(stacked, index):
    return lax.dynamic_index_in_dim(stacked, index, 0, keepdims=False)


def after(value, *before):
    return lax.optimization_barrier((value, before))[0]


anywhere = pl.BlockSpec(memory_space=pltpu.HBM)
in_vmem = pl.BlockSpec(memory_space=pltpu.VMEM)
in_smem = pl.BlockSpec(memory_space=pltpu.SMEM)
extra_rows = 16


def head_block(index):
    return ((index & 1) << 1) | (index >> 1)


def pack_kernel(vectors, me_ref, qkv, fc, segment, *refs):
    vector_refs, refs = refs[:vectors], refs[vectors:]
    q0, q1, q2, q3, f0, f1, f2, f3, scratch, extra = refs
    c = me_ref[0]
    owned, part, unit = qkv.shape[0], qkv.shape[1] // 12, fc.shape[1] // 8
    extra[...] = jnp.zeros_like(extra)
    for row, ref in enumerate(vector_refs):
        extra[row : row + 1, 0 : ref.shape[0]] = ref[...].astype(wide).reshape(1, -1)
    extra[8 : 8 + segment.shape[0], 0 : segment.shape[1]] = segment[...].astype(wide)
    for k in range(4):
        block = head_block(k)
        for t in range(3):
            lo = (4 * t + block) * part
            scratch[k ^ c, :, t * part : (t + 1) * part] = qkv[:, lo : lo + part]
    for k, (q, g) in enumerate(((q0, f0), (q1, f1), (q2, f2), (q3, f3))):
        q[...] = scratch[k]
        for t in range(2):
            lo = pl.multiple_of((4 * t + (c ^ k)) * unit, 128)
            g[0:owned, t * unit : (t + 1) * unit] = fc[:, pl.ds(lo, unit)]
        g[owned:, :] = extra[...].astype(low)


def pack_call(me, qkv, fc, segment, vectors):
    owned = qkv.shape[0]
    narrow, broad = (owned, qkv.shape[1] // 4), (owned + extra_rows, fc.shape[1] // 4)
    shapes = (narrow,) * 4 + (broad,) * 4
    return pl.pallas_call(
        partial(pack_kernel, len(vectors)),
        out_shape=tuple(jax.ShapeDtypeStruct(s, low) for s in shapes),
        in_specs=[in_smem] + [in_vmem] * (3 + len(vectors)),
        out_specs=(in_vmem,) * 8,
        scratch_shapes=[
            pltpu.VMEM((4, owned, narrow[1]), low),
            pltpu.VMEM((extra_rows, broad[1]), wide),
        ],
        name="pack_columns",
    )(me, qkv, fc, segment, *vectors)


def rows_kernel(owned, me_ref, p0, p1, p2, p3, half):
    c = me_ref[0]
    tail = p0.shape[0] - owned
    for k, p in enumerate((p0, p1, p2, p3)):
        half[pl.ds(pl.multiple_of((c ^ k) * owned, 16), owned), :] = p[0:owned, :]
        if tail:
            half[pl.ds(pl.multiple_of(4 * owned + (c ^ k) * tail, 16), tail), :] = p[owned:, :]


def rows_call(me, owned, pieces):
    rows, cols = pieces[0].shape
    return pl.pallas_call(
        partial(rows_kernel, owned),
        out_shape=jax.ShapeDtypeStruct((4 * rows, cols), low),
        in_specs=[in_smem] + [in_vmem] * 4,
        out_specs=in_vmem,
        name="rows_by_ctx",
    )(me, *pieces)


def prep_kernel(owned, part, seqs, me_ref, mine, other, vecs, bias, seg):
    c, f = me_ref[0], me_ref[1]
    extra_mine, extra_other = mine[...].astype(wide), other[...].astype(wide)
    first = jnp.where(f == 0, extra_mine, extra_other)
    last = jnp.where(f == 0, extra_other, extra_mine)

    def vector(row, size):
        pieces = [
            e[k * extra_rows + row : k * extra_rows + row + 1, 0:size]
            for e in (first, last)
            for k in range(4)
        ]
        return jnp.concatenate(pieces, axis=1)

    block = head_block(c)
    vecs[...] = jnp.zeros_like(vecs)
    for row in range(4):
        vecs[row : row + 1, :] = vector(row, owned)
    vecs[4:5, :] = vector(4, owned) + vector(5, owned)
    unit = mine.shape[1] // 2
    for t, e in enumerate((first, last)):
        chosen = e[7:8, 0:unit]
        for k in range(1, 4):
            chosen = jnp.where(c == k, e[k * extra_rows + 7 : k * extra_rows + 8, 0:unit], chosen)
        vecs[5:6, t * unit : (t + 1) * unit] = chosen
    all_qkv = vector(6, 3 * owned)
    picked = []
    for t in range(3):
        chosen = all_qkv[:, 4 * t * part : (4 * t + 1) * part]
        for k in range(1, 4):
            chosen = jnp.where(block == k, all_qkv[:, (4 * t + k) * part : (4 * t + k + 1) * part], chosen)
        picked.append(chosen)
    row_bias = jnp.concatenate(picked, axis=1)
    bias[...] = jnp.transpose(jnp.broadcast_to(row_bias, (128, 3 * part)))
    seg[...] = jnp.zeros_like(seg)
    width = seg.shape[1] // 4
    for s in range(seqs):
        for k in range(4):
            row = k * extra_rows + 8 + s
            seg[s : s + 1, k * width : (k + 1) * width] = extra_mine[row : row + 1, 0:width]


def prep_call(me, owned, part, seqs, length, mine, other):
    tail = pl.BlockSpec((4 * extra_rows, mine.shape[1]), lambda i: (4 * owned // (4 * extra_rows), 0))
    assert 4 * owned % (4 * extra_rows) == 0
    shapes = ((8, 8 * owned), (3 * part, 128), (8, length))
    return pl.pallas_call(
        partial(prep_kernel, owned, part, seqs),
        grid=(1,),
        out_shape=tuple(jax.ShapeDtypeStruct(s, wide) for s in shapes),
        in_specs=[in_smem, tail, tail],
        out_specs=tuple(pl.BlockSpec(s, lambda i: (0, 0)) for s in shapes),
        name="prepare_vectors",
    )(me, mine, other)


def row_norm(block):
    values = block.astype(wide)
    center = values - jnp.mean(values, axis=-1, keepdims=True)
    spread = jnp.mean(center * center, axis=-1, keepdims=True)
    return center * lax.rsqrt(spread + epsilon)


def gelu_parts(v):
    bell = jnp.exp2(v * v * (-0.5 * log2e))
    base = 1.0 + (0.3275911 / math.sqrt(2.0)) * jnp.abs(v)
    t = pl.reciprocal(base, approx=True)
    t = t * (2.0 - base * t)
    poly = 0.5 * 1.061405429
    for coef in (-1.453152027, 1.421413741, -0.284496736, 0.254829592):
        poly = poly * t + 0.5 * coef
    tail = poly * t * bell
    phi = jnp.where(v >= 0, 1.0 - tail, tail)
    return phi, phi + v * bell * (1.0 / math.sqrt(2.0 * math.pi))


def bring(pairs, sem):
    copies = [pltpu.make_async_copy(a, b, sem.at[k]) for k, (a, b) in enumerate(pairs)]
    for copy in copies:
        copy.start()
    return copies


def token_pairs(s, refs, xs, cs):
    tok, cot, tok1, cot1, far, far1 = refs
    pairs = []
    for j, (t, c) in enumerate(
        ((tok.at[s], cot.at[s]), (tok1.at[s], cot1.at[s]), (far.at[0], far.at[1]), (far1.at[0], far1.at[1]))
    ):
        pairs += [(t, xs.at[j]), (c, cs.at[j])]
    return pairs


def ff_kernel(s, with_acc, with_part, is_last, *refs):
    me_ref, refs = refs[0], refs[1:]
    token_refs, refs = refs[:6], refs[6:]
    fc_a, fc_b, proj_a, proj_b, vecs = refs[:5]
    refs = refs[5:]
    if with_acc:
        acc_fc_in, acc_proj_in, acc_vec_in = refs[:3]
        refs = refs[3:]
    if with_part:
        part_send, part_keep = refs[:2]
        refs = refs[2:]
    send, keep = refs[:2]
    refs = refs[2:]
    if is_last:
        grad_keep, grad_send, vec = refs[:3]
        refs = refs[3:]
    else:
        fc_out, proj_out, vec = refs[:3]
        refs = refs[3:]
    xs, cs, fc, proj, sec_s, hid_s, gp_s, send_s, keep_s, acc_fc, acc_proj, sem, sem_w, sem_p, sem_o = refs[:15]
    if is_last:
        stage_keep, stage_send = refs[15:]
    f = me_ref[1]
    blocks, rows, features = xs.shape
    hidden = fc.shape[1]
    third, half = features // 2, proj_a.shape[0]
    tokens_in = bring(token_pairs(s, token_refs, xs, cs), sem)
    weights_in = bring(
        [
            (fc_a.at[0:third], fc.at[pl.ds(pl.multiple_of(f * third, 16), third), :]),
            (fc_b.at[0:third], fc.at[pl.ds(pl.multiple_of((1 - f) * third, 16), third), :]),
            (proj_a, proj.at[pl.ds(pl.multiple_of(f * half, 16), half), :]),
            (proj_b, proj.at[pl.ds(pl.multiple_of((1 - f) * half, 16), half), :]),
        ],
        sem_w,
    )
    later = []
    if with_part:
        later += [(part_send, send_s), (part_keep, keep_s)]
    if with_acc:
        later += [(acc_fc_in, acc_fc), (acc_proj_in, acc_proj)]
    later = bring(later, sem_p)
    for copy in weights_in + tokens_in:
        copy.wait()
    gain, shift, bias = vecs[2:3, :], vecs[3:4, :], vecs[5:6, 0:hidden]
    dgain = jnp.zeros((1, features), wide)
    dshift = jnp.zeros((1, features), wide)
    dbias = jnp.zeros((1, hidden), wide)
    if with_part:
        later[0].wait()
        later[1].wait()
    for j in range(blocks):
        here = pl.ds(j * rows, rows)
        n = row_norm(xs[j])
        second = (n * gain + shift).astype(low)
        sec_s[here, :] = second
        cot = cs[j]
        pre = nn(second, fc[...]) + bias
        phi, slope = gelu_parts(pre)
        hid = (pre * phi).astype(low)
        gp = nt(cot, proj[...]) * slope
        dbias = dbias + jnp.sum(gp, axis=0, keepdims=True)
        gp = gp.astype(low)
        hid_s[here, :] = hid
        gp_s[here, :] = gp
        out = nn(hid, proj[...])
        dsec = nt(gp, fc[...])
        dgain = dgain + jnp.sum(dsec * n, axis=0, keepdims=True)
        dshift = dshift + jnp.sum(dsec, axis=0, keepdims=True)
        e = dsec * gain
        to = send_s if j % 2 else keep_s
        if with_part:
            out = out + to[j // 2 * 2].astype(wide)
            e = e + to[j // 2 * 2 + 1].astype(wide)
        to[j // 2 * 2] = out.astype(low)
        to[j // 2 * 2 + 1] = e.astype(low)
    results = bring([(send_s, send), (keep_s, keep)], sem_o)
    dcot = jnp.sum(cs[0].astype(wide), axis=0, keepdims=True)
    if with_acc:
        for copy in later[-2:]:
            copy.wait()
        dgain = dgain + acc_vec_in[0:1, :]
        dshift = dshift + acc_vec_in[1:2, :]
        dbias = dbias + acc_vec_in[2:3, 0:hidden]
        dcot = dcot + acc_vec_in[3:4, :]
    every_cot = cs[...].reshape(blocks * rows, features)
    for k, (acc, a, b, own) in enumerate(((acc_fc, sec_s, gp_s[...], third), (acc_proj, hid_s, every_cot, half))):
        grad = nn(jnp.transpose(a[...]), b)
        acc[...] = grad + acc[...] if with_acc else grad
        if is_last:
            lo = k * third
            stage_keep[lo : lo + own, :] = acc[pl.ds(pl.multiple_of(f * own, 16), own), :].astype(low)
            stage_send[lo : lo + own, :] = acc[pl.ds(pl.multiple_of((1 - f) * own, 16), own), :].astype(low)
            moves = [(stage_keep, grad_keep), (stage_send, grad_send)]
            moves = [(x.at[lo : lo + own], y.at[lo : lo + own]) for x, y in moves]
        else:
            moves = [(acc, (fc_out, proj_out)[k])]
        for x, y in moves:
            results.append(pltpu.make_async_copy(x, y, sem_o.at[len(results)]))
            results[-1].start()
    vec[0:1, :] = dgain
    vec[1:2, :] = dshift
    vec[2:3, 0:hidden] = dbias
    vec[3:4, :] = dcot
    for copy in results:
        copy.wait()


def ff_call(s, me, token_args, fc_a, fc_b, proj_a, proj_b, vecs, acc, part, is_last):
    rows, features = token_args[0].shape[1:]
    hidden, blocks = fc_a.shape[1], 4
    total = blocks * rows
    third = features // 2
    operands = [me, *token_args, fc_a, fc_b, proj_a, proj_b, vecs]
    specs = [in_smem] + [anywhere] * 10 + [in_vmem]
    aliases = {}
    if acc is not None:
        if not is_last:
            aliases = {len(operands): 2, len(operands) + 1: 3}
        operands += list(acc)
        specs += [anywhere, anywhere, in_vmem]
    if part is not None:
        aliases[len(operands)] = 0
        aliases[len(operands) + 1] = 1
        operands += list(part)
        specs += [anywhere, anywhere]
    shared = jax.ShapeDtypeStruct((4, rows, features), low)
    vec = jax.ShapeDtypeStruct((8, features), wide)
    if is_last:
        rows_out = third + proj_a.shape[0]
        grads = (
            jax.ShapeDtypeStruct((rows_out, features), low),
            jax.ShapeDtypeStruct((rows_out, features), low),
        )
        grad_specs = (anywhere,) * 2
        more = [pltpu.VMEM((rows_out, features), low)] * 2
    else:
        grads = (
            jax.ShapeDtypeStruct((features, hidden), wide),
            jax.ShapeDtypeStruct((hidden, features), wide),
        )
        grad_specs, more = (anywhere,) * 2, []
    return pl.pallas_call(
        partial(ff_kernel, s, acc is not None, part is not None, is_last),
        out_shape=(shared, shared, *grads, vec),
        in_specs=specs,
        out_specs=(anywhere, anywhere, *grad_specs, in_vmem),
        scratch_shapes=[
            pltpu.VMEM((blocks, rows, features), low),
            pltpu.VMEM((blocks, rows, features), low),
            pltpu.VMEM((features, hidden), low),
            pltpu.VMEM((hidden, features), low),
            pltpu.VMEM((total, features), low),
            pltpu.VMEM((total, hidden), low),
            pltpu.VMEM((total, hidden), low),
            pltpu.VMEM((4, rows, features), low),
            pltpu.VMEM((4, rows, features), low),
            pltpu.VMEM((features, hidden), wide),
            pltpu.VMEM((hidden, features), wide),
            pltpu.SemaphoreType.DMA((8,)),
            pltpu.SemaphoreType.DMA((4,)),
            pltpu.SemaphoreType.DMA((4,)),
            pltpu.SemaphoreType.DMA((8,)),
            *more,
        ],
        input_output_aliases=aliases,
        compiler_params=pltpu.CompilerParams(vmem_limit_bytes=50 * 2**20),
        cost_estimate=pl.CostEstimate(flops=1, bytes_accessed=1, transcendentals=0),
        name="feed_forward",
    )(*operands)


def turn(block, cosine, sine):
    half = ROT // 2
    a, b = block[0:half], block[half:ROT]
    return jnp.concatenate([a * cosine - b * sine, b * cosine + a * sine, block[ROT:]], axis=0)


def att_kernel(s, heads, with_acc, with_part, is_last, *refs):
    me_ref, refs = refs[0], refs[1:]
    token_refs, refs = refs[:6], refs[6:]
    w_a, w_b, bias, wout_a, wout_b, vecs, segs, cosine, sine = refs[:9]
    refs = refs[9:]
    if is_last:
        ff_vec, refs = refs[0], refs[1:]
    if with_acc:
        acc_w_in, acc_o_in, acc_vec_in = refs[:3]
        refs = refs[3:]
    if with_part:
        part_send, part_keep = refs[:2]
        refs = refs[2:]
    homes, refs = refs[:4], refs[4:]
    if is_last:
        messages, (o_keep, o_send, o_send_far) = refs[:8], refs[8:11]
        refs = refs[11:]
    else:
        w_out, o_out, vec = refs[:3]
        refs = refs[3:]
    xs, cs, wt_s, wout, first_s, n_s, cot_s, qt_s, kt_s, vt_s, k_s, v_s, dot_s, mask_s, att_s, d_s, dk_s, dv_s = refs[:18]
    send_s, keep_s, acc_w, acc_o, sem, sem_p, sem_o = refs[18:25]
    if is_last:
        by_rows = refs[25]
    me, f, core = me_ref[0], me_ref[1], me_ref[2]
    blocks, rows, features = xs.shape
    part = heads * HEAD
    length = blocks * rows
    reach = length // 2
    scale = 1.0 / math.sqrt(HEAD)
    tokens_in = bring(token_pairs(s, token_refs, xs, cs), sem)
    gain, shift = vecs[0:1, :], vecs[1:2, :]
    share = w_a.shape[0]
    wt_s[:, pl.ds(pl.multiple_of(f * share, 128), share)] = jnp.transpose(w_a[...])
    wt_s[:, pl.ds(pl.multiple_of((1 - f) * share, 128), share)] = jnp.transpose(w_b[...])
    owned = wout_a.shape[0]
    wout[pl.ds(pl.multiple_of(core * owned, 16), owned), :] = wout_a[...]
    wout[pl.ds(pl.multiple_of((1 - core) * owned, 16), owned), :] = wout_b[...]

    seg_row = segs[s : s + 1, :]
    seg_col = jnp.transpose(jnp.broadcast_to(seg_row, (128, length)))
    spans, place = [], 0
    for i in range(blocks):
        start = max(0, i * rows - reach)
        count = (i + 1) * rows - start
        spans.append((start, count, place))
        ours = seg_row[:, i * rows : (i + 1) * rows]
        theirs = seg_col[start : start + count]
        theirs = jnp.concatenate([theirs] * (rows // 128), axis=1)
        key = start + lax.broadcasted_iota(jnp.int32, (count, rows), 0)
        query = i * rows + lax.broadcasted_iota(jnp.int32, (count, rows), 1)
        allowed = (theirs == ours) & (key <= query)
        mask_s[place : place + count, :] = jnp.where(allowed, 0.0, far_below)
        place += count

    for copy in tokens_in:
        copy.wait()
    wide_bias = jnp.concatenate([bias[...]] * (rows // 128), axis=1)
    for j in range(blocks):
        off = pl.multiple_of((me ^ j) * rows, rows)
        n = row_norm(xs[j])
        n_s[pl.ds(off, rows), :] = n.astype(low)
        first = (n * gain + shift).astype(low)
        first_s[pl.ds(off, rows), :] = first
        cot = cs[j]
        cot_s[pl.ds(off, rows), :] = cot
        cos_b, sin_b = cosine[:, pl.ds(off, rows)], sine[:, pl.ds(off, rows)]
        made = nt(wt_s[...], first) + wide_bias
        for h in range(heads):
            lo, hi = h * HEAD, (h + 1) * HEAD
            query = turn(made[lo:hi], cos_b, sin_b).astype(low)
            qt_s[lo:hi, pl.ds(off, rows)] = (query.astype(wide) * scale).astype(low)
            key = turn(made[part + lo : part + hi], cos_b, sin_b).astype(low)
            kt_s[lo:hi, pl.ds(off, rows)] = key
            value = made[2 * part + lo : 2 * part + hi].astype(low)
            vt_s[lo:hi, pl.ds(off, rows)] = value
            k_s[h, pl.ds(off, rows), :] = jnp.transpose(key)
            v_s[h, pl.ds(off, rows), :] = jnp.transpose(value)
        dot_s[:, pl.ds(off, rows)] = nt(wout[...], cot).astype(low)

    later = []
    if with_part:
        later += [(part_send, send_s), (part_keep, keep_s)]
    if with_acc:
        later += [(acc_w_in, acc_w), (acc_o_in, acc_o)]
    later = bring(later, sem_p)
    dk_s[...] = jnp.zeros_like(dk_s)
    dv_s[...] = jnp.zeros_like(dv_s)

    def one_head(h, carry):
        base = pl.multiple_of(h * HEAD, HEAD)
        mine = pl.ds(base, HEAD)
        for i in range(blocks):
            start, count, place = spans[i]
            here, there = slice(i * rows, (i + 1) * rows), slice(start, start + count)
            query, grad = qt_s[mine, here], dot_s[mine, here]
            score = nn(k_s[h, there, :], query) + mask_s[place : place + count, :]
            top = jnp.max(score, axis=0, keepdims=True)
            lifted = jnp.exp2((score - top) * log2e)
            total = jnp.sum(lifted, axis=0, keepdims=True)
            prob = lifted * (1.0 / total)
            prob_low = prob.astype(low)
            att_s[mine, here] = nn(vt_s[mine, there], prob_low).astype(low)
            dprob = nn(v_s[h, there, :], grad)
            inner = jnp.sum(prob * dprob, axis=0, keepdims=True)
            dscore = (prob * (dprob - inner)).astype(low)
            dv_s[mine, there] += nt(grad, prob_low)
            dk_s[mine, there] += nt(query, dscore)
            dq = nn(kt_s[mine, there], dscore) * scale
            cos_b, sin_b = cosine[:, here], sine[:, here]
            d_s[mine, here] = turn(dq, cos_b, -sin_b).astype(low)
        return carry

    lax.fori_loop(0, heads, one_head, 0, unroll=True)
    for h in range(heads):
        lo, hi = h * HEAD, (h + 1) * HEAD
        d_s[part + lo : part + hi, :] = turn(dk_s[lo:hi, :], cosine[...], -sine[...]).astype(low)
    d_s[2 * part : 3 * part, :] = dv_s[...].astype(low)

    g_w = nn(d_s[...], first_s[...])
    g_o = nn(att_s[...], cot_s[...])
    if with_part:
        later[0].wait()
        later[1].wait()
    if with_acc:
        later[-2].wait()
        later[-1].wait()
        g_w = g_w + acc_w[...]
        g_o = g_o + acc_o[...]
    acc_w[...] = g_w
    results = []
    if is_last:
        by_rows[...] = jnp.transpose(acc_w[...])
        for k, message in enumerate(messages):
            shard = (f ^ (k // 4)) * 4 + (me ^ (k % 4))
            block = by_rows[pl.ds(pl.multiple_of(shard * owned, 8), owned), :]
            message[0:owned, :] = block.astype(message.dtype)
        acc_o[...] = g_o
        mine = acc_o[pl.ds(pl.multiple_of(f * owned, 16), owned), :]
        o_keep[...] = jnp.where(f == core, mine, 0.0)
        o_send[...] = acc_o[pl.ds(pl.multiple_of((1 - f) * owned, 16), owned), :].astype(low)
        o_send_far[...] = mine.astype(low)
    else:
        acc_o[...] = g_o
        results = [
            pltpu.make_async_copy(acc_w, w_out, sem_o.at[2]),
            pltpu.make_async_copy(acc_o, o_out, sem_o.at[3]),
        ]
        for copy in results:
            copy.start()
    dgain = jnp.zeros((1, features), wide)
    dshift = jnp.zeros((1, features), wide)
    dbias = jnp.zeros((8, 3 * part), wide)
    for j in range(blocks):
        off = pl.multiple_of((me ^ j) * rows, rows)
        att = jnp.transpose(att_s[:, pl.ds(off, rows)])
        out = nn(att, wout[...])
        dqkv = jnp.transpose(d_s[:, pl.ds(off, rows)])
        dbias = dbias + nn(jnp.ones((8, rows), low), dqkv)
        dfirst = nn(dqkv, wt_s[...])
        n = n_s[pl.ds(off, rows), :].astype(wide)
        dgain = dgain + jnp.sum(dfirst * n, axis=0, keepdims=True)
        dshift = dshift + jnp.sum(dfirst, axis=0, keepdims=True)
        e = dfirst * gain
        to, first = send_s if j % 2 else keep_s, j // 2 * 2
        if with_part:
            out = out + to[first].astype(wide)
            e = e + to[first + 1].astype(wide)
        to[first] = out.astype(low)
        to[first + 1] = e.astype(low)
        if j % 2:
            for k, (a, b) in enumerate(((send_s, homes[first]), (keep_s, homes[first + 1]))):
                results.append(pltpu.make_async_copy(a.at[first : first + 2], b, sem_o.at[4 + first + k]))
                results[-1].start()
    dbias = dbias[0:1]
    if with_acc:
        dgain = dgain + acc_vec_in[0:1, :]
        dshift = dshift + acc_vec_in[1:2, :]
        dbias = dbias + acc_vec_in[2:3, 0 : 3 * part]
    if is_last:
        cols = 3 * part
        rest = jnp.zeros((1, features - cols), wide)
        vec = jnp.concatenate(
            [dgain, dshift, ff_vec[0:2, :], ff_vec[3:4, :], ff_vec[2:3, :], jnp.concatenate([dbias, rest], axis=1)]
            + [jnp.zeros((1, features), wide)]
        )
        for message in messages:
            message[owned : owned + 8, :] = vec[:, 0:cols].astype(message.dtype)
            message[owned + 8 : owned + 16, 0 : features - cols] = vec[:, cols:].astype(message.dtype)
            message[owned + 8 : owned + 16, features - cols :] = jnp.zeros((8, 2 * cols - features), message.dtype)
    else:
        vec[0:1, :] = dgain
        vec[1:2, :] = dshift
        vec[2:3, 0 : 3 * part] = dbias
    for copy in results:
        copy.wait()


def att_call(s, me, token_args, w_a, w_b, bias, wout_a, wout_b, vecs, segs, cosine, sine, acc, part_in, ff_vec):
    rows, features = token_args[0].shape[1:]
    part, blocks = w_a.shape[1] // 3, 4
    heads = part // HEAD
    length = blocks * rows
    is_last = ff_vec is not None
    operands = [me, *token_args, w_a, w_b, bias, wout_a, wout_b, vecs, segs, cosine, sine]
    operands += [ff_vec] if is_last else []
    specs = [in_smem] + [anywhere] * 6 + [in_vmem] * (len(operands) - 7)
    aliases = {}
    if acc is not None:
        if not is_last:
            aliases = {len(operands): 4, len(operands) + 1: 5}
        operands += list(acc)
        specs += [anywhere, anywhere, in_vmem]
    if part_in is not None:
        operands += list(part_in)
        specs += [anywhere, anywhere]
    shared = jax.ShapeDtypeStruct((2, rows, features), low)
    if is_last:
        message = (part // 2 + 16, 3 * part)
        grads = (jax.ShapeDtypeStruct(message, wide),) + (jax.ShapeDtypeStruct(message, low),) * 7
        grads += (
            jax.ShapeDtypeStruct((part // 2, features), wide),
            jax.ShapeDtypeStruct((part // 2, features), low),
            jax.ShapeDtypeStruct((part // 2, features), low),
        )
        grad_specs = (in_vmem,) * 11
        last_vec, vec_specs = (), ()
        more = [pltpu.VMEM((features, 3 * part), wide)]
    else:
        grads = (
            jax.ShapeDtypeStruct((3 * part, features), wide),
            jax.ShapeDtypeStruct((part, features), wide),
        )
        grad_specs = (anywhere,) * 2
        last_vec, vec_specs, more = (jax.ShapeDtypeStruct((8, features), wide),), (in_vmem,), []
    reach = length // 2
    masked = sum((i + 1) * rows - max(0, i * rows - reach) for i in range(blocks))
    return pl.pallas_call(
        partial(att_kernel, s, heads, acc is not None, part_in is not None, is_last),
        out_shape=(shared,) * 4 + (*grads, *last_vec),
        in_specs=specs,
        out_specs=(anywhere,) * 4 + (*grad_specs, *vec_specs),
        scratch_shapes=[
            pltpu.VMEM((blocks, rows, features), low),
            pltpu.VMEM((blocks, rows, features), low),
            pltpu.VMEM((3 * part, features), low),
            pltpu.VMEM((part, features), low),
            pltpu.VMEM((length, features), low),
            pltpu.VMEM((length, features), low),
            pltpu.VMEM((length, features), low),
            pltpu.VMEM((part, length), low),
            pltpu.VMEM((part, length), low),
            pltpu.VMEM((part, length), low),
            pltpu.VMEM((heads, length, HEAD), low),
            pltpu.VMEM((heads, length, HEAD), low),
            pltpu.VMEM((part, length), low),
            pltpu.VMEM((masked, rows), wide),
            pltpu.VMEM((part, length), low),
            pltpu.VMEM((3 * part, length), low),
            pltpu.VMEM((part, length), wide),
            pltpu.VMEM((part, length), wide),
            pltpu.VMEM((4, rows, features), low),
            pltpu.VMEM((4, rows, features), low),
            pltpu.VMEM((3 * part, features), wide),
            pltpu.VMEM((part, features), wide),
            pltpu.SemaphoreType.DMA((8,)),
            pltpu.SemaphoreType.DMA((4,)),
            pltpu.SemaphoreType.DMA((8,)),
            *more,
        ],
        input_output_aliases=aliases,
        compiler_params=pltpu.CompilerParams(vmem_limit_bytes=56 * 2**20),
        cost_estimate=pl.CostEstimate(flops=1, bytes_accessed=1, transcendentals=0),
        name="attention",
    )(*operands)


def split_kernel(me_ref, keep, got, *refs):
    pieces, both = refs[:4], refs[4]
    r = me_ref[3]
    half = both.shape[0] // 2
    fine, short = half // 16, half // 4
    both[...] = keep[...].astype(wide) + got[...].astype(wide)
    for k, piece in enumerate(pieces):
        cut = r ^ k
        parts = [both[pl.ds(pl.multiple_of(b * 4 * fine + cut * fine, 8), fine), :] for b in range(4)]
        piece[0 : 4 * fine, :] = jnp.concatenate(parts).astype(piece.dtype)
        piece[4 * fine :, :] = both[pl.ds(pl.multiple_of(half + cut * short, 8), short), :].astype(piece.dtype)


def split_call(me, keep, got):
    shape = (keep.shape[0] // 4, keep.shape[1])
    return pl.pallas_call(
        split_kernel,
        out_shape=(jax.ShapeDtypeStruct(shape, wide),) + (jax.ShapeDtypeStruct(shape, low),) * 3,
        in_specs=[in_smem] + [in_vmem] * 2,
        out_specs=(in_vmem,) * 4,
        scratch_shapes=[pltpu.VMEM(keep.shape, wide)],
        name="split_gradients",
    )(me, keep, got)


def meet_kernel(me_ref, *refs):
    messages, (o_keep, o_near, o_far), pieces, (came, rows) = refs[:8], refs[8:11], refs[11:15], refs[15:]
    c, r = me_ref[0], me_ref[3]
    owned, features = o_keep.shape
    cols = came.shape[2]
    part, fine = cols // 3, owned // 4
    for k, message in enumerate(messages):
        came[k] = message[...].astype(wide)
    by_ctx = []
    for k in range(4):
        both = came[c ^ k] + came[4 + (c ^ k)]
        by_ctx.append(both)
        for t in range(3):
            lo = (4 * t + head_block(k)) * part
            rows[:, lo : lo + part] = both[0:owned, t * part : (t + 1) * part]
    rows[:, 3 * features :] = o_keep[...] + o_near[...].astype(wide) + o_far[...].astype(wide)
    vecs = [
        jnp.concatenate([b[owned : owned + 8, :], b[owned + 8 : owned + 16, 0 : features - cols]], axis=1)
        for b in by_ctx
    ]
    shared = (vecs[0] + vecs[1]) + (vecs[2] + vecs[3])
    vec = jnp.concatenate([shared[0:5]] + [v[5:6] for v in vecs] + [v[6:7] for v in vecs] + [shared[7:8]] * 3)
    for k, piece in enumerate(pieces):
        cut = r ^ k
        own = vec[0:4]
        for m in range(1, 4):
            own = jnp.where(cut == m, vec[4 * m : 4 * m + 4], own)
        piece[:, 0 : 4 * features] = rows[pl.ds(pl.multiple_of(cut * fine, 8), fine), :].astype(piece.dtype)
        lanes = [own[i // 6 : i // 6 + 1, i % 6 * 128 : i % 6 * 128 + 128] for i in range(24)]
        piece[:, 4 * features :] = jnp.concatenate(lanes).astype(piece.dtype)


def meet_call(me, messages, outs):
    owned, features = outs[0].shape
    assert features == 6 * 128 and owned == 96
    shape = (owned // 4, 4 * features + 128)
    return pl.pallas_call(
        meet_kernel,
        out_shape=(jax.ShapeDtypeStruct(shape, wide),) + (jax.ShapeDtypeStruct(shape, low),) * 3,
        in_specs=[in_smem] + [in_vmem] * 11,
        out_specs=(in_vmem,) * 4,
        scratch_shapes=[
            pltpu.VMEM((8, *messages[0].shape), wide),
            pltpu.VMEM((owned, 4 * features), wide),
        ],
        name="meet_gradients",
    )(me, *messages, *outs)


def spread_kernel(me_ref, p0, p1, p2, p3, b0, b1, b2, b3, rows_out, scratch):
    c, r = me_ref[0], me_ref[3]
    owned = b0.shape[0]
    fine, short = owned // 4, rows_out.shape[0] // 4
    for k, p in enumerate((p0, p1, p2, p3)):
        cut = r ^ k
        value = p[...].astype(wide)
        for b in range(4):
            scratch[b, pl.ds(pl.multiple_of(cut * fine, 8), fine), :] = value[b * fine : (b + 1) * fine]
        rows_out[pl.ds(pl.multiple_of(cut * short, 8), short), :] = value[owned:]
    for k, out in enumerate((b0, b1, b2, b3)):
        out[...] = scratch[c ^ k].astype(low)


def spread_call(me, owned, row_rows, pieces):
    features = pieces[0].shape[1]
    return pl.pallas_call(
        spread_kernel,
        out_shape=(jax.ShapeDtypeStruct((owned, features), low),) * 4
        + (jax.ShapeDtypeStruct((row_rows, features), wide),),
        in_specs=[in_smem] + [in_vmem] * 4,
        out_specs=(in_vmem,) * 5,
        scratch_shapes=[pltpu.VMEM((4, owned, features), wide)],
        name="spread_gradients",
    )(me, *pieces)


def join_ff_kernel(me_ref, b0, b1, b2, b3, out):
    c = me_ref[0]
    unit = out.shape[1] // 8
    for k, b in enumerate((b0, b1, b2, b3)):
        for t in range(2):
            lo = pl.multiple_of((4 * t + (c ^ k)) * unit, 128)
            out[:, pl.ds(lo, unit)] = b[:, t * unit : (t + 1) * unit].astype(wide)


def join_ff_call(me, blocks):
    owned, hidden = blocks[0].shape
    return pl.pallas_call(
        join_ff_kernel,
        out_shape=jax.ShapeDtypeStruct((owned, 4 * hidden), wide),
        in_specs=[in_smem] + [in_vmem] * 4,
        out_specs=in_vmem,
        name="join_fc_gradient",
    )(me, *blocks)


def join_att_kernel(me_ref, p0, p1, p2, p3, qkv_out, rows_out, *refs):
    outs, (vec, row) = refs[:8], refs[8:]
    c, f, r = me_ref[0], me_ref[1], me_ref[3]
    features, fine = rows_out.shape[1], p0.shape[0]
    part = features // 4
    for k, p in enumerate((p0, p1, p2, p3)):
        cut = r ^ k
        rows = pl.ds(pl.multiple_of(cut * fine, 8), fine)
        value = p[...].astype(wide)
        qkv_out[rows, :] = value[:, 0 : 3 * features]
        rows_out[rows, :] = value[:, 3 * features : 4 * features]
        vec[cut] = value[:, 4 * features :]

    mine = f * 4 + c
    total = [
        jnp.concatenate([vec[k // 4, k % 4 * 6 + i : k % 4 * 6 + i + 1, :] for i in range(6)], axis=1) for k in range(13)
    ]

    def choose(values, index):
        value = values[0]
        for k in range(1, len(values)):
            value = jnp.where(index == k, values[k], value)
        return value

    for i in (0, 1, 2, 3, 4, 7):
        size = outs[i].shape[0]
        source = total[min(i, 4)]
        outs[i][...] = choose([source[:, k * size : (k + 1) * size] for k in range(8)], mine).reshape(size)
    size = outs[5].shape[0]
    for k in range(4):
        for t in range(3):
            lo = (4 * t + head_block(k)) * part
            row[0:1, lo : lo + part] = total[9 + k][:, t * part : (t + 1) * part]
    outs[5][...] = choose([row[0:1, k * size : (k + 1) * size] for k in range(8)], mine).reshape(size)
    size = outs[6].shape[0]
    pieces = [total[5 + k][:, t * size : (t + 1) * size] for t in range(2) for k in range(4)]
    outs[6][...] = choose(pieces, mine).reshape(size)


def join_att_call(me, owned, features, pieces):
    sizes = (features // 8,) * 5 + (3 * features // 8, features // 2, features // 8)
    return pl.pallas_call(
        join_att_kernel,
        out_shape=(
            jax.ShapeDtypeStruct((owned, 3 * features), wide),
            jax.ShapeDtypeStruct((owned, features), wide),
        )
        + tuple(jax.ShapeDtypeStruct((n,), wide) for n in sizes),
        in_specs=[in_smem] + [in_vmem] * 4,
        out_specs=(in_vmem,) * 10,
        scratch_shapes=[pltpu.VMEM((4, owned // 4, 128), wide), pltpu.VMEM((8, 3 * features), wide)],
        name="join_qkv_gradient",
    )(me, *pieces)


def finish_kernel(first, count, x_ref, cot_ref, vecs, *refs):
    out, grad = refs[-2:]
    for k in range(count):
        mine, got, over = refs[3 * k : 3 * k + 3]
        s = first + k
        spot = k if x_ref.shape[0] == count else s
        x = x_ref[spot].astype(wide)
        total = mine[0].astype(wide) + got[0].astype(wide) + over[0].astype(wide)
        out[spot] = (x + total + vecs[4:5, :]).astype(low)
        e = mine[1].astype(wide) + got[1].astype(wide) + over[1].astype(wide)
        center = x - jnp.mean(x, axis=-1, keepdims=True)
        spread = jnp.mean(center * center, axis=-1, keepdims=True)
        root = lax.rsqrt(spread + epsilon)
        n = center * root
        back = root * (e - jnp.mean(e, axis=-1, keepdims=True) - n * jnp.mean(e * n, axis=-1, keepdims=True))
        grad[spot] = (cot_ref[spot].astype(wide) + back).astype(low)


def finish_call(first, tokens, cotangent, vecs, triples, before=None):
    count, shape = len(triples), jax.ShapeDtypeStruct(tokens.shape, low)
    block = pl.BlockSpec((count, *tokens.shape[1:]), lambda i: (first // count, 0, 0))
    assert first % count == 0
    whole = [pl.BlockSpec(v.shape, lambda i, d=v.ndim: (0,) * d) for v in (vecs, *sum(triples, ()))]
    operands = [tokens, cotangent, vecs, *sum(triples, ())]
    specs = [block, block, *whole]
    aliases = {}
    if before is not None:
        aliases = {len(operands): 0, len(operands) + 1: 1}
        operands += list(before)
        specs += [anywhere, anywhere]
    return pl.pallas_call(
        partial(finish_kernel, first, count),
        grid=(1,),
        out_shape=(shape, shape),
        in_specs=specs,
        out_specs=(block, block),
        input_output_aliases=aliases,
        name="finish_tokens",
    )(*operands)


def shards(
    tokens,
    segment,
    ln1_gain,
    ln1_bias,
    qkv_weight,
    qkv_bias,
    out_weight,
    out_bias,
    ln2_gain,
    ln2_bias,
    fc_weight,
    fc_bias,
    proj_weight,
    proj_bias,
    cotangent,
):
    ctx, fsdp, rep = lax.axis_size("ctx"), lax.axis_size("fsdp"), lax.axis_size("rep")
    c, f, r = lax.axis_index("ctx"), lax.axis_index("fsdp"), lax.axis_index("rep")
    paired = fsdp == 2 and ctx == 4 and rep == 4
    seqs, local_len, features = tokens.shape
    length = local_len * ctx
    owned = qkv_weight.shape[0]
    hidden_own = proj_weight.shape[0]
    hidden_all = fc_weight.shape[1]
    hidden = hidden_all // ctx
    part = features // ctx
    me = f * ctx + c
    core = c & 1

    half = ROT // 2
    inverse = (1.0 / np.float32(10000.0) ** (np.arange(0, ROT, 2, dtype=np.float32) / ROT)).astype(np.float32)
    angles = inverse[:, None] * np.arange(length, dtype=np.float32)[None, :]
    cosine, sine = jnp.asarray(np.cos(angles)), jnp.asarray(np.sin(angles))

    def far_rows(s, *before):
        both = jnp.stack([tokens[s], cotangent[s]])
        return swap(after(both, *before) if before else both, "ctx", 2)

    near = (swap(tokens, "ctx", 1), swap(cotangent, "ctx", 1))

    if paired:
        where = jnp.stack([c, f, core, r]).astype(jnp.int32)
        vectors = (ln1_gain, ln1_bias, ln2_gain, ln2_bias, out_bias, proj_bias, qkv_bias, fc_bias)
        proj_x = swap(proj_weight, "fsdp", 1)
        q0, q1, q2, q3, f0, f1, f2, f3 = pack_call(where, qkv_weight, fc_weight, segment, vectors)
        f_got = [swap(f1, "ctx", 1), swap(f2, "ctx", 2), swap(f3, "ctx", 3)]
        far_send = [jnp.stack([tokens[s], cotangent[s]]) for s in range(seqs)]
        f_got, far_send = lax.optimization_barrier((f_got, far_send))
        far = [swap(far_send[0], "ctx", 2)]
        f_half = rows_call(where, owned, (f0, *f_got))
        f_half, proj_x = lax.optimization_barrier((f_half, proj_x))
        f_other = swap(f_half, "fsdp", 1)
        far1 = swap(after(far_send[1], f_half), "ctx", 2)
        far[0], f_other = lax.optimization_barrier((far[0], f_other))
        far_core = [swap(far[0], "ctx", 1)]
        vecs, bias, segs = prep_call(where, owned, part, seqs, length, f_half, f_other)
        proj_pair, fc_pair = (proj_weight, proj_x), (f_half, f_other)
    else:
        zero = jnp.zeros_like(c)
        where = jnp.stack([c, zero, zero, zero]).astype(jnp.int32)

        def whole(v, axes=("fsdp", "ctx")):
            return lax.all_gather(v, axes, axis=0, tiled=True)

        far = [far_rows(s) for s in range(seqs)]
        far_core = [swap(v, "ctx", 1) for v in far]
        bias = pick(whole(qkv_bias).reshape(3, ctx, part).transpose(1, 0, 2), c).astype(wide)
        bias = jnp.broadcast_to(bias.reshape(3 * part, 1), (3 * part, 128))
        b_sum = (whole(out_bias).astype(wide) + whole(proj_bias).astype(wide)).reshape(1, features)
        vecs = [whole(v).astype(wide) for v in (ln1_gain, ln1_bias, ln2_gain, ln2_bias)]
        vecs += [b_sum.reshape(features), pick(whole(fc_bias).reshape(ctx, hidden), c).astype(wide)]
        vecs = jnp.concatenate([jnp.stack(vecs), jnp.zeros((2, features), wide)])
        segs = lax.all_gather(segment.astype(low), "ctx", axis=1, tiled=True).astype(wide)
        segs = jnp.concatenate([segs, jnp.zeros((8 - seqs, length), wide)])

        def halves(v):
            return v[: v.shape[0] // 2], v[v.shape[0] // 2 :]

        out_pair = halves(pick(whole(out_weight).reshape(ctx, part, features), c))
        proj_pair = halves(pick(whole(proj_weight).reshape(ctx, hidden, features), c))
        qkv_pair = pick(whole(qkv_weight).reshape(features, 3, ctx, part).transpose(2, 0, 1, 3), c)
        qkv_pair = halves(qkv_pair.reshape(features, 3 * part))
        fc_pair = halves(pick(whole(fc_weight).reshape(features, ctx, hidden).transpose(1, 0, 2), c))

    def run_ff(s, args, acc, part_in, is_last):
        send, keep, *grads = ff_call(s, where, args, *fc_pair, *proj_pair, vecs, acc, part_in, is_last)
        return (send, keep), grads

    def run_att(s, args, weights, acc, part_in, vec=None):
        send_near, keep_near, send_far, keep_far, *grads = att_call(
            s, where, args, *weights[0], bias, *weights[1], vecs, segs, cosine, sine, acc, part_in, vec
        )
        return (send_near, keep_near, send_far, keep_far), grads

    def chip_sum(send, keep):
        return (keep.astype(wide) + swap(send, "ctx", 1).astype(wide)).astype(low)

    def to_rep(pieces):
        return [swap(piece, "rep", k) for k, piece in zip(range(1, rep), pieces)]

    def to_ctx(pieces):
        return [swap(piece, "ctx", k) for k, piece in zip(range(1, ctx), pieces)]

    def add_up(first, others):
        total = first
        for value in others:
            total = total + value.astype(wide)
        return total.astype(low)

    phase = lax.optimization_barrier
    if paired:
        args = (tokens, cotangent, *near, far[0], far_core[0])
        far_send, q1, q2, q3, out_send, args = phase((far_send, q1, q2, q3, out_weight, args))
        q_got = [swap(q1, "ctx", 1), swap(q2, "ctx", 2), swap(q3, "ctx", 3)]
        out_x = swap(out_send, "fsdp", 1)
        part0, acc = run_ff(0, args, None, None, False)

        part0, acc, far1, q_got, far_send, out_x = phase((part0, acc, far1, q_got, far_send, out_x))
        far2 = swap(far_send[2], "ctx", 2)
        out_keep = jnp.where(core == f, out_weight, out_x)
        out_got = swap(jnp.where(core == f, out_x, out_weight), "ctx", 1)
        far1_core = swap(far1, "ctx", 1)
        part1, acc = run_ff(1, (tokens, cotangent, *near, far1, far1_core), acc, None, False)

        part1, acc, far2, q_got, out_got, out_keep = phase((part1, acc, far2, q_got, out_got, out_keep))
        q_half = rows_call(where, owned, (q0, *q_got))
        far2_core = swap(far2, "ctx", 1)
        far2_core, q_half, acc = phase((far2_core, q_half, acc))
        q_other = swap(q_half, "fsdp", 1)
        part2, ff_last = run_ff(2, (tokens, cotangent, *near, far2, far2_core), acc, None, True)

        part0, ff_last, q_other = phase((part0, ff_last, q_other))
        att_weights = ((q_half, q_other), (out_keep, out_got))
        ff_got = swap(ff_last[1], "fsdp", 1)
        args = (tokens, cotangent, *near, far[0], far_core[0])
        part0, att_acc = run_att(0, args, att_weights, None, part0)

        part0, att_acc, ff_got = phase((part0, att_acc, ff_got))
        ff_pieces = split_call(where, ff_last[0], ff_got)
        away = chip_sum(*part0[2:])
        ff_pieces, part0, away, part1, att_acc = phase((ff_pieces, part0, away, part1, att_acc))
        ff_got = to_rep(ff_pieces[1:])
        over0 = swap(away, "ctx", 2)
        got0 = swap(part0[0], "ctx", 1)
        args = (tokens, cotangent, *near, far1, far1_core)
        part1, att_acc = run_att(1, args, att_weights, att_acc, part1)

        part1, att_acc, ff_got, over0, got0 = phase((part1, att_acc, ff_got, over0, got0))
        ff_total = add_up(ff_pieces[0], ff_got)
        away = chip_sum(*part1[2:])
        ff_total, part1, away, part2, att_acc = phase((ff_total, part1, away, part2, att_acc))
        ff_got = to_rep([ff_total] * (rep - 1))
        over1 = swap(away, "ctx", 2)
        got1 = swap(part1[0], "ctx", 1)
        args = (tokens, cotangent, *near, far2, far2_core)
        part2, att_last = run_att(2, args, att_weights, att_acc, part2, ff_last[2])

        part2, att_last, ff_got, over1, got1 = phase((part2, att_last, ff_got, over1, got1))
        flat = [(k, i) for k in range(fsdp) for i in range(ctx)]
        messages = [att_last[0]]
        for g, h in flat[1:]:
            peers = [(k * ctx + i, (k ^ g) * ctx + (i ^ h)) for k, i in flat]
            messages.append(lax.ppermute(att_last[g * ctx + h], ("fsdp", "ctx"), peers))
        pairs = [(k, i, 1 - k, i) if (i & 1) != k else (k, i, k, i ^ 1) for k, i in flat]
        near_got = lax.ppermute(att_last[9], ("fsdp", "ctx"), [(a * ctx + b, d * ctx + e) for a, b, d, e in pairs])
        pairs = [(k * ctx + i, (1 - k) * ctx + (i ^ 1)) for k, i in flat if (i & 1) != k]
        far_got = lax.ppermute(att_last[10], ("fsdp", "ctx"), pairs)
        away = chip_sum(*part2[2:])
        messages, near_got, far_got, part2, away, ff_got = phase(
            (messages, near_got, far_got, part2, away, ff_got)
        )

        pieces = meet_call(where, messages, (att_last[8], near_got, far_got))
        pieces, away, part2 = phase((pieces, away, part2))
        got = to_rep(pieces[1:])
        over2 = swap(away, "ctx", 2)
        got2 = swap(part2[0], "ctx", 1)
        *ff_blocks, g_proj = spread_call(where, owned, hidden_own, (ff_total, *ff_got))
        done = finish_call(0, tokens, cotangent, vecs, [(part0[1], got0, over0), (part1[1], got1, over1)])
        got, over2, got2, ff_blocks, done = phase((got, over2, got2, ff_blocks, done))

        piece = add_up(pieces[0], got)
        piece, over2, got2, ff_blocks, done = phase((piece, over2, got2, ff_blocks, done))
        others = to_rep([piece] * (rep - 1))
        ff_blocks_got = to_ctx(ff_blocks[1:])
        output, grad_tokens = finish_call(2, tokens, cotangent, vecs, [(part2[1], got2, over2)], done)
        g_fc = join_ff_call(where, (ff_blocks[0], *ff_blocks_got))
        g_qkv, g_out, *vector_grads = join_att_call(where, owned, features, (piece, *others))
    else:
        att_acc = ff_acc = None
        done = None
        for s in range(seqs):
            args = (tokens, cotangent, *near, far[s], far_core[s])
            parts, ff_acc = run_ff(s, args, ff_acc, None, s == seqs - 1)
            vec = ff_acc[2] if s == seqs - 1 else None
            parts, att_acc = run_att(s, args, (qkv_pair, out_pair), att_acc, parts, vec)
            over = swap(chip_sum(*parts[2:]), "ctx", 2)
            done = finish_call(s, tokens, cotangent, vecs, [(parts[1], swap(parts[0], "ctx", 1), over)], done)
        output, grad_tokens = done

        def any_columns(kept, sent):
            grad = jnp.concatenate([kept.astype(low), sent])
            grad = lax.psum_scatter(grad, "fsdp", scatter_dimension=0, tiled=True)
            grad = lax.psum(grad, "rep").reshape(ctx, owned, -1)
            return lax.all_to_all(grad, "ctx", split_axis=0, concat_axis=0)

        def any_rows(kept, sent):
            grad = jnp.concatenate([kept.astype(low), sent])
            grad = jnp.where(jnp.arange(ctx)[:, None, None] == c, grad[None], 0).reshape(-1, features)
            return lax.psum(
                lax.psum_scatter(grad, ("fsdp", "ctx"), scatter_dimension=0, tiled=True), "rep"
            )

        cut = features // 2
        g_fc = any_columns(ff_acc[0][:cut], ff_acc[1][:cut])
        g_fc = g_fc.transpose(1, 0, 2).reshape(owned, hidden_all)
        g_proj = any_rows(ff_acc[0][cut:], ff_acc[1][cut:])
        sent = jnp.concatenate([att_acc[0][None].astype(low), jnp.stack(att_acc[1:8])])
        whole_w = jnp.concatenate(in_order([v[: part // 2] for v in sent], c))
        g_qkv = any_columns(whole_w[: features // 2], whole_w[features // 2 :]).reshape(ctx, owned, 3, part)
        g_qkv = g_qkv.transpose(1, 2, 0, 3).reshape(owned, 3 * features)
        g_out = any_rows(*att_acc[8:10])
        vec = att_acc[0][part // 2 :]
        vec = jnp.concatenate([vec[:8], vec[8:, : features - 3 * part]], axis=1)
        total_vec = jnp.zeros((16, features), wide).at[0:5].set(vec[0:5])
        total_vec = lax.dynamic_update_slice(total_vec, vec[5:6], (5 + c, 0))
        total_vec = lax.dynamic_update_slice(total_vec, vec[6:7], (9 + c, 0))
        total_vec = lax.psum(total_vec, ("ctx", "fsdp", "rep"))
        grads = [total_vec[k] for k in range(5)]
        grads.append(total_vec[9 : 9 + ctx, : 3 * part].reshape(ctx, 3, part).transpose(1, 0, 2).reshape(-1))
        grads.append(total_vec[5 : 5 + ctx, :hidden].reshape(-1))
        grads.append(total_vec[4])
        vector_grads = []
        for v in grads:
            size = v.shape[0] // (fsdp * ctx)
            vector_grads.append(lax.dynamic_slice(v, (me * size,), (size,)))
    g_gain_one, g_shift_one, g_gain_two, g_shift_two, g_b_out, g_b_qkv, g_b_fc, g_b_proj = vector_grads
    return (
        output,
        grad_tokens,
        g_gain_one,
        g_shift_one,
        g_qkv.astype(wide),
        g_b_qkv,
        g_out.astype(wide),
        g_b_out,
        g_gain_two,
        g_shift_two,
        g_fc.astype(wide),
        g_b_fc,
        g_proj.astype(wide),
        g_b_proj,
    )


def solution(mesh):
    rows, row = P(("rep", "fsdp"), "ctx", None), P(("rep", "fsdp"), "ctx")
    vector, matrix = P(("fsdp", "ctx")), P(("fsdp", "ctx"), None)
    params = (
        vector, vector, matrix, vector, matrix, vector,
        vector, vector, matrix, vector, matrix, vector,
    )
    return jax.shard_map(
        shards,
        mesh=mesh,
        in_specs=(rows, row, *params, rows),
        out_specs=(rows, rows, *params),
        check_vma=False,
    )
```
